32 devices in a mesh: dp: 8 (over z, x), head: 4 (over y, core).
Axes of the slice: x: 2, y: 2, z: 4, core: 2. Of those that a mesh axis runs over, the one named last changes fastest.
Arguments:
- layer_input: bfloat16 [4096, 768], P(('dp', 'head')), may hold values from -6 to 6
- segment_ids: int32 [4096], P('dp'), may hold values from 0 to 132, as said below
- upstream: bfloat16 [4096, 768], P(('dp', 'head')), may hold values from -6 to 6
- query_weight: float32 [768, 768], P(('dp', 'head')), may hold values from -0.21875 to 0.21875
- key_weight: float32 [768, 768], P(('dp', 'head')), may hold values from -0.21875 to 0.21875
- value_weight: float32 [768, 768], P(('dp', 'head')), may hold values from -0.21875 to 0.21875
- query_bias: float32 [768], P(('dp', 'head')), may hold values from -3 to 3
- value_bias: float32 [768], P(('dp', 'head')), may hold values from -0.6 to 0.6
- output_weight: float32 [768, 768], P(('dp', 'head')), may hold values from -1.75 to 1.75
- output_bias: float32 [768], P(('dp', 'head')), may hold values from -3 to 3
- attn_gain: float32 [768], P(('dp', 'head')), may hold values from 0.5 to 1.5
- attn_shift: float32 [768], P(('dp', 'head')), may hold values from -3 to 3
- up_weight: float32 [768, 3072], P(('dp', 'head')), may hold values from -0.21875 to 0.21875
- up_bias: float32 [3072], P(('dp', 'head')), may hold values from -3 to 3
- down_weight: float32 [3072, 768], P(('dp', 'head')), may hold values from -0.109375 to 0.109375
- down_bias: float32 [768], P(('dp', 'head')), may hold values from -3 to 3
- final_gain: float32 [768], P(('dp', 'head')), may hold values from 0.5 to 1.5
- final_shift: float32 [768], P(('dp', 'head')), may hold values from -3 to 3
Outputs:
- layer_output: bfloat16 [4096, 768], P(('dp', 'head'))
- input_grad: bfloat16 [4096, 768], P(('dp', 'head'))
- query_weight_grad: float32 [768, 768], P(('dp', 'head'))
- key_weight_grad: float32 [768, 768], P(('dp', 'head'))
- value_weight_grad: float32 [768, 768], P(('dp', 'head'))
- query_bias_grad: float32 [768], P(('dp', 'head'))
- value_bias_grad: float32 [768], P(('dp', 'head'))
- output_weight_grad: float32 [768, 768], P(('dp', 'head'))
- output_bias_grad: float32 [768], P(('dp', 'head'))
- attn_gain_grad: float32 [768], P(('dp', 'head'))
- attn_shift_grad: float32 [768], P(('dp', 'head'))
- up_weight_grad: float32 [768, 3072], P(('dp', 'head'))
- up_bias_grad: float32 [3072], P(('dp', 'head'))
- down_weight_grad: float32 [3072, 768], P(('dp', 'head'))
- down_bias_grad: float32 [768], P(('dp', 'head'))
- final_gain_grad: float32 [768], P(('dp', 'head'))
- final_shift_grad: float32 [768], P(('dp', 'head'))
The draws below stay inside these ranges and needn't reach their ends.
Inputs may be any that keep to these rules, and one draw needn't show every extreme that they name: `segment_ids`: along each packed row of 512 tokens the nonzero document numbers never fall, the row's last document is numbered 128 + 4, and 0 marks padding at the row's end, one token or more in every row; only tokens with equal numbers in one row see each other.
All inputs are finite; a program needn't handle non-finite values.
Results may differ from the reference program's by a relative error of at most 0.015.
The reference program's roundings to bfloat16 on the way count: a program that leaves them out, or rounds other values in their place, can miss the bound.
Values may be sent and summed in bfloat16 or wider, within the bound.
No kernel may reach another device: no remote copies, remote signals or barrier semaphores. Data moves between devices by JAX's collectives and lax.ppermute only.
A program may use at most 128 MiB of HBM per device.

```python
import math
import jax
import jax.numpy as jnp
from jax import lax

D = 768
H = 12
HD = 64
FF = 3072
ROW = 512
TOK_DEV = 128
ROWS = 8
TOKENS = 4096


def draw_segment_ids(key, part):
    gap_key = jax.random.fold_in(key, 11)
    cut_key = jax.random.fold_in(key, 12)
    begin_key = jax.random.fold_in(key, 13)
    pad_key = jax.random.fold_in(key, 14)
    tail_key = jax.random.fold_in(key, 15)
    positions = jnp.arange(ROW, dtype=jnp.int32)[None, :]
    quarter = max(TOK_DEV // 4, 1)
    gap_sizes = jax.random.randint(gap_key, (ROWS, 1), 4, 48)
    breaks = (jax.random.randint(cut_key, (ROWS, ROW), 0, 1 << 20) % gap_sizes == 0).astype(jnp.int32)
    doc_start = jax.random.randint(begin_key, (ROWS, 1), 1, max(TOK_DEV // 2, 2))
    pad_count = jax.random.randint(pad_key, (ROWS, 1), 1, quarter + 1)
    doc_stop = ROW - pad_count - jax.random.randint(tail_key, (ROWS, 1), 0, quarter)
    inside = (positions > doc_start) & (positions < doc_stop)
    at_edges = (positions == doc_start) | (positions == doc_stop)
    breaks = jnp.where(inside, 0, jnp.where(at_edges, 1, breaks))
    breaks = jnp.where(positions == 0, 0, breaks)
    numbers = 1 + jnp.cumsum(breaks, axis=1)
    padding = positions >= ROW - pad_count
    last_doc = jnp.max(jnp.where(padding, 0, numbers), axis=1, keepdims=True)
    numbers = TOK_DEV + 4 - (last_doc - numbers)
    numbers = jnp.where(padding, 0, numbers)
    return numbers.reshape(ROWS * ROW).astype(jnp.int32)


def spiked(entries, key, source, target, parts, factor):
    def block_of(dim):
        return (jnp.arange(entries.shape[dim]) // (entries.shape[dim] // parts)).reshape((-1,) + (1,) * (entries.ndim - 1 - dim))

    one_side = jax.random.permutation(key, parts)[block_of(target)]
    other_side = (block_of(target) + parts // 2) % parts
    return jnp.where((block_of(source) == one_side) | (block_of(source) == other_side), factor * entries, entries)


def block_scale(own_key, shape, split, low, high):
    factor_of, own = 1.0, jax.random.fold_in(own_key, 6)
    for dim, parts in split:
        draws = jnp.exp(jax.random.uniform(jax.random.fold_in(own, dim), (parts,), jnp.float32, low / len(split), high / len(split)))
        factor_of = factor_of * jnp.repeat(draws, shape[dim] // parts).reshape([-1 if axis == dim else 1 for axis in range(len(shape))])
    return factor_of


def normal_values(stream_key, shape, scale, limit, split=(), kind=jnp.bfloat16):
    entries = scale * jax.random.normal(stream_key, shape, jnp.float32)
    if split:
        entries = entries * block_scale(stream_key, shape, split, -0.22, 0.18)
    return jnp.clip(entries, -limit, limit).astype(kind)


def noise_with(rng, dims, deviation, bound, pieces, heavy, held_as=jnp.bfloat16):
    values = deviation * jax.random.normal(rng, dims, jnp.float32)
    if pieces:
        values = values * block_scale(rng, dims, pieces, -0.22, 0.18)
    return jnp.clip(spiked(values, jax.random.fold_in(rng, 3), *heavy), -bound, bound).astype(held_as)


def setup_inputs(seed: int = 0) -> dict:
    streams_of = jax.random.split(jax.random.key(seed), 19)
    layer_input = noise_with(streams_of[0], (TOKENS, D), 1.0, 6.0, ((0, 32),), (0, 1, 32, 2.75))
    segment_ids = draw_segment_ids(jax.random.fold_in(streams_of[18], 71), 0)
    upstream = normal_values(streams_of[2], (TOKENS, D), 1.0, 6.0, ((0, 32),))
    query_weight = normal_values(streams_of[3], (D, D), D ** -0.5, 0.21875, ((0, 32),), jnp.float32)
    key_weight = normal_values(streams_of[4], (D, D), D ** -0.5, 0.21875, ((0, 32),), jnp.float32)
    value_weight = normal_values(streams_of[5], (D, D), D ** -0.5, 0.21875, ((0, 32),), jnp.float32)
    query_bias = normal_values(streams_of[6], (D,), 0.5, 3.0, ((0, 32),), jnp.float32)
    value_bias = normal_values(streams_of[7], (D,), 0.1, 0.6, ((0, 32),), jnp.float32)
    output_weight = normal_values(streams_of[8], (D, D), (max(D // 64, 1)) ** -0.5, 1.75, ((0, 32),), jnp.float32)
    output_bias = normal_values(streams_of[9], (D,), 0.5, 3.0, ((0, 32),), jnp.float32)
    attn_gain = jnp.clip(1.0 + 0.1 * jax.random.normal(streams_of[10], (D,), jnp.float32), 0.5, 1.5)
    attn_shift = normal_values(streams_of[11], (D,), 0.5, 3.0, ((0, 32),), jnp.float32)
    up_weight = normal_values(streams_of[12], (D, FF), D ** -0.5, 0.21875, ((0, 32),), jnp.float32)
    up_bias = normal_values(streams_of[13], (FF,), 0.5, 3.0, ((0, 32),), jnp.float32)
    down_weight = normal_values(streams_of[14], (FF, D), FF ** -0.5, 0.109375, ((0, 32),), jnp.float32)
    down_bias = normal_values(streams_of[15], (D,), 0.5, 3.0, ((0, 32),), jnp.float32)
    final_gain = jnp.clip(1.0 + 0.1 * jax.random.normal(streams_of[16], (D,), jnp.float32), 0.5, 1.5)
    final_shift = normal_values(streams_of[17], (D,), 0.5, 3.0, ((0, 32),), jnp.float32)
    return {"layer_input": layer_input, "segment_ids": segment_ids, "upstream": upstream, "query_weight": query_weight, "key_weight": key_weight, "value_weight": value_weight, "query_bias": query_bias, "value_bias": value_bias, "output_weight": output_weight, "output_bias": output_bias, "attn_gain": attn_gain, "attn_shift": attn_shift, "up_weight": up_weight, "up_bias": up_bias, "down_weight": down_weight, "down_bias": down_bias, "final_gain": final_gain, "final_shift": final_shift}


@jax.custom_vjp
def low(v):
    return lax.optimization_barrier(v.astype(jnp.bfloat16)).astype(jnp.float32)

@jax.custom_vjp
def low_back(v):
    return v

def low_keep(v):
    return (low(v), None)

def low_pass(kept, grad):
    return (grad,)

def back_keep(v):
    return (v, None)

def back_low(kept, grad):
    return (low(grad),)
low.defvjp(low_keep, low_pass)
low_back.defvjp(back_keep, back_low)
EPSILON = 1e-12
NEG_FILL = -1000000000.0

def matmul_high(left, right):
    return jnp.dot(left, right, precision=lax.Precision.HIGHEST)

def layer_norm(values, gain, shift):
    center = values - lax.optimization_barrier(jnp.mean(values, axis=-1, keepdims=True))
    spread = lax.optimization_barrier(jnp.mean(center * center, axis=-1, keepdims=True))
    return center * lax.rsqrt(spread + EPSILON) * gain + shift

def row_forward(layer_row, seg_row, params):
    query_weight, key_weight, value_weight, query_bias, value_bias, output_weight, output_bias, attn_gain, attn_shift, up_weight, up_bias, down_weight, down_bias, final_gain, final_shift = [low(param) for param in params]
    row_count = layer_row.shape[0]
    scale = 1.0 / math.sqrt(HD)
    queries = low_back(low(matmul_high(layer_row, query_weight) + query_bias)).reshape(row_count, H, HD)
    key_rows = low_back(low(matmul_high(layer_row, key_weight))).reshape(row_count, H, HD)
    value_rows = low_back(low(matmul_high(layer_row, value_weight) + value_bias)).reshape(row_count, H, HD)
    block_rows = min(512, row_count)
    block_count = row_count // block_rows

    def attend_block(block_args):
        query_block, seg_block = block_args
        scores = jnp.einsum('qhd,khd->hqk', query_block, key_rows, precision=lax.Precision.HIGHEST)
        scores = low_back(scores * scale)
        same_doc = seg_block[:, None] == seg_row[None, :]
        scores = jnp.where(same_doc[None], scores, NEG_FILL)
        row_top = lax.optimization_barrier(jnp.max(scores, axis=-1, keepdims=True))
        raised = jnp.exp(scores - row_top)
        attn_probs = low(raised / lax.optimization_barrier(jnp.sum(raised, axis=-1, keepdims=True)))
        return jnp.einsum('hqk,khd->qhd', attn_probs, value_rows, precision=lax.Precision.HIGHEST)
    context = lax.map(jax.checkpoint(attend_block), (queries.reshape(block_count, block_rows, H, HD), seg_row.reshape(block_count, block_rows)))
    context = low_back(low(context.reshape(row_count, H * HD)))
    first_sum = layer_row + low_back(matmul_high(context, output_weight)) + output_bias
    normed = layer_norm(first_sum, attn_gain, attn_shift)
    hidden_pre = low_back(matmul_high(low(normed), up_weight)) + up_bias
    activated = low(jax.nn.gelu(hidden_pre, approximate=False))
    second_sum = normed + low_back(matmul_high(activated, down_weight)) + down_bias
    return layer_norm(second_sum, final_gain, final_shift)

def reference(layer_input, segment_ids, upstream, query_weight, key_weight, value_weight, query_bias, value_bias, output_weight, output_bias, attn_gain, attn_shift, up_weight, up_bias, down_weight, down_bias, final_gain, final_shift):
    params = (query_weight, key_weight, value_weight, query_bias, value_bias, output_weight, output_bias, attn_gain, attn_shift, up_weight, up_bias, down_weight, down_bias, final_gain, final_shift)
    inputs = layer_input.astype(jnp.float32).reshape(ROWS, ROW, D)
    cotangents = upstream.astype(jnp.float32).reshape(ROWS, ROW, D)
    segments = segment_ids.reshape(ROWS, ROW)

    def one_row(totals, row_args):
        layer_row, seg_row, cot_row = row_args

        def forward_row(row_in, weights):
            return row_forward(row_in, seg_row, weights)
        output_row, pullback = jax.vjp(forward_row, layer_row, params)
        input_row, weight_grads = pullback(cot_row)
        totals = jax.tree.map(lambda running, fresh: running + fresh, totals, weight_grads)
        return (totals, (output_row.astype(jnp.bfloat16), input_row.astype(jnp.bfloat16)))
    zero_grads = jax.tree.map(jnp.zeros_like, params)
    totals, (outputs, input_grads) = lax.scan(one_row, zero_grads, (inputs, segments, cotangents))
    return (outputs.reshape(TOKENS, D), input_grads.reshape(TOKENS, D), totals[0], totals[1], totals[2], totals[3], totals[4], totals[5], totals[6], totals[7], totals[8], totals[9], totals[10], totals[11], totals[12], totals[13], totals[14])
```

```python
import math

import jax
import jax.numpy as jnp
from jax import lax
from jax.sharding import PartitionSpec as P

H = 12
HD = 64
EPSILON = 1e-12
NEG_FILL = -1000000000.0
BF = jnp.bfloat16
F32 = jnp.float32
ALL = ("dp", "head")
CORE = [(i, i ^ 1) for i in range(4)]
CHIP = [(i, i ^ 2) for i in range(4)]
XSWAP = [(i, i ^ 1) for i in range(8)]


def zshift(k):
    return [(i, (i + 2 * k) % 8) for i in range(8)]


def dot(left, right):
    return jnp.dot(left, right, preferred_element_type=F32)


def gather_dp(piece):
    count = lax.axis_size("dp")
    if count != 8:
        return lax.all_gather(piece, "dp", axis=0, tiled=True)
    place = lax.axis_index("dp")
    found = [piece] + [lax.ppermute(piece, "dp", zshift(k)) for k in (1, 2, 3)]
    found = jnp.stack(found + [lax.ppermute(part, "dp", XSWAP) for part in found])
    wanted = jnp.arange(8)
    order = (place // 2 - wanted // 2) % 4 + 4 * ((place ^ wanted) & 1)
    return jnp.take(found, order, axis=0).reshape(8 * piece.shape[0], piece.shape[1])


def scatter_dp(whole):
    count = lax.axis_size("dp")
    rows = whole.shape[0] // count
    if count != 8:
        return lax.psum_scatter(whole, "dp", scatter_dimension=0, tiled=True)
    place = lax.axis_index("dp")
    chunks = whole.reshape(4, 2, rows, whole.shape[1])
    mine = lax.dynamic_index_in_dim(chunks, place % 2, 1, keepdims=False)
    theirs = lax.dynamic_index_in_dim(chunks, 1 - place % 2, 1, keepdims=False).astype(BF)
    mine = mine + lax.ppermute(theirs, "dp", XSWAP).astype(F32)
    total = lax.dynamic_index_in_dim(mine, place // 2, 0, keepdims=False)
    for k in (1, 2, 3):
        part = lax.dynamic_index_in_dim(mine, (place // 2 + k) % 4, 0, keepdims=False)
        total = total + lax.ppermute(part.astype(BF), "dp", zshift(k)).astype(F32)
    return total


def blocks(values, order):
    tokens = values.shape[0] // 4
    parts = values.reshape(4, tokens, values.shape[1])
    return jnp.concatenate([parts[i] for i in order], axis=0)


def norm_stats(values):
    center = values - jnp.mean(values, axis=-1, keepdims=True)
    spread = jnp.mean(center * center, axis=-1, keepdims=True)
    rate = lax.rsqrt(spread + EPSILON)
    return center * rate, rate


def norm_back(unit, rate, dyg):
    return rate * (
        dyg
        - jnp.mean(dyg, axis=-1, keepdims=True)
        - unit * jnp.mean(dyg * unit, axis=-1, keepdims=True)
    )


def body(
    layer_input,
    segment_ids,
    upstream,
    query_weight,
    key_weight,
    value_weight,
    query_bias,
    value_bias,
    output_weight,
    output_bias,
    attn_gain,
    attn_shift,
    up_weight,
    up_bias,
    down_weight,
    down_bias,
    final_gain,
    final_shift,
):
    tok, width = layer_input.shape
    dp_count = lax.axis_size("dp")
    heads = lax.axis_size("head")
    here = lax.axis_index("head")
    core = here % 2
    rows = query_weight.shape[0]
    group_rows = heads * rows
    share = width // heads
    hidden_piece = down_weight.shape[0]
    scale = 1.0 / math.sqrt(HD)
    my_heads = H // heads

    x_chip = lax.ppermute(layer_input, "head", CHIP)
    x_pair = jnp.concatenate([layer_input, x_chip], axis=0)
    xs = jnp.concatenate([x_pair, lax.ppermute(x_pair, "head", CORE)], axis=0)
    up_pair = jnp.concatenate([upstream, lax.ppermute(upstream, "head", CHIP)], axis=0)
    order = jnp.stack([here, here ^ 2, here ^ 1, here ^ 3])
    seg = jnp.take(segment_ids.reshape(heads, tok), order, axis=0).reshape(heads * tok)

    def by_head(weight):
        return weight.reshape(rows, heads, share).transpose(1, 0, 2)

    bias_cols = jnp.stack(
        [
            query_bias,
            value_bias,
            output_bias,
            attn_gain,
            attn_shift,
            down_bias,
            final_gain,
            final_shift,
        ],
        axis=1,
    )
    bias_cols = jnp.pad(bias_cols, ((0, 0), (0, 120)))
    first_send = jnp.concatenate(
        [
            by_head(query_weight),
            by_head(key_weight),
            by_head(value_weight),
            jnp.broadcast_to(bias_cols[None], (heads, rows, 128)),
        ],
        axis=2,
    ).astype(BF)
    first_send = first_send.reshape(group_rows, 3 * share + 128)
    first_piece = lax.all_to_all(first_send, "head", 0, 0, tiled=True)
    halves = output_weight.reshape(rows, 2, width // 2).transpose(1, 0, 2)
    up_cols = up_weight.reshape(rows, dp_count, heads, hidden_piece).transpose(2, 0, 1, 3)
    second_send = jnp.concatenate(
        [up_cols.reshape(heads, rows, width), jnp.concatenate([halves, halves], axis=0)], axis=2
    ).astype(BF)
    second_piece = lax.all_to_all(
        second_send.reshape(group_rows, width + width // 2), "head", 0, 0, tiled=True
    )
    third_piece = jnp.concatenate(
        [down_weight, jnp.pad(up_bias[:, None], ((0, 0), (0, 127)))], axis=1
    ).astype(BF)

    first_full = gather_dp(first_piece)
    second_full = gather_dp(second_piece)
    third_full = gather_dp(third_piece)
    qkv_weight = first_full[:, : 3 * share]
    bias_rows = first_full[:, 3 * share : 3 * share + 8].T.astype(F32)
    q_bias, v_bias, o_bias, a_gain, a_shift, d_bias, f_gain, f_shift = [bias_rows[i] for i in range(8)]
    q_bias = lax.dynamic_slice_in_dim(q_bias, here * share, share)
    v_bias = lax.dynamic_slice_in_dim(v_bias, here * share, share)
    up_full = second_full[:, :width]
    half = second_full[:, width:]
    other = lax.ppermute(half, "head", CORE)
    output_full = jnp.concatenate(
        [jnp.where(core == 0, half, other), jnp.where(core == 0, other, half)], axis=1
    )
    down_full = third_full[:, :width]
    u_bias = third_full[:, width].astype(F32)

    qkv_bias = jnp.concatenate([q_bias, jnp.zeros_like(q_bias), v_bias])
    qkv = (dot(xs, qkv_weight) + qkv_bias).astype(BF)
    same = seg[:, None] == seg[None, :]
    contexts, sums = [], []
    for j in range(my_heads):
        q = qkv[:, j * HD : (j + 1) * HD]
        k = qkv[:, share + j * HD : share + (j + 1) * HD]
        v = qkv[:, 2 * share + j * HD : 2 * share + (j + 1) * HD]
        scores = jnp.where(same, dot(q, k.T) * scale, NEG_FILL)
        top = jnp.max(scores, axis=1, keepdims=True)
        raised = jnp.exp(scores - top)
        totals = jnp.sum(raised, axis=1, keepdims=True)
        contexts.append(dot((raised / totals).astype(BF), v).astype(BF))
        sums.append(top + jnp.log(totals))
    ctx = jnp.concatenate(contexts, axis=1)

    ctx_chip = lax.ppermute(ctx, "head", CHIP)
    ctx_core = lax.ppermute(jnp.stack([ctx, ctx_chip]), "head", CORE)
    ctx_of = [
        (here, ctx),
        (here ^ 2, blocks(ctx_chip, (1, 0, 3, 2))),
        (here ^ 1, blocks(ctx_core[0], (2, 3, 0, 1))),
        (here ^ 3, blocks(ctx_core[1], (3, 2, 1, 0))),
    ]
    first_sum = xs.astype(F32) + o_bias
    for rank, part in ctx_of:
        first_sum = first_sum + dot(
            part, lax.dynamic_slice_in_dim(output_full, rank * share, share, 0)
        )
    unit1, rate1 = norm_stats(first_sum)
    normed = unit1 * a_gain + a_shift
    normed_low = normed.astype(BF)
    mine = 2 * tok
    unit1, rate1, normed = unit1[:mine], rate1[:mine], normed[:mine]
    pre = dot(normed_low, up_full) + u_bias
    phi = 0.5 * (1.0 + lax.erf(pre * math.sqrt(0.5)))
    act = (pre * phi).astype(BF)
    slope = phi + pre * jnp.exp(-0.5 * pre * pre) * (1.0 / math.sqrt(2 * math.pi))
    part = dot(act, down_full)

    def pair_sum(part):
        total = part[:mine] + lax.ppermute(part[mine:].astype(BF), "head", CORE).astype(F32)
        far = lax.ppermute(total.astype(BF), "head", CHIP).astype(F32)
        return total + jnp.concatenate([far[tok:], far[:tok]], axis=0)

    second = normed + pair_sum(part) + d_bias
    unit2, rate2 = norm_stats(second)
    layer_output = (unit2[:tok] * f_gain + f_shift).astype(BF)
    dy = up_pair.astype(F32)
    d_second = norm_back(unit2, rate2, dy * f_gain)
    f_gain_grad = jnp.sum(dy[:tok] * unit2[:tok], axis=0)
    f_shift_grad = jnp.sum(dy[:tok], axis=0)
    d_bias_grad = jnp.sum(d_second[:tok], axis=0)
    ds_low = d_second.astype(BF)
    ds_low = jnp.concatenate([ds_low, lax.ppermute(ds_low, "head", CORE)], axis=0)
    d_hidden = dot(ds_low, down_full.T) * slope
    u_bias_grad = jnp.sum(d_hidden, axis=0)
    dh_low = d_hidden.astype(BF)
    d_normed = d_second + pair_sum(dot(dh_low, up_full.T))
    down_grad = dot(act.T, ds_low)
    up_grad = dot(normed_low.T, dh_low)
    d_first = norm_back(unit1, rate1, d_normed * a_gain)
    a_gain_grad = jnp.sum(d_normed[:tok] * unit1[:tok], axis=0)
    a_shift_grad = jnp.sum(d_normed[:tok], axis=0)
    o_bias_grad = jnp.sum(d_first[:tok], axis=0)
    df_low = d_first.astype(BF)
    df_low = jnp.concatenate([df_low, lax.ppermute(df_low, "head", CORE)], axis=0)
    my_output = lax.dynamic_slice_in_dim(output_full, here * share, share, 0)
    d_ctx = dot(df_low, my_output.T).astype(BF)
    df_cols = lax.dynamic_slice_in_dim(df_low, here * share, share, 1)
    output_grad = jnp.zeros((width, share), F32)
    for rank, part in ctx_of:
        output_grad = lax.dynamic_update_slice_in_dim(
            output_grad, dot(part.T, df_cols), rank * share, 0
        )

    d_parts = [[], [], []]
    for j in range(my_heads):
        q = qkv[:, j * HD : (j + 1) * HD]
        k = qkv[:, share + j * HD : share + (j + 1) * HD]
        v = qkv[:, 2 * share + j * HD : 2 * share + (j + 1) * HD]
        grad = d_ctx[:, j * HD : (j + 1) * HD]
        scores = jnp.where(same, dot(q, k.T) * scale, NEG_FILL)
        probs = jnp.exp(scores - sums[j])
        low_probs = probs.astype(BF)
        d_probs = dot(grad, v.T)
        inner = jnp.sum(d_probs * probs, axis=1, keepdims=True)
        d_scores = (probs * (d_probs - inner)).astype(BF)
        d_parts[0].append((dot(d_scores, k) * scale).astype(BF))
        d_parts[1].append((dot(d_scores.T, q) * scale).astype(BF))
        d_parts[2].append(dot(low_probs.T, grad).astype(BF))
    d_qkv = jnp.concatenate(d_parts[0] + d_parts[1] + d_parts[2], axis=1)
    qkv_grad = dot(xs.T, d_qkv)
    qkv_bias_grad = jnp.sum(d_qkv.astype(F32), axis=0)
    part = dot(d_qkv, qkv_weight.T)
    total = part[:mine] + lax.ppermute(part[mine:].astype(BF), "head", CORE).astype(F32)
    far = lax.ppermute(total[tok:].astype(BF), "head", CHIP).astype(F32)
    input_grad = (d_first[:tok] + total[:tok] + far).astype(BF)

    wide = jnp.zeros((width,), F32)
    q_wide = lax.dynamic_update_slice_in_dim(wide, qkv_bias_grad[:share], here * share, 0)
    v_wide = lax.dynamic_update_slice_in_dim(wide, qkv_bias_grad[2 * share :], here * share, 0)
    bias_grads = jnp.stack(
        [
            q_wide,
            v_wide,
            o_bias_grad,
            a_gain_grad,
            a_shift_grad,
            d_bias_grad,
            f_gain_grad,
            f_shift_grad,
        ],
        axis=1,
    )
    bias_grads = jnp.pad(bias_grads, ((0, 0), (0, 120)))
    last = jnp.concatenate([qkv_grad, bias_grads], axis=1).astype(BF)
    last = lax.all_to_all(last, ALL, 0, 0, tiled=True).astype(F32)
    last = jnp.sum(last.reshape(dp_count, heads, rows, 3 * share + 128), axis=0)

    def by_row(grad):
        return grad.transpose(1, 0, 2).reshape(rows, -1)

    query_grad = by_row(last[:, :, :share])
    key_grad = by_row(last[:, :, share : 2 * share])
    value_grad = by_row(last[:, :, 2 * share : 3 * share])
    bias_out = jnp.sum(last[:, :, 3 * share : 3 * share + 8], axis=0).T

    down_part = scatter_dp(
        jnp.concatenate([down_grad, jnp.pad(u_bias_grad[:, None], ((0, 0), (0, 127)))], axis=1)
    )
    up_part = scatter_dp(jnp.concatenate([up_grad, output_grad], axis=1)).astype(BF)
    up_part = lax.all_to_all(up_part, "head", 0, 0, tiled=True).astype(F32)
    up_part = up_part.reshape(heads, rows, width + share)
    up_out = up_part[:, :, :width].reshape(heads, rows, dp_count, hidden_piece)
    up_out = up_out.transpose(1, 2, 0, 3).reshape(rows, -1)
    output_out = by_row(up_part[:, :, width:])

    return (
        layer_output,
        input_grad,
        query_grad,
        key_grad,
        value_grad,
        bias_out[0],
        bias_out[1],
        output_out,
        bias_out[2],
        bias_out[3],
        bias_out[4],
        up_out,
        down_part[:, width],
        down_part[:, :width],
        bias_out[5],
        bias_out[6],
        bias_out[7],
    )


def solution(mesh):
    matrix = P(ALL, None)
    vector = P(ALL)
    placed = (
        matrix, P("dp"), matrix, matrix, matrix, matrix, vector, vector, matrix,
        vector, vector, vector, matrix, vector, matrix, vector, vector, vector,
    )
    given = (
        matrix, matrix, matrix, matrix, matrix, vector, vector, matrix, vector,
        vector, vector, matrix, vector, matrix, vector, vector, vector,
    )
    return jax.shard_map(body, mesh=mesh, in_specs=placed, out_specs=given, check_vma=False)
```

```python
import functools
import math

import jax
import jax.numpy as jnp
from jax import lax
from jax.experimental import pallas as pl
from jax.experimental.pallas import tpu as pltpu
from jax.sharding import PartitionSpec as P

H = 12
HD = 64
EPSILON = 1e-12
NEG_FILL = -1000000000.0
BF = jnp.bfloat16
F32 = jnp.float32
ALL = ("dp", "head")
CORE = [(i, i ^ 1) for i in range(4)]
CHIP = [(i, i ^ 2) for i in range(4)]
XSWAP = [(i, i ^ 1) for i in range(8)]
GROUPS = [[(2 * z + x) * 4 + h for z in range(4) for h in range(4)] for x in range(2)]


def zshift(k):
    return [(i, (i + 2 * k) % 8) for i in range(8)]


def shape(dims, kind):
    return jax.ShapeDtypeStruct(dims, kind)


def call(kernel, outs, *args, after=(), micros=2, limit=8):
    spec = pl.BlockSpec(memory_space=pltpu.VMEM)
    count, extra = len(args), len(after)

    def run(*refs):
        kernel(*refs[:count], *refs[count + extra :])

    return pl.pallas_call(
        run,
        out_shape=outs,
        in_specs=[spec] * count + [pl.BlockSpec(memory_space=pl.ANY)] * extra,
        out_specs=jax.tree.map(lambda _: spec, outs),
        compiler_params=pltpu.CompilerParams(vmem_limit_bytes=limit << 20),
        cost_estimate=pl.CostEstimate(
            flops=int(micros * 2e7), bytes_accessed=int(micros * 1e5), transcendentals=0
        ),
    )(*args, *after)


def later(value, *after):
    anywhere = pl.BlockSpec(memory_space=pl.ANY)
    return pl.pallas_call(
        lambda *refs: None,
        out_shape=shape(value.shape, value.dtype),
        in_specs=[anywhere] * (1 + len(after)),
        out_specs=anywhere,
        input_output_aliases={0: 0},
        compiler_params=pltpu.CompilerParams(vmem_limit_bytes=1 << 20),
        cost_estimate=pl.CostEstimate(flops=0, bytes_accessed=0, transcendentals=0),
    )(value, *after)


def dot(left, right, dims=((1,), (0,))):
    return lax.dot_general(left, right, (dims, ((), ())), preferred_element_type=F32)


NT = ((1,), (1,))
TN = ((0,), (0,))


def norm_stats(values):
    center = values - jnp.mean(values, axis=-1, keepdims=True)
    spread = jnp.mean(center * center, axis=-1, keepdims=True)
    rate = lax.rsqrt(spread + EPSILON)
    return center * rate, rate


def norm_back(unit, rate, dyg):
    return rate * (
        dyg
        - jnp.mean(dyg, axis=-1, keepdims=True)
        - unit * jnp.mean(dyg * unit, axis=-1, keepdims=True)
    )


def transpose_wide(values):
    rows, lanes = values.shape
    full = jnp.concatenate([values, jnp.zeros((128 - rows, lanes), F32)], axis=0)
    tiles = [full[:, i : i + 128].T for i in range(0, lanes, 128)]
    return jnp.concatenate(tiles, axis=0)


SPARE = 64


def pack_kernel(query, key, value, output, up, down, *refs):
    biases, outs, scratch = refs[:9], refs[9:14], refs[14:]
    second, third = outs[:4], outs[4]
    matrices, vectors, square, sems = scratch[:6], scratch[6:15], scratch[15], scratch[16]
    pairs = list(zip((query, key, value, output, up, down) + biases, matrices + vectors))
    copies = [pltpu.make_async_copy(a, b, sems.at[i]) for i, (a, b) in enumerate(pairs)]
    for copy in copies:
        copy.start()
    rows, width = query.shape
    share = width // 4
    piece = down.shape[0]
    here = lax.axis_index("head")
    square[...] = jnp.zeros_like(square)
    for copy in copies:
        copy.wait()
    query, key, value, output, up, down = matrices
    for i in range(8):
        square[i : i + 1, 0:rows] = vectors[i][...].reshape(1, rows)
    long = vectors[8][...].reshape(1, piece)
    for j in range(4):
        square[8 + j : 9 + j, 0:rows] = long[:, j * rows : (j + 1) * rows]
    columns = square[...].T[:rows, :SPARE]
    slabs = []
    for h in range(4):
        half = (h % 2) * (width // 2)
        slabs.append(
            jnp.concatenate(
                [w[:, h * share : (h + 1) * share] for w in (query, key, value)]
                + [columns]
                + [up[:, piece * (4 * j + h) : piece * (4 * j + h + 1)] for j in range(width // piece)]
                + [output[:, half : half + width // 2]],
                axis=1,
            )
        )
        third[h] = down[h * rows : (h + 1) * rows, :].astype(BF)
    for flip in range(4):
        chosen = slabs[flip]
        for h in range(1, 4):
            chosen = jnp.where(here == h, slabs[h ^ flip], chosen)
        second[flip][...] = chosen.astype(BF)


def pack(matrices, biases):
    rows, width = matrices[0].shape
    piece = matrices[5].shape[0]
    share = width // 4
    hbm = pl.BlockSpec(memory_space=pltpu.HBM)
    vmem = pl.BlockSpec(memory_space=pltpu.VMEM)
    return pl.pallas_call(
        pack_kernel,
        out_shape=(shape((rows, 3 * share + SPARE + width + width // 2), BF),) * 4
        + (shape((4, rows, width), BF),),
        in_specs=[hbm] * 15,
        out_specs=(vmem,) * 5,
        scratch_shapes=[pltpu.VMEM(v.shape, F32) for v in matrices + biases]
        + [pltpu.VMEM((128, 128), F32), pltpu.SemaphoreType.DMA((15,))],
        compiler_params=pltpu.CompilerParams(vmem_limit_bytes=56 << 20),
    )(*matrices, *biases)


def gather_any(matrices, biases):
    query, key, value, output, up, down = matrices
    rows, width = query.shape
    piece = down.shape[0]
    share = width // 4

    def by_head(weight):
        return weight.reshape(rows, 4, share).transpose(1, 0, 2)

    columns = jnp.concatenate([jnp.stack(biases[:8]), biases[8].reshape(4, rows)], axis=0).T
    columns = jnp.pad(columns, ((0, 0), (0, SPARE - 12)))
    columns = jnp.broadcast_to(columns[None], (4, rows, SPARE))
    halves = output.reshape(rows, 2, width // 2).transpose(1, 0, 2)
    ups = up.reshape(rows, width // piece, 4, piece).transpose(2, 0, 1, 3).reshape(4, rows, width)
    every = jnp.concatenate(
        [by_head(query), by_head(key), by_head(value), columns, ups]
        + [jnp.concatenate([halves, halves], axis=0)],
        axis=2,
    ).astype(BF)
    every = lax.all_to_all(every, "head", 0, 0, tiled=True).reshape(4 * rows, -1)
    every = jnp.concatenate([every, down.astype(BF)], axis=1)
    every = lax.all_gather(every, "dp", axis=0, tiled=True)
    cuts = [3 * share, 3 * share + SPARE, 3 * share + SPARE + width]
    cuts.append(cuts[-1] + width // 2)
    return jnp.split(every, cuts, axis=1)


def merge_kernel(own, core, chip, far, third, first_out, second_out):
    here = lax.axis_index("head")
    cut = first_out.shape[2]
    rest = own.shape[1] - cut
    for flip, piece in ((0, own), (1, core), (2, chip), (3, far)):
        first_out[here ^ flip] = piece[:, :cut]
        second_out[here ^ flip, :, :rest] = piece[:, cut:]
    second_out[:, :, rest:] = third[...]


def join_kernel(splits, *refs):
    outs = refs[-len(splits) :]
    pieces = refs[: -len(splits)]
    rows = pieces[0].shape[0]
    place = lax.axis_index("dp")
    for i, piece in enumerate(pieces):
        owner = lax.rem(place + 8 - 2 * (i % 4), 8) ^ (i // 4)
        at = pl.ds(pl.multiple_of(owner * rows, 16), rows)
        column = 0
        for out in outs:
            out[at, :] = piece[:, column : column + out.shape[1]]
            column += out.shape[1]


def attend_kernel(rows, seg, x0, x1, x2, x3, weight, columns, qkv_out, probs_out, ctx_out, bias_out):
    share = ctx_out.shape[1]
    width = x0.shape[1]
    tok = seg.shape[1]
    here = lax.axis_index("head")
    across = columns[...].astype(F32)
    across = jnp.concatenate([across, jnp.zeros((width, 128 - SPARE), F32)], axis=1)
    across = jnp.concatenate(
        [across[i : i + 128].T[:16] for i in range(0, width, 128)], axis=1
    )
    mine = pltpu.roll(across[:8], lax.rem(width - here * share, width), 1)
    lane = lax.broadcasted_iota(jnp.int32, (8, width), 1)
    up_bias = jnp.zeros((8, width), F32)
    for j in range(4):
        moved = pltpu.roll(across[8:], lax.rem(width + rows * (j - here), width), 1)
        up_bias = jnp.where(lax.rem(lane, 4 * rows) // rows == j, moved[j : j + 1], up_bias)
    bias_out[...] = jnp.concatenate([mine[:2], across[2:8], up_bias], axis=0)
    q_bias = mine[0:1, :share]
    v_bias = mine[1:2, :share]
    bias = jnp.concatenate([q_bias, jnp.zeros((1, share), F32), v_bias], axis=1)
    scale = 1.0 / math.sqrt(HD)
    factor = jnp.concatenate(
        [jnp.full((1, share), scale, F32), jnp.ones((1, 2 * share), F32)], axis=1
    )
    xs = jnp.concatenate([x0[...], x1[...], x2[...], x3[...]], axis=0)
    qkv = (dot(xs, weight[...]) + bias).astype(BF)
    qkv = (qkv.astype(F32) * factor).astype(BF)
    qkv_out[...] = qkv
    ids = [seg[pl.ds(here ^ flip, 1), :].astype(F32) for flip in (0, 2, 1, 3)]
    contexts = []
    for b in range(4):
        column = jnp.broadcast_to(ids[b], (tok, tok)).T
        same = jnp.concatenate([column == ids[t] for t in range(4)], axis=1)
        parts = []
        for j in range(share // HD):
            q = qkv[b * tok : (b + 1) * tok, j * HD : (j + 1) * HD]
            k = qkv[:, share + j * HD : share + (j + 1) * HD]
            v = qkv[:, 2 * share + j * HD : 2 * share + (j + 1) * HD]
            scores = jnp.where(same, dot(q, k, NT), NEG_FILL)
            raised = jnp.exp(scores - jnp.max(scores, axis=1, keepdims=True))
            probs = raised * (1.0 / jnp.sum(raised, axis=1, keepdims=True))
            probs_out[j, b * tok : (b + 1) * tok, :] = probs
            parts.append(dot(probs.astype(BF), v))
        contexts.append(jnp.concatenate(parts, axis=1).astype(BF))
    ctx_out[...] = jnp.concatenate(contexts, axis=0)


def ffn_kernel(half, x0, x1, ctx, ctx_chip, ctx_core, ctx_far, near, other, up, down, bias, *outs):
    if half == 0:
        nl_out, act_out, slope_out, part_out, unit_out, rate_out, normed_out = outs
    else:
        nl_out, act_out, slope_out, part_out = outs
    mine = nl_out.shape[0]
    tok = mine // 2
    share = ctx.shape[1]
    here = lax.axis_index("head")
    o_bias, a_gain, a_shift, u_bias = [bias[i : i + 1, :] for i in (2, 3, 4, 8)]
    total = jnp.concatenate([x0[...], x1[...]], axis=0).astype(F32) + o_bias
    sums = [jnp.zeros((mine, near.shape[1]), F32)] * 2

    def pick(ref, order):
        order = order[2 * half : 2 * half + 2]
        return jnp.concatenate([ref[i * tok : (i + 1) * tok, :] for i in order], axis=0)

    for flip, ref, order in (
        (0, ctx, (0, 1, 2, 3)),
        (2, ctx_chip, (1, 0, 3, 2)),
        (1, ctx_core, (2, 3, 0, 1)),
        (3, ctx_far, (3, 2, 1, 0)),
    ):
        at = pl.multiple_of((here ^ flip) * share, 64)
        part = pick(ref, order)
        sums = [t + dot(part, w[pl.ds(at, share), :]) for t, w in zip(sums, (near, other))]
    total = total + jnp.concatenate(in_order(*sums), axis=1)
    unit, rate = norm_stats(total)
    normed = unit * a_gain + a_shift
    low = normed.astype(BF)
    nl_out[...] = low
    if half == 0:
        unit_out[...] = unit
        rate_out[...] = jnp.broadcast_to(rate, rate_out.shape)
        normed_out[...] = normed
    pre = dot(low, up[...]) + u_bias
    phi = 0.5 * (1.0 + lax.erf(pre * math.sqrt(0.5)))
    act = (pre * phi).astype(BF)
    act_out[...] = act
    slope_out[...] = phi + pre * jnp.exp(-0.5 * pre * pre) * (1.0 / math.sqrt(2 * math.pi))
    part_out[...] = dot(act, down[...]).astype(part_out.dtype)


def in_order(near, other):
    first = lax.axis_index("head") % 2 == 0
    return [jnp.where(first, near, other), jnp.where(first, other, near)]


def add_kernel(part, got, kept, sent):
    total = part[...] + got[...].astype(F32)
    kept[...] = total
    sent[...] = total.astype(BF)


def swap_blocks(values):
    tok = values.shape[0] // 2
    return jnp.concatenate([values[tok:], values[:tok]], axis=0)


def final_kernel(part, far, normed, up0, up1, bias, layer_out, d_second_out, low_out, grads):
    tok = layer_out.shape[0]
    d_bias, f_gain, f_shift = [bias[i : i + 1, :] for i in (5, 6, 7)]
    second = normed[...] + part[...] + swap_blocks(far[...].astype(F32)) + d_bias
    unit, rate = norm_stats(second)
    layer_out[...] = (unit[:tok] * f_gain + f_shift).astype(BF)
    dy = jnp.concatenate([up0[...], up1[...]], axis=0).astype(F32)
    d_second = norm_back(unit, rate, dy * f_gain)
    d_second_out[...] = d_second
    low_out[...] = d_second.astype(BF)
    sums = [d_second[:tok], dy[:tok] * unit[:tok], dy[:tok]]
    sums = [jnp.sum(s, axis=0, keepdims=True) for s in sums]
    grads[...] = jnp.concatenate(sums + [jnp.zeros_like(grads[3:, :])], axis=0)


def ffn_back_kernel(low, slope, up, down, dh_out, part_out, sum_out):
    d_hidden = dot(low[...], down[...], NT) * slope[...]
    total = jnp.sum(d_hidden, axis=0, keepdims=True)
    sum_out[...] = jnp.broadcast_to(total, sum_out.shape)
    dh = d_hidden.astype(BF)
    dh_out[...] = dh
    part_out[...] = dot(dh, up[...], NT).astype(part_out.dtype)


def split_rows(kept, sent, values):
    if sent is None:
        kept[...] = values
        return
    rows = kept.shape[1]
    mine = lax.axis_index("dp") & 1
    pieces = values.reshape(4, 2, rows, values.shape[1])
    for z in range(4):
        even, odd = pieces[z, 0], pieces[z, 1]
        kept[z] = jnp.where(mine == 0, even, odd)
        sent[z] = jnp.where(mine == 0, odd, even).astype(BF)


def weight_grad_kernel(left0, left1, right0, right1, kept, *sent):
    grad = dot(left0[...], right0[...], TN) + dot(left1[...], right1[...], TN)
    split_rows(kept, sent[0] if sent else None, grad)


def first_back_kernel(part, far, d_second, unit, rate, bias, d_first_out, low_out, grads):
    tok = unit.shape[0] // 2
    a_gain = bias[3:4, :]
    d_normed = d_second[...] + part[...] + swap_blocks(far[...].astype(F32))
    u = unit[...]
    d_first = norm_back(u, rate[:, 0:1], d_normed * a_gain)
    d_first_out[...] = d_first[:tok]
    low_out[...] = d_first.astype(BF)
    sums = [d_first[:tok], d_normed[:tok] * u[:tok], d_normed[:tok]]
    sums = [jnp.sum(s, axis=0, keepdims=True) for s in sums]
    grads[...] = jnp.concatenate(sums + [jnp.zeros_like(grads[3:, :])], axis=0)


def attend_back_kernel(low0, low1, near, other, qkv, probs, d_qkv_out):
    share = qkv.shape[1] // 3
    here = lax.axis_index("head")
    at = pl.multiple_of(here * share, 64)
    halves = [near[pl.ds(at, share), :].astype(F32), other[pl.ds(at, share), :].astype(F32)]
    mine = jnp.concatenate(in_order(*halves), axis=1).astype(BF)
    d_ctx = jnp.concatenate([dot(low0[...], mine, NT), dot(low1[...], mine, NT)], axis=0).astype(BF)
    scale = 1.0 / math.sqrt(HD)
    parts = [[], [], []]
    for j in range(share // HD):
        q = qkv[:, j * HD : (j + 1) * HD]
        k = qkv[:, share + j * HD : share + (j + 1) * HD]
        v = qkv[:, 2 * share + j * HD : 2 * share + (j + 1) * HD]
        grad = d_ctx[:, j * HD : (j + 1) * HD]
        p = probs[j]
        d_probs = dot(grad, v, NT)
        inner = jnp.sum(d_probs * p, axis=1, keepdims=True)
        d_scores = (p * (d_probs - inner)).astype(BF)
        parts[0].append(dot(d_scores, k) * scale)
        parts[1].append(dot(d_scores, q, TN))
        parts[2].append(dot(p.astype(BF), grad, TN))
    d_qkv_out[...] = jnp.concatenate(parts[0] + parts[1] + parts[2], axis=1).astype(BF)


def output_grad_kernel(ctx, ctx_chip, ctx_core, ctx_far, low0, low1, *outs):
    out, kept, *sent = outs[-1:] + outs[:-1]
    share = ctx.shape[1]
    width = low0.shape[1]
    tok = ctx.shape[0] // 4
    here = lax.axis_index("head")
    low = jnp.concatenate([low0[...], low1[...]], axis=0).astype(F32)
    low = pltpu.roll(low, lax.rem(width - here * share, width), 1)[:, :share].astype(BF)

    def pick(ref, order):
        return jnp.concatenate([ref[i * tok : (i + 1) * tok, :] for i in order], axis=0)

    for flip, ref, order in (
        (0, ctx, (0, 1, 2, 3)),
        (2, ctx_chip, (1, 0, 3, 2)),
        (1, ctx_core, (2, 3, 0, 1)),
        (3, ctx_far, (3, 2, 1, 0)),
    ):
        at = pl.multiple_of((here ^ flip) * share, 64)
        out[pl.ds(at, share), :] = dot(pick(ref, order), low, TN)
    split_rows(kept, sent[0] if sent else None, out[...])


def last_grad_kernel(rows, x0, x1, x2, x3, d_qkv, grads2, grads1, sum0, sum1, kept, *sent):
    width = x0.shape[1]
    share = width // 4
    here = lax.axis_index("head")
    d = d_qkv[...]
    xs = jnp.concatenate([x0[...], x1[...], x2[...], x3[...]], axis=0)
    weights = dot(xs, d, TN)
    sums = jnp.sum(d.astype(F32), axis=0, keepdims=True)
    zero = jnp.zeros((1, width - share), F32)
    two = jnp.concatenate(
        [
            jnp.concatenate([sums[:, :share], zero], axis=1),
            jnp.concatenate([sums[:, 2 * share :], zero], axis=1),
            jnp.zeros((6, width), F32),
        ],
        axis=0,
    )
    two = pltpu.roll(two, here * share, 1)
    hidden = sum0[...] + sum1[...]
    lane = lax.broadcasted_iota(jnp.int32, (1, width), 1)
    owner = lax.rem(lane, 4 * rows) // rows == here
    ups = [
        jnp.where(owner, pltpu.roll(hidden, lax.rem(width + rows * (here - j), width), 1)[0:1], 0.0)
        for j in range(4)
    ]
    g1, g2 = grads1[...], grads2[...]
    every = jnp.concatenate([two[:2], g1[0:3], g2[0:3]] + ups, axis=0)
    every = jnp.concatenate([every, jnp.zeros((4, width), F32)], axis=0)
    columns = transpose_wide(every)[:, :SPARE]
    split_rows(kept, sent[0] if sent else None, jnp.concatenate([weights, columns], axis=1))


def finish_up_kernel(rows, got, up_out, output_out):
    depth, _, _, columns = got.shape
    width = output_out.shape[1]
    share = width // 4
    piece = 4 * rows
    sums = []
    for h in range(4):
        total = got[0, h].astype(F32)
        for z in range(1, depth):
            total = total + got[z, h].astype(F32)
        sums.append(total)
    output_out[...] = jnp.concatenate([t[:, width : width + share] for t in sums], axis=1)
    up_out[...] = jnp.concatenate(
        [sums[h][:, j * piece : (j + 1) * piece] for j in range(width // piece) for h in range(4)],
        axis=1,
    )


def finish_last_kernel(got, query_out, key_out, value_out, *bias_outs):
    depth, _, rows, columns = got.shape
    share = query_out.shape[1] // 4
    sums = []
    for h in range(4):
        total = got[0, h].astype(F32)
        for z in range(1, depth):
            total = total + got[z, h].astype(F32)
        sums.append(total)
    for i, out in enumerate((query_out, key_out, value_out)):
        out[...] = jnp.concatenate([t[:, i * share : (i + 1) * share] for t in sums], axis=1)
    every = sums[0] + sums[1] + sums[2] + sums[3]
    every = jnp.concatenate([every[:, 3 * share :], jnp.zeros((rows, 128 - SPARE), F32)], axis=1)
    every = jnp.concatenate([every, jnp.zeros((128 - rows, 128), F32)], axis=0).T
    for i in range(8):
        bias_outs[i][...] = every[i : i + 1, :rows].reshape(rows)
    long = jnp.concatenate([every[8 + j : 9 + j, :rows] for j in range(4)], axis=1)
    bias_outs[8][...] = long.reshape(4 * rows)


def sum_up_kernel(kept0, got0, kept1, got1, out):
    cut = kept0.shape[2]
    out[:, :, :cut] = (kept0[...] + got0[...].astype(F32)).astype(BF)
    out[:, :, cut:] = (kept1[...] + got1[...].astype(F32)).astype(BF)


def sum_one_kernel(kept, got, out):
    out[...] = (kept[...] + got[...].astype(F32)).astype(BF)


def to_owners(summed, rows):
    columns = summed.shape[2]
    got = lax.all_to_all(
        summed.reshape(16 * rows, columns), ALL, 0, 0, tiled=True, axis_index_groups=GROUPS
    )
    return got.reshape(4, 4, rows, columns)


def to_owners_any(whole, rows):
    part = lax.psum_scatter(whole, "dp", scatter_dimension=0, tiled=True).astype(BF)
    return lax.all_to_all(part, "head", 0, 0, tiled=True).reshape(1, 4, rows, -1)


def rows_kernel(kept, got, mine, *sent):
    z = lax.axis_index("dp") // 2
    mine[...] = kept[z] + got[z].astype(F32)
    for k in (1, 2, 3):
        at = lax.rem(z + k, 4)
        sent[k - 1][...] = (kept[at] + got[at].astype(F32)).astype(BF)


def sum_kernel(mine, a, b, c, out):
    total = mine[...] + a[...].astype(F32) + b[...].astype(F32) + c[...].astype(F32)
    out[...] = total.astype(out.dtype)


def body(
    layer_input,
    segment_ids,
    upstream,
    query_weight,
    key_weight,
    value_weight,
    query_bias,
    value_bias,
    output_weight,
    output_bias,
    attn_gain,
    attn_shift,
    up_weight,
    up_bias,
    down_weight,
    down_bias,
    final_gain,
    final_shift,
):
    tok, width = layer_input.shape
    cube = lax.axis_size("dp") == 8
    rows = query_weight.shape[0]
    share = width // 4
    mine = 2 * tok

    x1 = lax.ppermute(layer_input, "head", CHIP)
    x2 = lax.ppermute(layer_input, "head", CORE)
    x3 = lax.ppermute(x1, "head", CORE)
    x = (layer_input, x1, x2, x3)

    up1 = lax.ppermute(upstream, "head", CHIP)
    matrices = (query_weight, key_weight, value_weight, output_weight, up_weight, down_weight)
    biases = (
        query_bias,
        value_bias,
        output_bias,
        attn_gain,
        attn_shift,
        down_bias,
        final_gain,
        final_shift,
        up_bias,
    )
    if cube:
        *pieces, third = pack(matrices, biases)
        for flip in (3, 2, 1):
            pieces[flip] = lax.ppermute(pieces[flip], "head", [(i, i ^ flip) for i in range(4)])
        narrow, wide = call(
            merge_kernel,
            (
                shape((4, rows, 3 * share + SPARE), BF),
                shape((4, rows, 2 * width + width // 2), BF),
            ),
            *pieces,
            third,
            micros=1,
        )
        wide = wide.reshape(4 * rows, -1)
        parts = [narrow.reshape(4 * rows, -1)]
        parts += [lax.ppermute(parts[0], "dp", zshift(k)) for k in (1, 2, 3)]
        parts += [lax.ppermute(part, "dp", XSWAP) for part in parts]
        found = [wide, later(lax.ppermute(wide, "dp", zshift(1)), *parts[1:4])]
        qkv_weight, columns = call(
            functools.partial(join_kernel, (3 * share, SPARE)),
            (shape((width, 3 * share), BF), shape((width, SPARE), BF)),
            *parts,
            after=(found[1],),
            micros=1,
        )
    else:
        qkv_weight, columns, up_full, near, down_full = gather_any(matrices, biases)
    qkv, probs, ctx, bias = call(
        functools.partial(attend_kernel, rows),
        (
            shape((4 * tok, 3 * share), BF),
            shape((share // HD, 4 * tok, 4 * tok), F32),
            shape((4 * tok, share), BF),
            shape((16, width), F32),
        ),
        segment_ids.reshape(4, tok),
        *x,
        qkv_weight,
        columns,
        after=(up1,),
        micros=5,
    )
    ctx_chip = lax.ppermute(ctx, "head", CHIP)
    ctx_core = lax.ppermute(ctx, "head", CORE)
    ctx_far = lax.ppermute(ctx_chip, "head", CORE)
    contexts = (ctx, ctx_chip, ctx_core, ctx_far)
    if cube:
        found.append(later(lax.ppermute(found[1], "dp", zshift(1)), ctx))
        found.append(later(lax.ppermute(found[2], "dp", zshift(1)), ctx_far))
        parts = found + [lax.ppermute(part, "dp", XSWAP) for part in found]
        splits = (width, width // 2, width)
        up_full, near, down_full = call(
            functools.partial(join_kernel, splits),
            tuple(shape((width, s), BF) for s in splits),
            *parts,
            micros=1,
        )
    other = lax.ppermute(near, "head", CORE)

    def ffn(half):
        outs = (
            shape((mine, width), BF),
            shape((mine, width), BF),
            shape((mine, width), F32),
            shape((mine, width), F32 if half == 0 else BF),
        )
        if half == 0:
            outs += (shape((mine, width), F32), shape((mine, 128), F32), shape((mine, width), F32))
        return call(
            functools.partial(ffn_kernel, half),
            outs,
            *x[2 * half : 2 * half + 2],
            *contexts,
            near,
            other,
            up_full,
            down_full,
            bias,
            micros=3,
        )

    def pair_sum(part, sent):
        got = lax.ppermute(sent, "head", CORE)
        kept, low = call(
            add_kernel, (shape((mine, width), F32), shape((mine, width), BF)), part, got, micros=1
        )
        return kept, lax.ppermute(low, "head", CHIP)

    nl1, act1, slope1, sent = ffn(1)
    nl0, act0, slope0, part, unit1, rate1, normed = ffn(0)
    part, far = pair_sum(part, sent)
    layer_output, d_second, ds0, grads2 = call(
        final_kernel,
        (
            shape((tok, width), BF),
            shape((mine, width), F32),
            shape((mine, width), BF),
            shape((8, width), F32),
        ),
        part,
        far,
        normed,
        upstream,
        up1,
        bias,
    )
    ds1 = lax.ppermute(ds0, "head", CORE)

    def grad_outs(columns):
        if cube:
            dims = (4, width // 8, columns)
            return (shape(dims, F32), shape(dims, BF))
        return (shape((width, columns), F32),)

    def ffn_back(low, slope, kind, after):
        return call(
            ffn_back_kernel,
            (shape((mine, width), BF), shape((mine, width), kind), shape((8, width), F32)),
            low,
            slope,
            up_full,
            down_full,
            after=after,
            micros=1,
        )

    down_terms = call(
        weight_grad_kernel, grad_outs(width), act0, act1, ds0, ds1, micros=1
    )
    dh1, sent, hidden1 = ffn_back(ds1, slope1, BF, (down_terms[-1],))
    dh0, part, hidden0 = ffn_back(ds0, slope0, F32, (down_terms[-1],))
    part, far = pair_sum(part, sent)
    up_terms = call(
        weight_grad_kernel, grad_outs(width), nl0, nl1, dh0, dh1, after=(part,), micros=1
    )
    order = (up_terms[-1],)
    if cube:
        got_down = lax.ppermute(down_terms[1], "dp", XSWAP)
        order += (got_down,)
    d_first, df0, grads1 = call(
        first_back_kernel,
        (shape((tok, width), F32), shape((mine, width), BF), shape((8, width), F32)),
        part,
        far,
        d_second,
        unit1,
        rate1,
        bias,
        after=order,
        micros=1,
    )
    df1 = lax.ppermute(df0, "head", CORE)
    order = ()
    if cube:
        down_kept, *down_sent = call(
            rows_kernel,
            (shape((4 * rows, width), F32),) + (shape((4 * rows, width), BF),) * 3,
            down_terms[0],
            got_down,
            after=(df0,),
            micros=1,
        )
        down_got = [lax.ppermute(o, "dp", zshift(k)) for k, o in zip((1, 2, 3), down_sent)]
        order = (down_sent[0],)
    output_terms = call(
        output_grad_kernel,
        grad_outs(share) + (shape((width, share), F32),),
        *contexts,
        df0,
        df1,
        after=order,
        micros=1,
    )[:-1]
    d_qkv = call(
        attend_back_kernel,
        shape((4 * tok, 3 * share), BF),
        df0,
        df1,
        near,
        other,
        qkv,
        probs,
        after=(output_terms[-1],),
        micros=4,
    )
    order = ()
    if cube:
        got_up = lax.ppermute(up_terms[1], "dp", XSWAP)
        got_output = lax.ppermute(output_terms[1], "dp", XSWAP)
        down_grad = call(
            sum_kernel,
            shape((4 * rows, width), F32),
            down_kept,
            *down_got,
            after=(d_qkv,),
            micros=1,
        )
        order = (got_up, down_grad)
    last_terms = call(
        functools.partial(last_grad_kernel, rows),
        grad_outs(3 * share + SPARE),
        *x,
        d_qkv,
        grads2,
        grads1,
        hidden0,
        hidden1,
        after=order,
        micros=2,
    )
    part, sent = call(
        input_grad_kernel,
        (shape((mine, width), F32), shape((mine, width), BF)),
        d_qkv,
        qkv_weight,
        after=(last_terms[-1],),
        micros=1,
    )
    if cube:
        summed = call(
            sum_up_kernel,
            shape((4, 4 * rows, width + share), BF),
            up_terms[0],
            got_up,
            output_terms[0],
            got_output,
            after=(last_terms[-1],),
            micros=1,
        )
        up_got = to_owners(summed, rows)
        got = lax.ppermute(last_terms[1], "dp", XSWAP)
        summed = call(
            sum_one_kernel, shape((4, 4 * rows, 3 * share + SPARE), BF), last_terms[0], got, micros=1
        )
        last_got = to_owners(summed, rows)
    else:
        up_got = to_owners_any(jnp.concatenate([up_terms[0], output_terms[0]], axis=1), rows)
        last_got = to_owners_any(last_terms[0], rows)
        down_grad = lax.psum_scatter(down_terms[0], "dp", scatter_dimension=0, tiled=True)
    got = lax.ppermute(sent, "head", CORE)
    part, sent = call(
        input_add_kernel,
        (shape((tok, width), F32), shape((tok, width), BF)),
        part,
        got,
        d_first,
        micros=1,
    )
    far = lax.ppermute(sent, "head", CHIP)
    input_grad = call(input_end_kernel, shape((tok, width), BF), part, far, micros=1)

    up_grad, output_grad = call(
        functools.partial(finish_up_kernel, rows),
        (shape((rows, 4 * width), F32), shape((rows, width), F32)),
        up_got,
    )
    query_grad, key_grad, value_grad, *bias_out = call(
        finish_last_kernel,
        (shape((rows, width), F32),) * 3 + (shape((rows,), F32),) * 8 + (shape((4 * rows,), F32),),
        last_got,
    )

    return (
        layer_output,
        input_grad,
        query_grad,
        key_grad,
        value_grad,
        bias_out[0],
        bias_out[1],
        output_grad,
        bias_out[2],
        bias_out[3],
        bias_out[4],
        up_grad,
        bias_out[8],
        down_grad,
        bias_out[5],
        bias_out[6],
        bias_out[7],
    )


def input_add_kernel(part, got, d_first, kept, sent):
    tok = kept.shape[0]
    total = part[...] + got[...].astype(F32)
    kept[...] = total[:tok] + d_first[...]
    sent[...] = total[tok:].astype(BF)


def input_end_kernel(kept, far, out):
    out[...] = (kept[...] + far[...].astype(F32)).astype(BF)


def input_grad_kernel(d_qkv, weight, part, sent):
    mine = part.shape[0]
    share = weight.shape[1] // 3
    d = d_qkv[...]
    total = dot(d, weight[...], NT)
    part[...] = total[:mine]
    sent[...] = total[mine:].astype(BF)


def solution(mesh):
    matrix = P(ALL, None)
    vector = P(ALL)
    placed = (
        matrix, P("dp"), matrix, matrix, matrix, matrix, vector, vector, matrix,
        vector, vector, vector, matrix, vector, matrix, vector, vector, vector,
    )
    given = (
        matrix, matrix, matrix, matrix, matrix, vector, vector, matrix, vector,
        vector, vector, matrix, vector, matrix, vector, vector, vector,
    )
    return jax.shard_map(body, mesh=mesh, in_specs=placed, out_specs=given, check_vma=False)
```

```python
import functools
import math

import jax
import jax.numpy as jnp
from jax import lax
from jax.experimental import pallas as pl
from jax.experimental.pallas import tpu as pltpu
from jax.sharding import PartitionSpec as P

H = 12
HD = 64
EPSILON = 1e-12
NEG_FILL = -1000000000.0
BF = jnp.bfloat16
F32 = jnp.float32
ALL = ("dp", "head")
CORE = [(i, i ^ 1) for i in range(4)]
CHIP = [(i, i ^ 2) for i in range(4)]
XSWAP = [(i, i ^ 1) for i in range(8)]
GROUPS = [[(2 * z + x) * 4 + h for z in range(4) for h in range(4)] for x in range(2)]


def zshift(k):
    return [(i, (i + 2 * k) % 8) for i in range(8)]


def shape(dims, kind):
    return jax.ShapeDtypeStruct(dims, kind)


def call(kernel, outs, *args, after=(), micros=0.05, limit=8, scratch=()):
    spec = pl.BlockSpec(memory_space=pltpu.VMEM)
    count, extra = len(args), len(after)

    def run(*refs):
        kernel(*refs[:count], *refs[count + extra :])

    named = getattr(kernel, "func", kernel).__name__.removesuffix("_kernel")
    with jax.named_scope(named):
        return pl.pallas_call(
            run,
            out_shape=outs,
            in_specs=[spec] * count + [pl.BlockSpec(memory_space=pl.ANY)] * extra,
            scratch_shapes=list(scratch),
            out_specs=jax.tree.map(lambda _: spec, outs),
            compiler_params=pltpu.CompilerParams(vmem_limit_bytes=limit << 20),
            cost_estimate=pl.CostEstimate(
                flops=int(micros * SCALE * 1e9), bytes_accessed=int(micros * SCALE * 3e6), transcendentals=0
            ),
        )(*args, *after)


def later(value, *after):
    anywhere = pl.BlockSpec(memory_space=pl.ANY)
    return pl.pallas_call(
        lambda *refs: None,
        out_shape=shape(value.shape, value.dtype),
        in_specs=[anywhere] * (1 + len(after)),
        out_specs=anywhere,
        input_output_aliases={0: 0},
        compiler_params=pltpu.CompilerParams(vmem_limit_bytes=1 << 20),
        cost_estimate=pl.CostEstimate(flops=0, bytes_accessed=0, transcendentals=0),
    )(value, *after)


def dot(left, right, dims=((1,), (0,))):
    return lax.dot_general(left, right, (dims, ((), ())), preferred_element_type=F32)


NT = ((1,), (1,))
TN = ((0,), (0,))


def norm_stats(values):
    center = values - jnp.mean(values, axis=-1, keepdims=True)
    spread = jnp.mean(center * center, axis=-1, keepdims=True)
    rate = lax.rsqrt(spread + EPSILON)
    return center * rate, rate


def norm_back(unit, rate, dyg):
    return rate * (
        dyg
        - jnp.mean(dyg, axis=-1, keepdims=True)
        - unit * jnp.mean(dyg * unit, axis=-1, keepdims=True)
    )


def transpose_wide(values):
    rows, lanes = values.shape
    full = jnp.concatenate([values, jnp.zeros((128 - rows, lanes), F32)], axis=0)
    tiles = [full[:, i : i + 128].T for i in range(0, lanes, 128)]
    return jnp.concatenate(tiles, axis=0)


SPARE = 64
RINGS = 1
R3CTX = 1
X3CHIP = 1
R1Z = 0
BFIRST = 1
XW1 = 1
DOWNFIRST = 0
ROWSLATE = 1
INFIRST = 0
HOLDUP = 1
OEARLY = 1
Z1FIRST = 1
HOLDDOWN = 1
C_MERGE = 0.3
C_JOIN = 0.6
C_ATT = 5
C_FFN = 1.9
C_ADD = 0.2
C_FIN = 1.2
C_WG = 0.8
C_FB = 1.0
C_FIRST = 0.5
C_ROWS = 0.3
C_OUT = 1.7
C_AB = 3.0
C_LG = 0.9
C_IN = 0.8
C_LAST = 10
C_SUM = 0.5
SCALE = 0.3


def pack_kernel(query, key, value, output, up, down, *refs):
    biases, outs, scratch = refs[:9], refs[9:14], refs[14:]
    second, third = outs[:4], outs[4]
    matrices, vectors, square, sems = scratch[:6], scratch[6:15], scratch[15], scratch[16]
    pairs = list(zip((query, key, value, output, up, down) + biases, matrices + vectors))
    copies = [pltpu.make_async_copy(a, b, sems.at[i]) for i, (a, b) in enumerate(pairs)]
    for copy in copies:
        copy.start()
    rows, width = query.shape
    share = width // 4
    piece = down.shape[0]
    here = lax.axis_index("head")
    square[...] = jnp.zeros_like(square)
    for copy in copies:
        copy.wait()
    query, key, value, output, up, down = matrices
    for i in range(8):
        square[i : i + 1, 0:rows] = vectors[i][...].reshape(1, rows)
    long = vectors[8][...].reshape(1, piece)
    for j in range(4):
        square[8 + j : 9 + j, 0:rows] = long[:, j * rows : (j + 1) * rows]
    columns = square[...].T[:rows, :SPARE]
    slabs = []
    for h in range(4):
        half = (h % 2) * (width // 2)
        slabs.append(
            jnp.concatenate(
                [w[:, h * share : (h + 1) * share] for w in (query, key, value)]
                + [columns]
                + [up[:, piece * (4 * j + h) : piece * (4 * j + h + 1)] for j in range(width // piece)]
                + [output[:, half : half + width // 2]],
                axis=1,
            )
        )
        third[h] = down[h * rows : (h + 1) * rows, :].astype(BF)
    for flip in range(4):
        chosen = slabs[flip]
        for h in range(1, 4):
            chosen = jnp.where(here == h, slabs[h ^ flip], chosen)
        second[flip][...] = chosen.astype(BF)


def pack(matrices, biases):
    rows, width = matrices[0].shape
    piece = matrices[5].shape[0]
    share = width // 4
    hbm = pl.BlockSpec(memory_space=pltpu.HBM)
    vmem = pl.BlockSpec(memory_space=pltpu.VMEM)
    return pl.pallas_call(
        pack_kernel,
        out_shape=(shape((rows, 3 * share + SPARE + width + width // 2), BF),) * 4
        + (shape((4, rows, width), BF),),
        in_specs=[hbm] * 15,
        out_specs=(vmem,) * 5,
        scratch_shapes=[pltpu.VMEM(v.shape, F32) for v in matrices + biases]
        + [pltpu.VMEM((128, 128), F32), pltpu.SemaphoreType.DMA((15,))],
        compiler_params=pltpu.CompilerParams(vmem_limit_bytes=56 << 20),
    )(*matrices, *biases)


def gather_any(matrices, biases):
    query, key, value, output, up, down = matrices
    rows, width = query.shape
    piece = down.shape[0]
    share = width // 4

    def by_head(weight):
        return weight.reshape(rows, 4, share).transpose(1, 0, 2)

    columns = jnp.concatenate([jnp.stack(biases[:8]), biases[8].reshape(4, rows)], axis=0).T
    columns = jnp.pad(columns, ((0, 0), (0, SPARE - 12)))
    columns = jnp.broadcast_to(columns[None], (4, rows, SPARE))
    halves = output.reshape(rows, 2, width // 2).transpose(1, 0, 2)
    ups = up.reshape(rows, width // piece, 4, piece).transpose(2, 0, 1, 3).reshape(4, rows, width)
    every = jnp.concatenate(
        [by_head(query), by_head(key), by_head(value), columns, ups]
        + [jnp.concatenate([halves, halves], axis=0)],
        axis=2,
    ).astype(BF)
    every = lax.all_to_all(every, "head", 0, 0, tiled=True).reshape(4 * rows, -1)
    every = jnp.concatenate([every, down.astype(BF)], axis=1)
    every = lax.all_gather(every, "dp", axis=0, tiled=True)
    cuts = [3 * share, 3 * share + SPARE, 3 * share + SPARE + width]
    cuts.append(cuts[-1] + width // 2)
    return jnp.split(every, cuts, axis=1)


def merge_first_kernel(own, core, chip, far, out):
    here = lax.axis_index("head")
    for flip, piece in ((0, own), (1, core), (2, chip), (3, far)):
        out[here ^ flip] = piece[:, : out.shape[2]]


def merge_rest_kernel(own, core, chip, far, out):
    here = lax.axis_index("head")
    rest = out.shape[2]
    for flip, piece in ((0, own), (1, core), (2, chip), (3, far)):
        out[here ^ flip] = piece[:, piece.shape[1] - rest :]


def merge_kernel(own, core, chip, far, third, out):
    here = lax.axis_index("head")
    rest = out.shape[2] - third.shape[2]
    for flip, piece in ((0, own), (1, core), (2, chip), (3, far)):
        out[here ^ flip, :, :rest] = piece[:, piece.shape[1] - rest :]
    out[:, :, rest:] = third[...]


def join_kernel(splits, *refs):
    outs = refs[-len(splits) :]
    pieces = refs[: -len(splits)]
    rows = pieces[0].shape[0]
    place = lax.axis_index("dp")
    for i, piece in enumerate(pieces):
        owner = lax.rem(place + 8 - 2 * (i % 4), 8) ^ (i // 4)
        at = pl.ds(pl.multiple_of(owner * rows, 16), rows)
        column = 0
        for out in outs:
            out[at, :] = piece[:, column : column + out.shape[1]]
            column += out.shape[1]


def attend_kernel(rows, seg, x0, x1, x2, x3, weight, columns, qkv_out, probs_out, ctx_out, bias_out):
    share = ctx_out.shape[1]
    width = x0.shape[1]
    tok = seg.shape[1]
    here = lax.axis_index("head")
    across = columns[...].astype(F32)
    across = jnp.concatenate([across, jnp.zeros((width, 128 - SPARE), F32)], axis=1)
    across = jnp.concatenate(
        [across[i : i + 128].T[:16] for i in range(0, width, 128)], axis=1
    )
    mine = pltpu.roll(across[:8], lax.rem(width - here * share, width), 1)
    lane = lax.broadcasted_iota(jnp.int32, (8, width), 1)
    up_bias = jnp.zeros((8, width), F32)
    for j in range(4):
        moved = pltpu.roll(across[8:], lax.rem(width + rows * (j - here), width), 1)
        up_bias = jnp.where(lax.rem(lane, 4 * rows) // rows == j, moved[j : j + 1], up_bias)
    bias_out[...] = jnp.concatenate([mine[:2], across[2:8], up_bias], axis=0)
    q_bias = mine[0:1, :share]
    v_bias = mine[1:2, :share]
    bias = jnp.concatenate([q_bias, jnp.zeros((1, share), F32), v_bias], axis=1)
    scale = 1.0 / math.sqrt(HD)
    factor = jnp.concatenate(
        [jnp.full((1, share), scale, F32), jnp.ones((1, 2 * share), F32)], axis=1
    )
    xs = jnp.concatenate([x0[...], x1[...], x2[...], x3[...]], axis=0)
    qkv = (dot(xs, weight[...]) + bias).astype(BF)
    qkv = (qkv.astype(F32) * factor).astype(BF)
    qkv_out[...] = qkv
    ids = [seg[pl.ds(here ^ flip, 1), :].astype(F32) for flip in (0, 2, 1, 3)]
    contexts = []
    for b in range(4):
        column = jnp.broadcast_to(ids[b], (tok, tok)).T
        same = jnp.concatenate([column == ids[t] for t in range(4)], axis=1)
        parts = []
        for j in range(share // HD):
            q = qkv[b * tok : (b + 1) * tok, j * HD : (j + 1) * HD]
            k = qkv[:, share + j * HD : share + (j + 1) * HD]
            v = qkv[:, 2 * share + j * HD : 2 * share + (j + 1) * HD]
            scores = jnp.where(same, dot(q, k, NT), NEG_FILL)
            raised = jnp.exp(scores - jnp.max(scores, axis=1, keepdims=True))
            probs = raised * (1.0 / jnp.sum(raised, axis=1, keepdims=True))
            probs_out[j, b * tok : (b + 1) * tok, :] = probs
            parts.append(dot(probs.astype(BF), v))
        contexts.append(jnp.concatenate(parts, axis=1).astype(BF))
    ctx_out[...] = jnp.concatenate(contexts, axis=0)


def ffn_kernel(half, x0, x1, ctx, ctx_chip, ctx_core, ctx_far, near, other, up, down, bias, *outs):
    if half == 0:
        nl_out, act_out, slope_out, part_out, unit_out, rate_out, normed_out = outs
    else:
        nl_out, act_out, slope_out, part_out = outs
    mine = nl_out.shape[0]
    tok = mine // 2
    share = ctx.shape[1]
    here = lax.axis_index("head")
    o_bias, a_gain, a_shift, u_bias = [bias[i : i + 1, :] for i in (2, 3, 4, 8)]
    total = jnp.concatenate([x0[...], x1[...]], axis=0).astype(F32) + o_bias
    sums = [jnp.zeros((mine, near.shape[1]), F32)] * 2

    def pick(ref, order):
        order = order[2 * half : 2 * half + 2]
        return jnp.concatenate([ref[i * tok : (i + 1) * tok, :] for i in order], axis=0)

    for flip, ref, order in (
        (0, ctx, (0, 1, 2, 3)),
        (2, ctx_chip, (1, 0, 3, 2)),
        (1, ctx_core, (2, 3, 0, 1)),
        (3, ctx_far, (3, 2, 1, 0)),
    ):
        at = pl.multiple_of((here ^ flip) * share, 64)
        part = pick(ref, order)
        sums = [t + dot(part, w[pl.ds(at, share), :]) for t, w in zip(sums, (near, other))]
    total = total + jnp.concatenate(in_order(*sums), axis=1)
    unit, rate = norm_stats(total)
    normed = unit * a_gain + a_shift
    low = normed.astype(BF)
    nl_out[...] = low
    if half == 0:
        unit_out[...] = unit
        rate_out[...] = jnp.broadcast_to(rate, rate_out.shape)
        normed_out[...] = normed
    pre = dot(low, up[...]) + u_bias
    phi = 0.5 * (1.0 + lax.erf(pre * math.sqrt(0.5)))
    act = (pre * phi).astype(BF)
    act_out[...] = act
    slope_out[...] = phi + pre * jnp.exp(-0.5 * pre * pre) * (1.0 / math.sqrt(2 * math.pi))
    part_out[...] = dot(act, down[...]).astype(part_out.dtype)


def in_order(near, other):
    first = lax.axis_index("head") % 2 == 0
    return [jnp.where(first, near, other), jnp.where(first, other, near)]


def add_kernel(part, got, kept, sent):
    total = part[...] + got[...].astype(F32)
    kept[...] = total
    sent[...] = total.astype(BF)


def swap_blocks(values):
    tok = values.shape[0] // 2
    return jnp.concatenate([values[tok:], values[:tok]], axis=0)


def final_kernel(part, far, normed, up0, up1, bias, layer_out, d_second_out, low_out, grads):
    tok = layer_out.shape[0]
    d_bias, f_gain, f_shift = [bias[i : i + 1, :] for i in (5, 6, 7)]
    second = normed[...] + part[...] + swap_blocks(far[...].astype(F32)) + d_bias
    unit, rate = norm_stats(second)
    layer_out[...] = (unit[:tok] * f_gain + f_shift).astype(BF)
    dy = jnp.concatenate([up0[...], up1[...]], axis=0).astype(F32)
    d_second = norm_back(unit, rate, dy * f_gain)
    d_second_out[...] = d_second
    low_out[...] = d_second.astype(BF)
    sums = [d_second[:tok], dy[:tok] * unit[:tok], dy[:tok]]
    sums = [jnp.sum(s, axis=0, keepdims=True) for s in sums]
    grads[...] = jnp.concatenate(sums + [jnp.zeros_like(grads[3:, :])], axis=0)


def ffn_back_kernel(low, slope, up, down, dh_out, part_out, sum_out):
    d_hidden = dot(low[...], down[...], NT) * slope[...]
    total = jnp.sum(d_hidden, axis=0, keepdims=True)
    sum_out[...] = jnp.broadcast_to(total, sum_out.shape)
    dh = d_hidden.astype(BF)
    dh_out[...] = dh
    part_out[...] = dot(dh, up[...], NT).astype(part_out.dtype)


def split_rows(kept, sent, values):
    if sent is None:
        kept[...] = values
        return
    rows = kept.shape[1]
    mine = lax.axis_index("dp") & 1
    pieces = values.reshape(4, 2, rows, values.shape[1])
    for z in range(4):
        even, odd = pieces[z, 0], pieces[z, 1]
        kept[z] = jnp.where(mine == 0, even, odd)
        sent[z] = jnp.where(mine == 0, odd, even).astype(BF)


def weight_grad_kernel(left0, left1, right0, right1, kept, *sent):
    grad = dot(left0[...], right0[...], TN) + dot(left1[...], right1[...], TN)
    split_rows(kept, sent[0] if sent else None, grad)


def first_back_kernel(part, far, d_second, unit, rate, bias, d_first_out, low_out, grads):
    tok = unit.shape[0] // 2
    a_gain = bias[3:4, :]
    d_normed = d_second[...] + part[...] + swap_blocks(far[...].astype(F32))
    u = unit[...]
    d_first = norm_back(u, rate[:, 0:1], d_normed * a_gain)
    d_first_out[...] = d_first[:tok]
    low_out[...] = d_first.astype(BF)
    sums = [d_first[:tok], d_normed[:tok] * u[:tok], d_normed[:tok]]
    sums = [jnp.sum(s, axis=0, keepdims=True) for s in sums]
    grads[...] = jnp.concatenate(sums + [jnp.zeros_like(grads[3:, :])], axis=0)


def attend_back_kernel(low0, low1, near, other, qkv, probs, d_qkv_out):
    share = qkv.shape[1] // 3
    here = lax.axis_index("head")
    at = pl.multiple_of(here * share, 64)
    halves = [near[pl.ds(at, share), :].astype(F32), other[pl.ds(at, share), :].astype(F32)]
    mine = jnp.concatenate(in_order(*halves), axis=1).astype(BF)
    d_ctx = jnp.concatenate([dot(low0[...], mine, NT), dot(low1[...], mine, NT)], axis=0).astype(BF)
    scale = 1.0 / math.sqrt(HD)
    parts = [[], [], []]
    for j in range(share // HD):
        q = qkv[:, j * HD : (j + 1) * HD]
        k = qkv[:, share + j * HD : share + (j + 1) * HD]
        v = qkv[:, 2 * share + j * HD : 2 * share + (j + 1) * HD]
        grad = d_ctx[:, j * HD : (j + 1) * HD]
        p = probs[j]
        d_probs = dot(grad, v, NT)
        inner = jnp.sum(d_probs * p, axis=1, keepdims=True)
        d_scores = (p * (d_probs - inner)).astype(BF)
        parts[0].append(dot(d_scores, k) * scale)
        parts[1].append(dot(d_scores, q, TN))
        parts[2].append(dot(p.astype(BF), grad, TN))
    d_qkv_out[...] = jnp.concatenate(parts[0] + parts[1] + parts[2], axis=1).astype(BF)


def output_grad_kernel(ctx, ctx_chip, ctx_core, ctx_far, low0, low1, kept, *rest):
    *sent, out = rest
    share = ctx.shape[1]
    width = low0.shape[1]
    tok = ctx.shape[0] // 4
    here = lax.axis_index("head")
    low = jnp.concatenate([low0[...], low1[...]], axis=0).astype(F32)
    low = pltpu.roll(low, lax.rem(width - here * share, width), 1)[:, :share].astype(BF)

    def pick(ref, order):
        return jnp.concatenate([ref[i * tok : (i + 1) * tok, :] for i in order], axis=0)

    for flip, ref, order in (
        (0, ctx, (0, 1, 2, 3)),
        (2, ctx_chip, (1, 0, 3, 2)),
        (1, ctx_core, (2, 3, 0, 1)),
        (3, ctx_far, (3, 2, 1, 0)),
    ):
        at = pl.multiple_of((here ^ flip) * share, 64)
        out[pl.ds(at, share), :] = dot(pick(ref, order), low, TN)
    split_rows(kept, sent[0] if sent else None, out[...])


def last_grad_kernel(rows, x0, x1, x2, x3, d_qkv, grads2, grads1, sum0, sum1, kept, *sent):
    width = x0.shape[1]
    share = width // 4
    here = lax.axis_index("head")
    d = d_qkv[...]
    xs = jnp.concatenate([x0[...], x1[...], x2[...], x3[...]], axis=0)
    weights = dot(xs, d, TN)
    sums = jnp.sum(d.astype(F32), axis=0, keepdims=True)
    zero = jnp.zeros((1, width - share), F32)
    two = jnp.concatenate(
        [
            jnp.concatenate([sums[:, :share], zero], axis=1),
            jnp.concatenate([sums[:, 2 * share :], zero], axis=1),
            jnp.zeros((6, width), F32),
        ],
        axis=0,
    )
    two = pltpu.roll(two, here * share, 1)
    hidden = sum0[...] + sum1[...]
    lane = lax.broadcasted_iota(jnp.int32, (1, width), 1)
    owner = lax.rem(lane, 4 * rows) // rows == here
    ups = [
        jnp.where(owner, pltpu.roll(hidden, lax.rem(width + rows * (here - j), width), 1)[0:1], 0.0)
        for j in range(4)
    ]
    g1, g2 = grads1[...], grads2[...]
    every = jnp.concatenate([two[:2], g1[0:3], g2[0:3]] + ups, axis=0)
    every = jnp.concatenate([every, jnp.zeros((4, width), F32)], axis=0)
    columns = transpose_wide(every)[:, :SPARE]
    split_rows(kept, sent[0] if sent else None, jnp.concatenate([weights, columns], axis=1))


def finish_up_kernel(relative, p0, p1, p2, p3, out):
    width = p0.shape[1]
    piece = out.shape[1] // width * p0.shape[0]
    given = [p[...].astype(F32) for p in (p0, p1, p2, p3)]
    if relative:
        given = by_rank(given)
    out[...] = jnp.concatenate(
        [given[h][:, j * piece : (j + 1) * piece] for j in range(width // piece) for h in range(4)],
        axis=1,
    )


def by_rank(given):
    here = lax.axis_index("head")
    chosen = []
    for i in range(4):
        value = given[i]
        for h in range(1, 4):
            value = jnp.where(here == h, given[h ^ i], value)
        chosen.append(value)
    return chosen


def finish_last_kernel(got, query_out, key_out, value_out, output_out, *bias_outs):
    depth, _, rows, columns = got.shape
    share = query_out.shape[1] // 4
    sums = []
    for h in range(4):
        total = got[0, h].astype(F32)
        for z in range(1, depth):
            total = total + got[z, h].astype(F32)
        sums.append(total)
    for i, out in enumerate((query_out, key_out, value_out)):
        out[...] = jnp.concatenate([t[:, i * share : (i + 1) * share] for t in sums], axis=1)
    every = sums[0] + sums[1] + sums[2] + sums[3]
    output_out[...] = jnp.concatenate([t[:, 3 * share + SPARE :] for t in sums], axis=1)
    every = jnp.concatenate([every[:, 3 * share : 3 * share + SPARE], jnp.zeros((rows, 128 - SPARE), F32)], axis=1)
    every = jnp.concatenate([every, jnp.zeros((128 - rows, 128), F32)], axis=0).T
    for i in range(8):
        bias_outs[i][...] = every[i : i + 1, :rows].reshape(rows)
    long = jnp.concatenate([every[8 + j : 9 + j, :rows] for j in range(4)], axis=1)
    bias_outs[8][...] = long.reshape(4 * rows)


def sum_two_kernel(kept0, got0, kept1, got1, out):
    cut = kept0.shape[2]
    out[:, :, :cut] = (kept0[...] + got0[...].astype(F32)).astype(BF)
    out[:, :, cut:] = (kept1[...] + got1[...].astype(F32)).astype(BF)


def to_owners(summed, rows):
    columns = summed.shape[2]
    got = lax.all_to_all(
        summed.reshape(16 * rows, columns), ALL, 0, 0, tiled=True, axis_index_groups=GROUPS
    )
    return got.reshape(4, 4, rows, columns)


def to_owners_any(whole, rows):
    part = lax.psum_scatter(whole, "dp", scatter_dimension=0, tiled=True).astype(BF)
    return lax.all_to_all(part, "head", 0, 0, tiled=True).reshape(1, 4, rows, -1)


def z_grad_kernel(left0, left1, right0, right1, whole, sent):
    grad = dot(left0[...], right0[...], TN) + dot(left1[...], right1[...], TN)
    whole[...] = grad.reshape(whole.shape)
    sent[...] = whole[lax.rem(lax.axis_index("dp") // 2 + 3, 4)].astype(BF)


def z_step_kernel(step, whole, got, sent):
    at = lax.rem(lax.axis_index("dp") // 2 + 4 - step, 4)
    sent[...] = (whole[at] + got[...].astype(F32)).astype(BF)


def z_sum_kernel(whole, got, kept, sent):
    place = lax.axis_index("dp")
    x = place & 1
    total = whole.at[place // 2]
    kept[...] = total[x] + got[x].astype(F32)
    sent[...] = (total[1 - x] + got[1 - x].astype(F32)).astype(BF)


def heads_kernel(kept, got, *outs):
    rows = outs[0].shape[0]
    total = kept[...] + got[...].astype(F32)
    for out, value in zip(outs, by_rank([total[h * rows : (h + 1) * rows] for h in range(4)])):
        out[...] = value.astype(BF)


def rows_kernel(kept, got, mine, *sent):
    z = lax.axis_index("dp") // 2
    mine[...] = kept[z] + got[z].astype(F32)
    for k in (1, 2, 3):
        at = lax.rem(z + k, 4)
        sent[k - 1][...] = (kept[at] + got[at].astype(F32)).astype(BF)


def sum_kernel(mine, a, b, c, out):
    total = mine[...] + a[...].astype(F32) + b[...].astype(F32) + c[...].astype(F32)
    out[...] = total.astype(out.dtype)


def body(
    layer_input,
    segment_ids,
    upstream,
    query_weight,
    key_weight,
    value_weight,
    query_bias,
    value_bias,
    output_weight,
    output_bias,
    attn_gain,
    attn_shift,
    up_weight,
    up_bias,
    down_weight,
    down_bias,
    final_gain,
    final_shift,
):
    tok, width = layer_input.shape
    cube = lax.axis_size("dp") == 8
    rows = query_weight.shape[0]
    share = width // 4
    mine = 2 * tok

    x1 = lax.ppermute(layer_input, "head", CHIP)
    x2 = lax.ppermute(layer_input, "head", CORE)
    x3 = lax.ppermute(x1, "head", CORE)
    x = (layer_input, x1, x2, x3)

    up1 = lax.ppermute(upstream, "head", CHIP)
    matrices = (query_weight, key_weight, value_weight, output_weight, up_weight, down_weight)
    biases = (
        query_bias,
        value_bias,
        output_bias,
        attn_gain,
        attn_shift,
        down_bias,
        final_gain,
        final_shift,
        up_bias,
    )
    if cube:
        *pieces, third = pack(matrices, biases)
        for flip in (3, 2, 1):
            pieces[flip] = lax.ppermute(pieces[flip], "head", [(i, i ^ flip) for i in range(4)])
        narrow = call(
            merge_first_kernel, shape((4, rows, 3 * share + SPARE), BF), *pieces, micros=C_MERGE
        )
        parts = [narrow.reshape(4 * rows, -1)]
        parts += [lax.ppermute(parts[0], "dp", zshift(k)) for k in (1, 2, 3)]
        parts += [lax.ppermute(part, "dp", XSWAP) for part in parts]
        if RINGS == 1:
            rings = [
                call(
                    merge_kernel,
                    shape((4, rows, 2 * width + width // 2), BF),
                    *pieces,
                    third,
                    after=(narrow,),
                    micros=C_MERGE,
                )
            ]
        else:
            rings = [
                call(
                    merge_rest_kernel,
                    shape((4, rows, width + width // 2), BF),
                    *pieces,
                    after=(narrow,),
                    micros=C_MERGE,
                ),
                third,
            ]
            if BFIRST:
                rings = rings[::-1]
        rings = [ring.reshape(4 * rows, -1) for ring in rings]
        found = [
            [ring, lax.ppermute(later(ring, *parts[1:4]) if R1Z else ring, "dp", zshift(1))]
            for ring in rings
        ]
        crossed = [[lax.ppermute(ring, "dp", XSWAP)] for ring in rings]
        qkv_weight, columns = call(
            functools.partial(join_kernel, (3 * share, SPARE)),
            (shape((width, 3 * share), BF), shape((width, SPARE), BF)),
            *parts,
            after=tuple(c[0] for c in crossed),
            micros=C_JOIN,
        )
    else:
        qkv_weight, columns, up_full, near, down_full = gather_any(matrices, biases)
    qkv, probs, ctx, bias = call(
        functools.partial(attend_kernel, rows),
        (
            shape((4 * tok, 3 * share), BF),
            shape((share // HD, 4 * tok, 4 * tok), F32),
            shape((4 * tok, share), BF),
            shape((16, width), F32),
        ),
        segment_ids.reshape(4, tok),
        *x,
        qkv_weight,
        columns,
        micros=C_ATT,
    )
    ctx_chip = lax.ppermute(ctx, "head", CHIP)
    ctx_core = lax.ppermute(ctx, "head", CORE)
    ctx_far = lax.ppermute(ctx_chip, "head", CORE)
    contexts = (ctx, ctx_chip, ctx_core, ctx_far)
    if cube:
        joined = []
        for ring, (have, swapped) in enumerate(zip(found, crossed)):
            swapped.append(lax.ppermute(have[1], "dp", XSWAP))
            have.append(lax.ppermute(have[1], "dp", zshift(1)))
            swapped.append(lax.ppermute(have[2], "dp", XSWAP))
            hold = have[2]
            if R3CTX:
                hold = later(hold, ctx, *swapped[1 : 1 + XW1])
            have.append(lax.ppermute(hold, "dp", zshift(1)))
            hold = have[3]
            if X3CHIP:
                hold = later(hold, ctx_chip, *swapped[2 : 2 + XW1])
            swapped.append(lax.ppermute(hold, "dp", XSWAP))
            columns_of = have[0].shape[1]
            splits = {
                5 * width // 2: (width, width // 2, width),
                3 * width // 2: (width, width // 2),
                width: (width,),
            }[columns_of]
            joined.append(
                call(
                    functools.partial(join_kernel, splits),
                    tuple(shape((width, s), BF) for s in splits),
                    *have,
                    *swapped,
                    after=(ctx_far, up1),
                    micros=C_JOIN,
                )
            )
        if RINGS == 1:
            up_full, near, down_full = joined[0]
        else:
            (down_full,), (up_full, near) = joined if BFIRST else joined[::-1]
    other = lax.ppermute(near, "head", CORE)

    def ffn(half):
        outs = (
            shape((mine, width), BF),
            shape((mine, width), BF),
            shape((mine, width), F32),
            shape((mine, width), F32 if half == 0 else BF),
        )
        if half == 0:
            outs += (shape((mine, width), F32), shape((mine, 128), F32), shape((mine, width), F32))
        return call(
            functools.partial(ffn_kernel, half),
            outs,
            *x[2 * half : 2 * half + 2],
            *contexts,
            near,
            other,
            up_full,
            down_full,
            bias,
            micros=C_FFN,
        )

    def pair_sum(part, sent):
        got = lax.ppermute(sent, "head", CORE)
        kept, low = call(
            add_kernel, (shape((mine, width), F32), shape((mine, width), BF)), part, got, micros=C_ADD
        )
        return kept, lax.ppermute(low, "head", CHIP)

    nl1, act1, slope1, sent = ffn(1)
    nl0, act0, slope0, part, unit1, rate1, normed = ffn(0)
    part, far = pair_sum(part, sent)
    layer_output, d_second, ds0, grads2 = call(
        final_kernel,
        (
            shape((tok, width), BF),
            shape((mine, width), F32),
            shape((mine, width), BF),
            shape((8, width), F32),
        ),
        part,
        far,
        normed,
        upstream,
        up1,
        bias,
 micros=C_FIN,
)
    ds1 = lax.ppermute(ds0, "head", CORE)

    def grad_outs(columns):
        if cube:
            dims = (4, width // 8, columns)
            return (shape(dims, F32), shape(dims, BF))
        return (shape((width, columns), F32),)

    def ffn_back(low, slope, kind, after):
        return call(
            ffn_back_kernel,
            (shape((mine, width), BF), shape((mine, width), kind), shape((8, width), F32)),
            low,
            slope,
            up_full,
            down_full,
            after=after,
            micros=C_FB,
        )

    down_first = DOWNFIRST or not cube
    if down_first:
        down_terms = call(
            weight_grad_kernel, grad_outs(width), act0, act1, ds0, ds1, micros=C_WG
        )
    order = (down_terms[-1],) if down_first else ()
    dh1, sent, hidden1 = ffn_back(ds1, slope1, BF, order)
    dh0, part, hidden0 = ffn_back(ds0, slope0, F32, order)
    part, far = pair_sum(part, sent)
    if cube:
        up_whole, up_run = call(
            z_grad_kernel,
            (shape((4, 2, 4 * rows, width), F32), shape((2, 4 * rows, width), BF)),
            nl0,
            nl1,
            dh0,
            dh1,
            after=(part,),
            micros=C_WG,
        )
        up_got = [lax.ppermute(up_run, "dp", zshift(1))]
        if not down_first:
            down_terms = call(
                weight_grad_kernel,
                grad_outs(width),
                act0,
                act1,
                ds0,
                ds1,
                after=(up_run,),
                micros=C_WG,
            )
        order = (down_terms[-1],) + ((up_got[0],) if Z1FIRST else ())
        got_down = lax.ppermute(down_terms[1], "dp", XSWAP)
    else:
        up_terms = call(
            weight_grad_kernel, grad_outs(width), nl0, nl1, dh0, dh1, after=(part,), micros=C_WG
        )
        order = (up_terms[-1],)
    d_first, df0, grads1 = call(
        first_back_kernel,
        (shape((tok, width), F32), shape((mine, width), BF), shape((8, width), F32)),
        part,
        far,
        d_second,
        unit1,
        rate1,
        bias,
        after=order,
        micros=C_FIRST,
    )
    df1 = lax.ppermute(df0, "head", CORE)
    def next_step(step, after):
        run = call(
            functools.partial(z_step_kernel, step),
            shape((2, 4 * rows, width), BF),
            up_whole,
            up_got[-1],
            after=after,
            micros=0.3,
        )
        up_got.append(lax.ppermute(run, "dp", zshift(1)))
        return run

    order = (next_step(2, (df0,)),) if cube else ()
    output_terms = call(
        output_grad_kernel,
        grad_outs(share),
        *contexts,
        df0,
        df1,
        after=order,
        scratch=(pltpu.VMEM((width, share), F32),),
        micros=C_OUT,
    )
    d_qkv = call(
        attend_back_kernel,
        shape((4 * tok, 3 * share), BF),
        df0,
        df1,
        near,
        other,
        qkv,
        probs,
        after=(output_terms[-1],),
        micros=C_AB,
    )
    last_columns = 4 * share + SPARE
    order = ()
    if cube:
        down_kept, *down_sent = call(
            rows_kernel,
            (shape((4 * rows, width), F32),) + (shape((4 * rows, width), BF),) * 3,
            down_terms[0],
            got_down,
            after=(d_qkv,) if ROWSLATE else (df0,),
            micros=C_ROWS,
        )
        down_got = [lax.ppermute(o, "dp", zshift(k)) for k, o in zip((1, 2, 3), down_sent)]
        order = (down_sent[0],)
    last_terms = call(
        functools.partial(last_grad_kernel, rows),
        grad_outs(3 * share + SPARE),
        *x,
        d_qkv,
        grads2,
        grads1,
        hidden0,
        hidden1,
        after=order,
        micros=C_LG,
    )
    order = (last_terms[-1],)
    if cube:
        got_last = lax.ppermute(last_terms[1], "dp", XSWAP)
        got_output = lax.ppermute(output_terms[1], "dp", XSWAP)
        order = (next_step(3, order),)
    part, sent = call(
        input_grad_kernel,
        (shape((mine, width), F32), shape((mine, width), BF)),
        d_qkv,
        qkv_weight,
        after=order,
        micros=C_IN,
    )
    got = lax.ppermute(sent, "head", CORE)
    if cube:
        up_kept, up_cross = call(
            z_sum_kernel,
            (shape((4 * rows, width), F32), shape((4 * rows, width), BF)),
            up_whole,
            up_got[-1],
            after=order + ((sent,) if INFIRST else ()),
            micros=C_SUM,
        )
    part, sent = call(
        input_add_kernel,
        (shape((tok, width), F32), shape((tok, width), BF)),
        part,
        got,
        d_first,
        micros=0.4,
    )
    far = lax.ppermute(sent, "head", CHIP)
    input_grad = call(input_end_kernel, shape((tok, width), BF), part, far, micros=0.3)
    if cube:
        up_pieces = list(
            call(
                heads_kernel,
                (shape((rows, width), BF),) * 4,
                up_kept,
                lax.ppermute(up_cross, "dp", XSWAP),
                micros=C_SUM,
            )
        )
        for flip in (1, 2, 3):
            up_pieces[flip] = lax.ppermute(up_pieces[flip], "head", [(i, i ^ flip) for i in range(4)])
        down_grad = call(
            sum_kernel,
            shape((4 * rows, width), F32),
            down_kept,
            *down_got,
            after=(got_output,) if OEARLY else (),
            micros=C_SUM,
        )
    else:
        up_pieces = to_owners_any(up_terms[0], rows)
        up_pieces = [up_pieces[0, h] for h in range(4)]
        down_grad = lax.psum_scatter(down_terms[0], "dp", scatter_dimension=0, tiled=True)
    up_grad = call(
        functools.partial(finish_up_kernel, cube),
        shape((rows, 4 * width), F32),
        *up_pieces,
    )
    if cube:
        summed = call(
            sum_two_kernel,
            shape((4, 4 * rows, last_columns), BF),
            last_terms[0],
            got_last,
            output_terms[0],
            got_output,
            micros=C_LAST,
        )
        hold = ((up_kept,) if HOLDUP else ()) + ((down_grad,) if HOLDDOWN else ())
        last_got = to_owners(later(summed, *hold) if hold else summed, rows)
    else:
        last_got = to_owners_any(jnp.concatenate([last_terms[0], output_terms[0]], axis=1), rows)
    query_grad, key_grad, value_grad, output_grad, *bias_out = call(
        finish_last_kernel,
        (shape((rows, width), F32),) * 4 + (shape((rows,), F32),) * 8 + (shape((4 * rows,), F32),),
        last_got,
    )

    return (
        layer_output,
        input_grad,
        query_grad,
        key_grad,
        value_grad,
        bias_out[0],
        bias_out[1],
        output_grad,
        bias_out[2],
        bias_out[3],
        bias_out[4],
        up_grad,
        bias_out[8],
        down_grad,
        bias_out[5],
        bias_out[6],
        bias_out[7],
    )


def input_add_kernel(part, got, d_first, kept, sent):
    tok = kept.shape[0]
    total = part[...] + got[...].astype(F32)
    kept[...] = total[:tok] + d_first[...]
    sent[...] = total[tok:].astype(BF)


def input_end_kernel(kept, far, out):
    out[...] = (kept[...] + far[...].astype(F32)).astype(BF)


def input_grad_kernel(d_qkv, weight, part, sent):
    mine = part.shape[0]
    share = weight.shape[1] // 3
    d = d_qkv[...]
    total = dot(d, weight[...], NT)
    part[...] = total[:mine]
    sent[...] = total[mine:].astype(BF)


def solution(mesh):
    matrix = P(ALL, None)
    vector = P(ALL)
    placed = (
        matrix, P("dp"), matrix, matrix, matrix, matrix, vector, vector, matrix,
        vector, vector, vector, matrix, vector, matrix, vector, vector, vector,
    )
    given = (
        matrix, matrix, matrix, matrix, matrix, vector, vector, matrix, vector,
        vector, vector, matrix, vector, matrix, vector, vector, vector,
    )
    return jax.shard_map(body, mesh=mesh, in_specs=placed, out_specs=given, check_vma=False)
```

```python
import functools
import math

import jax
import jax.numpy as jnp
from jax import lax
from jax.experimental import pallas as pl
from jax.experimental.pallas import tpu as pltpu
from jax.sharding import PartitionSpec as P

H = 12
HD = 64
EPSILON = 1e-12
NEG_FILL = -1000000000.0
BF = jnp.bfloat16
F32 = jnp.float32
ALL = ("dp", "head")
CORE = [(i, i ^ 1) for i in range(4)]
CHIP = [(i, i ^ 2) for i in range(4)]
XSWAP = [(i, i ^ 1) for i in range(8)]
GROUPS = [[(2 * z + x) * 4 + h for z in range(4) for h in range(4)] for x in range(2)]


def zshift(k):
    return [(i, (i + 2 * k) % 8) for i in range(8)]


def shape(dims, kind):
    return jax.ShapeDtypeStruct(dims, kind)


def call(kernel, outs, *args, after=(), micros=0.05, limit=8, scratch=()):
    spec = pl.BlockSpec(memory_space=pltpu.VMEM)
    count, extra = len(args), len(after)

    def run(*refs):
        kernel(*refs[:count], *refs[count + extra :])

    named = getattr(kernel, "func", kernel).__name__.removesuffix("_kernel")
    with jax.named_scope(named):
        return pl.pallas_call(
            run,
            out_shape=outs,
            in_specs=[spec] * count + [pl.BlockSpec(memory_space=pl.ANY)] * extra,
            scratch_shapes=list(scratch),
            out_specs=jax.tree.map(lambda _: spec, outs),
            compiler_params=pltpu.CompilerParams(vmem_limit_bytes=limit << 20),
            cost_estimate=pl.CostEstimate(
                flops=int(micros * SCALE * 1e9), bytes_accessed=int(micros * SCALE * 3e6), transcendentals=0
            ),
        )(*args, *after)


def later(value, *after):
    anywhere = pl.BlockSpec(memory_space=pl.ANY)
    return pl.pallas_call(
        lambda *refs: None,
        out_shape=shape(value.shape, value.dtype),
        in_specs=[anywhere] * (1 + len(after)),
        out_specs=anywhere,
        input_output_aliases={0: 0},
        compiler_params=pltpu.CompilerParams(vmem_limit_bytes=1 << 20),
        cost_estimate=pl.CostEstimate(flops=0, bytes_accessed=0, transcendentals=0),
    )(value, *after)


def dot(left, right, dims=((1,), (0,))):
    return lax.dot_general(left, right, (dims, ((), ())), preferred_element_type=F32)


NT = ((1,), (1,))
TN = ((0,), (0,))


def norm_stats(values):
    center = values - jnp.mean(values, axis=-1, keepdims=True)
    spread = jnp.mean(center * center, axis=-1, keepdims=True)
    rate = lax.rsqrt(spread + EPSILON)
    return center * rate, rate


def norm_back(unit, rate, dyg):
    return rate * (
        dyg
        - jnp.mean(dyg, axis=-1, keepdims=True)
        - unit * jnp.mean(dyg * unit, axis=-1, keepdims=True)
    )


def transpose_wide(values):
    rows, lanes = values.shape
    full = jnp.concatenate([values, jnp.zeros((128 - rows, lanes), F32)], axis=0)
    tiles = [full[:, i : i + 128].T for i in range(0, lanes, 128)]
    return jnp.concatenate(tiles, axis=0)


SPARE = 64
R3CTX = 0
HOLD1 = 0
HOLDX0 = 1
R2FIRST = 1
X3CHIP = 0
XW1 = 1
X1R3 = 0
MERGE2 = 0
HOLDB1 = 0
B2FIRST = 0
B3CTX = 0
HOLDB3 = 1
UP1CTX = 1
AFTERY = 0
DOWNFIRST = 0
ROWSLATE = 1
INFIRST = 0
HOLDUP = 1
OEARLY = 1
Z1FIRST = 1
HOLDDOWN = 1
C_MERGE = 0.3
C_JOIN = 0.6
C_ATT = 5
C_FFN = 1.9
C_ADD = 0.2
C_FIN = 1.2
C_WG = 0.8
C_FB = 1.0
C_FIRST = 0.5
C_ROWS = 0.3
C_OUT = 1.7
C_AB = 3.0
C_LG = 0.9
C_IN = 0.8
C_LAST = 10
C_SUM = 0.5
SCALE = 0.3


def pack_kernel(query, key, value, output, up, down, *refs):
    biases, outs, scratch = refs[:9], refs[9:15], refs[15:]
    first, second, third = outs[0], outs[1:5], outs[5]
    matrices, vectors, square, sems = scratch[:6], scratch[6:15], scratch[15], scratch[16]
    pairs = list(zip((query, key, value, output, up, down) + biases, matrices + vectors))
    copies = [pltpu.make_async_copy(a, b, sems.at[i]) for i, (a, b) in enumerate(pairs)]
    for copy in copies:
        copy.start()
    rows, width = query.shape
    share = width // 4
    piece = down.shape[0]
    here = lax.axis_index("head")
    square[...] = jnp.zeros_like(square)
    for copy in copies:
        copy.wait()
    query, key, value, output, up, down = matrices
    for i in range(8):
        square[i : i + 1, 0:rows] = vectors[i][...].reshape(1, rows)
    long = vectors[8][...].reshape(1, piece)
    for j in range(4):
        square[8 + j : 9 + j, 0:rows] = long[:, j * rows : (j + 1) * rows]
    columns = square[...].T[:rows, :SPARE]
    slabs = []
    for h in range(4):
        slab = jnp.concatenate(
            [w[:, h * share : (h + 1) * share] for w in (query, key, value)] + [columns], axis=1
        ).astype(BF)
        for z in range(4):
            first[z, h] = slab
        half = (h % 2) * (width // 2)
        slabs.append(
            jnp.concatenate(
                [up[:, piece * (4 * j + h) : piece * (4 * j + h + 1)] for j in range(width // piece)]
                + [output[:, half : half + width // 2]],
                axis=1,
            )
        )
        third[h] = down[h * rows : (h + 1) * rows, :].astype(BF)
    for flip in range(4):
        chosen = slabs[flip]
        for h in range(1, 4):
            chosen = jnp.where(here == h, slabs[h ^ flip], chosen)
        second[flip][...] = chosen.astype(BF)


def pack(matrices, biases):
    rows, width = matrices[0].shape
    piece = matrices[5].shape[0]
    share = width // 4
    hbm = pl.BlockSpec(memory_space=pltpu.HBM)
    vmem = pl.BlockSpec(memory_space=pltpu.VMEM)
    return pl.pallas_call(
        pack_kernel,
        out_shape=(shape((4, 4, rows, 3 * share + SPARE), BF),)
        + (shape((rows, width + width // 2), BF),) * 4
        + (shape((4, rows, width), BF),),
        in_specs=[hbm] * 15,
        out_specs=(vmem,) * 6,
        scratch_shapes=[pltpu.VMEM(v.shape, F32) for v in matrices + biases]
        + [pltpu.VMEM((128, 128), F32), pltpu.SemaphoreType.DMA((15,))],
        compiler_params=pltpu.CompilerParams(vmem_limit_bytes=56 << 20),
    )(*matrices, *biases)


def gather_any(matrices, biases):
    query, key, value, output, up, down = matrices
    rows, width = query.shape
    piece = down.shape[0]
    share = width // 4

    def by_head(weight):
        return weight.reshape(rows, 4, share).transpose(1, 0, 2)

    columns = jnp.concatenate([jnp.stack(biases[:8]), biases[8].reshape(4, rows)], axis=0).T
    columns = jnp.pad(columns, ((0, 0), (0, SPARE - 12)))
    columns = jnp.broadcast_to(columns[None], (4, rows, SPARE))
    halves = output.reshape(rows, 2, width // 2).transpose(1, 0, 2)
    ups = up.reshape(rows, width // piece, 4, piece).transpose(2, 0, 1, 3).reshape(4, rows, width)
    every = jnp.concatenate(
        [by_head(query), by_head(key), by_head(value), columns, ups]
        + [jnp.concatenate([halves, halves], axis=0)],
        axis=2,
    ).astype(BF)
    every = lax.all_to_all(every, "head", 0, 0, tiled=True).reshape(4 * rows, -1)
    every = jnp.concatenate([every, down.astype(BF)], axis=1)
    every = lax.all_gather(every, "dp", axis=0, tiled=True)
    cuts = [3 * share, 3 * share + SPARE, 3 * share + SPARE + width]
    cuts.append(cuts[-1] + width // 2)
    return jnp.split(every, cuts, axis=1)


def join_first_kernel(mine, theirs, weight, columns):
    rows = mine.shape[1]
    cut = weight.shape[1]
    x = lax.axis_index("dp") & 1
    for z in range(4):
        for flip, ref in ((0, mine), (1, theirs)):
            at = pl.ds(pl.multiple_of((2 * z + (x ^ flip)) * rows, 16), rows)
            weight[at, :] = ref[z, :, :cut]
            columns[at, :] = ref[z, :, cut:]


def merge_rest_kernel(own, core, chip, far, out):
    here = lax.axis_index("head")
    for flip, piece in ((0, own), (1, core), (2, chip), (3, far)):
        out[here ^ flip] = piece[...]


def pair_kernel(own, other, out):
    out[0] = own[...]
    out[1] = other[...]


def join_pairs_kernel(p0, p1, p2, p3, out):
    rows = p0.shape[1]
    place = lax.axis_index("dp")
    for i, piece in enumerate((p0, p1, p2, p3)):
        for flip in range(2):
            owner = lax.rem(place + 8 - 2 * i, 8) ^ flip
            out[pl.ds(pl.multiple_of(owner * rows, 16), rows), :] = piece[flip]


def join_kernel(splits, *refs):
    outs = refs[-len(splits) :]
    pieces = refs[: -len(splits)]
    rows = pieces[0].shape[0]
    place = lax.axis_index("dp")
    for i, piece in enumerate(pieces):
        owner = lax.rem(place + 8 - 2 * (i % 4), 8) ^ (i // 4)
        at = pl.ds(pl.multiple_of(owner * rows, 16), rows)
        column = 0
        for out in outs:
            out[at, :] = piece[:, column : column + out.shape[1]]
            column += out.shape[1]


def attend_kernel(rows, seg, x0, x1, x2, x3, weight, columns, qkv_out, probs_out, ctx_out, bias_out):
    share = ctx_out.shape[1]
    width = x0.shape[1]
    tok = seg.shape[1]
    here = lax.axis_index("head")
    across = columns[...].astype(F32)
    across = jnp.concatenate([across, jnp.zeros((width, 128 - SPARE), F32)], axis=1)
    across = jnp.concatenate(
        [across[i : i + 128].T[:16] for i in range(0, width, 128)], axis=1
    )
    mine = pltpu.roll(across[:8], lax.rem(width - here * share, width), 1)
    lane = lax.broadcasted_iota(jnp.int32, (8, width), 1)
    up_bias = jnp.zeros((8, width), F32)
    for j in range(4):
        moved = pltpu.roll(across[8:], lax.rem(width + rows * (j - here), width), 1)
        up_bias = jnp.where(lax.rem(lane, 4 * rows) // rows == j, moved[j : j + 1], up_bias)
    bias_out[...] = jnp.concatenate([mine[:2], across[2:8], up_bias], axis=0)
    q_bias = mine[0:1, :share]
    v_bias = mine[1:2, :share]
    bias = jnp.concatenate([q_bias, jnp.zeros((1, share), F32), v_bias], axis=1)
    scale = 1.0 / math.sqrt(HD)
    factor = jnp.concatenate(
        [jnp.full((1, share), scale, F32), jnp.ones((1, 2 * share), F32)], axis=1
    )
    xs = jnp.concatenate([x0[...], x1[...], x2[...], x3[...]], axis=0)
    qkv = (dot(xs, weight[...]) + bias).astype(BF)
    qkv = (qkv.astype(F32) * factor).astype(BF)
    qkv_out[...] = qkv
    ids = [seg[pl.ds(here ^ flip, 1), :].astype(F32) for flip in (0, 2, 1, 3)]
    contexts = []
    for b in range(4):
        column = jnp.broadcast_to(ids[b], (tok, tok)).T
        same = jnp.concatenate([column == ids[t] for t in range(4)], axis=1)
        parts = []
        for j in range(share // HD):
            q = qkv[b * tok : (b + 1) * tok, j * HD : (j + 1) * HD]
            k = qkv[:, share + j * HD : share + (j + 1) * HD]
            v = qkv[:, 2 * share + j * HD : 2 * share + (j + 1) * HD]
            scores = jnp.where(same, dot(q, k, NT), NEG_FILL)
            raised = jnp.exp(scores - jnp.max(scores, axis=1, keepdims=True))
            probs = raised * (1.0 / jnp.sum(raised, axis=1, keepdims=True))
            probs_out[j, b * tok : (b + 1) * tok, :] = probs
            parts.append(dot(probs.astype(BF), v))
        contexts.append(jnp.concatenate(parts, axis=1).astype(BF))
    ctx_out[...] = jnp.concatenate(contexts, axis=0)


def ffn_kernel(half, x0, x1, ctx, ctx_chip, ctx_core, ctx_far, near, other, up, down, bias, *outs):
    if half == 0:
        nl_out, act_out, slope_out, part_out, unit_out, rate_out, normed_out = outs
    else:
        nl_out, act_out, slope_out, part_out = outs
    mine = nl_out.shape[0]
    tok = mine // 2
    share = ctx.shape[1]
    here = lax.axis_index("head")
    o_bias, a_gain, a_shift, u_bias = [bias[i : i + 1, :] for i in (2, 3, 4, 8)]
    total = jnp.concatenate([x0[...], x1[...]], axis=0).astype(F32) + o_bias
    sums = [jnp.zeros((mine, near.shape[1]), F32)] * 2

    def pick(ref, order):
        order = order[2 * half : 2 * half + 2]
        return jnp.concatenate([ref[i * tok : (i + 1) * tok, :] for i in order], axis=0)

    for flip, ref, order in (
        (0, ctx, (0, 1, 2, 3)),
        (2, ctx_chip, (1, 0, 3, 2)),
        (1, ctx_core, (2, 3, 0, 1)),
        (3, ctx_far, (3, 2, 1, 0)),
    ):
        at = pl.multiple_of((here ^ flip) * share, 64)
        part = pick(ref, order)
        sums = [t + dot(part, w[pl.ds(at, share), :]) for t, w in zip(sums, (near, other))]
    total = total + jnp.concatenate(in_order(*sums), axis=1)
    unit, rate = norm_stats(total)
    normed = unit * a_gain + a_shift
    low = normed.astype(BF)
    nl_out[...] = low
    if half == 0:
        unit_out[...] = unit
        rate_out[...] = jnp.broadcast_to(rate, rate_out.shape)
        normed_out[...] = normed
    pre = dot(low, up[...]) + u_bias
    phi = 0.5 * (1.0 + lax.erf(pre * math.sqrt(0.5)))
    act = (pre * phi).astype(BF)
    act_out[...] = act
    slope_out[...] = phi + pre * jnp.exp(-0.5 * pre * pre) * (1.0 / math.sqrt(2 * math.pi))
    part_out[...] = dot(act, down[...]).astype(part_out.dtype)


def in_order(near, other):
    first = lax.axis_index("head") % 2 == 0
    return [jnp.where(first, near, other), jnp.where(first, other, near)]


def add_kernel(part, got, kept, sent):
    total = part[...] + got[...].astype(F32)
    kept[...] = total
    sent[...] = total.astype(BF)


def swap_blocks(values):
    tok = values.shape[0] // 2
    return jnp.concatenate([values[tok:], values[:tok]], axis=0)


def final_kernel(part, far, normed, up0, up1, bias, layer_out, d_second_out, low_out, grads):
    tok = layer_out.shape[0]
    d_bias, f_gain, f_shift = [bias[i : i + 1, :] for i in (5, 6, 7)]
    second = normed[...] + part[...] + swap_blocks(far[...].astype(F32)) + d_bias
    unit, rate = norm_stats(second)
    layer_out[...] = (unit[:tok] * f_gain + f_shift).astype(BF)
    dy = jnp.concatenate([up0[...], up1[...]], axis=0).astype(F32)
    d_second = norm_back(unit, rate, dy * f_gain)
    d_second_out[...] = d_second
    low_out[...] = d_second.astype(BF)
    sums = [d_second[:tok], dy[:tok] * unit[:tok], dy[:tok]]
    sums = [jnp.sum(s, axis=0, keepdims=True) for s in sums]
    grads[...] = jnp.concatenate(sums + [jnp.zeros_like(grads[3:, :])], axis=0)


def ffn_back_kernel(low, slope, up, down, dh_out, part_out, sum_out):
    d_hidden = dot(low[...], down[...], NT) * slope[...]
    total = jnp.sum(d_hidden, axis=0, keepdims=True)
    sum_out[...] = jnp.broadcast_to(total, sum_out.shape)
    dh = d_hidden.astype(BF)
    dh_out[...] = dh
    part_out[...] = dot(dh, up[...], NT).astype(part_out.dtype)


def split_rows(kept, sent, values):
    if sent is None:
        kept[...] = values
        return
    rows = kept.shape[1]
    mine = lax.axis_index("dp") & 1
    pieces = values.reshape(4, 2, rows, values.shape[1])
    for z in range(4):
        even, odd = pieces[z, 0], pieces[z, 1]
        kept[z] = jnp.where(mine == 0, even, odd)
        sent[z] = jnp.where(mine == 0, odd, even).astype(BF)


def weight_grad_kernel(left0, left1, right0, right1, kept, *sent):
    grad = dot(left0[...], right0[...], TN) + dot(left1[...], right1[...], TN)
    split_rows(kept, sent[0] if sent else None, grad)


def first_back_kernel(part, far, d_second, unit, rate, bias, d_first_out, low_out, grads):
    tok = unit.shape[0] // 2
    a_gain = bias[3:4, :]
    d_normed = d_second[...] + part[...] + swap_blocks(far[...].astype(F32))
    u = unit[...]
    d_first = norm_back(u, rate[:, 0:1], d_normed * a_gain)
    d_first_out[...] = d_first[:tok]
    low_out[...] = d_first.astype(BF)
    sums = [d_first[:tok], d_normed[:tok] * u[:tok], d_normed[:tok]]
    sums = [jnp.sum(s, axis=0, keepdims=True) for s in sums]
    grads[...] = jnp.concatenate(sums + [jnp.zeros_like(grads[3:, :])], axis=0)


def attend_back_kernel(low0, low1, near, other, qkv, probs, d_qkv_out):
    share = qkv.shape[1] // 3
    here = lax.axis_index("head")
    at = pl.multiple_of(here * share, 64)
    halves = [near[pl.ds(at, share), :].astype(F32), other[pl.ds(at, share), :].astype(F32)]
    mine = jnp.concatenate(in_order(*halves), axis=1).astype(BF)
    d_ctx = jnp.concatenate([dot(low0[...], mine, NT), dot(low1[...], mine, NT)], axis=0).astype(BF)
    scale = 1.0 / math.sqrt(HD)
    parts = [[], [], []]
    for j in range(share // HD):
        q = qkv[:, j * HD : (j + 1) * HD]
        k = qkv[:, share + j * HD : share + (j + 1) * HD]
        v = qkv[:, 2 * share + j * HD : 2 * share + (j + 1) * HD]
        grad = d_ctx[:, j * HD : (j + 1) * HD]
        p = probs[j]
        d_probs = dot(grad, v, NT)
        inner = jnp.sum(d_probs * p, axis=1, keepdims=True)
        d_scores = (p * (d_probs - inner)).astype(BF)
        parts[0].append(dot(d_scores, k) * scale)
        parts[1].append(dot(d_scores, q, TN))
        parts[2].append(dot(p.astype(BF), grad, TN))
    d_qkv_out[...] = jnp.concatenate(parts[0] + parts[1] + parts[2], axis=1).astype(BF)


def output_grad_kernel(ctx, ctx_chip, ctx_core, ctx_far, low0, low1, kept, *rest):
    *sent, out = rest
    share = ctx.shape[1]
    width = low0.shape[1]
    tok = ctx.shape[0] // 4
    here = lax.axis_index("head")
    low = jnp.concatenate([low0[...], low1[...]], axis=0).astype(F32)
    low = pltpu.roll(low, lax.rem(width - here * share, width), 1)[:, :share].astype(BF)

    def pick(ref, order):
        return jnp.concatenate([ref[i * tok : (i + 1) * tok, :] for i in order], axis=0)

    for flip, ref, order in (
        (0, ctx, (0, 1, 2, 3)),
        (2, ctx_chip, (1, 0, 3, 2)),
        (1, ctx_core, (2, 3, 0, 1)),
        (3, ctx_far, (3, 2, 1, 0)),
    ):
        at = pl.multiple_of((here ^ flip) * share, 64)
        out[pl.ds(at, share), :] = dot(pick(ref, order), low, TN)
    split_rows(kept, sent[0] if sent else None, out[...])


def last_grad_kernel(rows, x0, x1, x2, x3, d_qkv, grads2, grads1, sum0, sum1, kept, *sent):
    width = x0.shape[1]
    share = width // 4
    here = lax.axis_index("head")
    d = d_qkv[...]
    xs = jnp.concatenate([x0[...], x1[...], x2[...], x3[...]], axis=0)
    weights = dot(xs, d, TN)
    sums = jnp.sum(d.astype(F32), axis=0, keepdims=True)
    zero = jnp.zeros((1, width - share), F32)
    two = jnp.concatenate(
        [
            jnp.concatenate([sums[:, :share], zero], axis=1),
            jnp.concatenate([sums[:, 2 * share :], zero], axis=1),
            jnp.zeros((6, width), F32),
        ],
        axis=0,
    )
    two = pltpu.roll(two, here * share, 1)
    hidden = sum0[...] + sum1[...]
    lane = lax.broadcasted_iota(jnp.int32, (1, width), 1)
    owner = lax.rem(lane, 4 * rows) // rows == here
    ups = [
        jnp.where(owner, pltpu.roll(hidden, lax.rem(width + rows * (here - j), width), 1)[0:1], 0.0)
        for j in range(4)
    ]
    g1, g2 = grads1[...], grads2[...]
    every = jnp.concatenate([two[:2], g1[0:3], g2[0:3]] + ups, axis=0)
    every = jnp.concatenate([every, jnp.zeros((4, width), F32)], axis=0)
    columns = transpose_wide(every)[:, :SPARE]
    split_rows(kept, sent[0] if sent else None, jnp.concatenate([weights, columns], axis=1))


def finish_up_kernel(relative, p0, p1, p2, p3, out):
    width = p0.shape[1]
    piece = out.shape[1] // width * p0.shape[0]
    given = [p[...].astype(F32) for p in (p0, p1, p2, p3)]
    if relative:
        given = by_rank(given)
    out[...] = jnp.concatenate(
        [given[h][:, j * piece : (j + 1) * piece] for j in range(width // piece) for h in range(4)],
        axis=1,
    )


def by_rank(given):
    here = lax.axis_index("head")
    chosen = []
    for i in range(4):
        value = given[i]
        for h in range(1, 4):
            value = jnp.where(here == h, given[h ^ i], value)
        chosen.append(value)
    return chosen


def finish_last_kernel(got, query_out, key_out, value_out, output_out, *bias_outs):
    depth, _, rows, columns = got.shape
    share = query_out.shape[1] // 4
    sums = []
    for h in range(4):
        total = got[0, h].astype(F32)
        for z in range(1, depth):
            total = total + got[z, h].astype(F32)
        sums.append(total)
    for i, out in enumerate((query_out, key_out, value_out)):
        out[...] = jnp.concatenate([t[:, i * share : (i + 1) * share] for t in sums], axis=1)
    every = sums[0] + sums[1] + sums[2] + sums[3]
    output_out[...] = jnp.concatenate([t[:, 3 * share + SPARE :] for t in sums], axis=1)
    every = jnp.concatenate([every[:, 3 * share : 3 * share + SPARE], jnp.zeros((rows, 128 - SPARE), F32)], axis=1)
    every = jnp.concatenate([every, jnp.zeros((128 - rows, 128), F32)], axis=0).T
    for i in range(8):
        bias_outs[i][...] = every[i : i + 1, :rows].reshape(rows)
    long = jnp.concatenate([every[8 + j : 9 + j, :rows] for j in range(4)], axis=1)
    bias_outs[8][...] = long.reshape(4 * rows)


def sum_two_kernel(kept0, got0, kept1, got1, out):
    cut = kept0.shape[2]
    out[:, :, :cut] = (kept0[...] + got0[...].astype(F32)).astype(BF)
    out[:, :, cut:] = (kept1[...] + got1[...].astype(F32)).astype(BF)


def to_owners(summed, rows):
    columns = summed.shape[2]
    got = lax.all_to_all(
        summed.reshape(16 * rows, columns), ALL, 0, 0, tiled=True, axis_index_groups=GROUPS
    )
    return got.reshape(4, 4, rows, columns)


def to_owners_any(whole, rows):
    part = lax.psum_scatter(whole, "dp", scatter_dimension=0, tiled=True).astype(BF)
    return lax.all_to_all(part, "head", 0, 0, tiled=True).reshape(1, 4, rows, -1)


def z_grad_kernel(left0, left1, right0, right1, whole, sent):
    grad = dot(left0[...], right0[...], TN) + dot(left1[...], right1[...], TN)
    whole[...] = grad.reshape(whole.shape)
    sent[...] = whole[lax.rem(lax.axis_index("dp") // 2 + 3, 4)].astype(BF)


def z_step_kernel(step, whole, got, sent):
    at = lax.rem(lax.axis_index("dp") // 2 + 4 - step, 4)
    sent[...] = (whole[at] + got[...].astype(F32)).astype(BF)


def z_sum_kernel(whole, got, kept, sent):
    place = lax.axis_index("dp")
    x = place & 1
    total = whole.at[place // 2]
    kept[...] = total[x] + got[x].astype(F32)
    sent[...] = (total[1 - x] + got[1 - x].astype(F32)).astype(BF)


def heads_kernel(kept, got, *outs):
    rows = outs[0].shape[0]
    total = kept[...] + got[...].astype(F32)
    for out, value in zip(outs, by_rank([total[h * rows : (h + 1) * rows] for h in range(4)])):
        out[...] = value.astype(BF)


def rows_kernel(kept, got, mine, *sent):
    z = lax.axis_index("dp") // 2
    mine[...] = kept[z] + got[z].astype(F32)
    for k in (1, 2, 3):
        at = lax.rem(z + k, 4)
        sent[k - 1][...] = (kept[at] + got[at].astype(F32)).astype(BF)


def sum_kernel(mine, a, b, c, out):
    total = mine[...] + a[...].astype(F32) + b[...].astype(F32) + c[...].astype(F32)
    out[...] = total.astype(out.dtype)


def body(
    layer_input,
    segment_ids,
    upstream,
    query_weight,
    key_weight,
    value_weight,
    query_bias,
    value_bias,
    output_weight,
    output_bias,
    attn_gain,
    attn_shift,
    up_weight,
    up_bias,
    down_weight,
    down_bias,
    final_gain,
    final_shift,
):
    tok, width = layer_input.shape
    cube = lax.axis_size("dp") == 8
    rows = query_weight.shape[0]
    share = width // 4
    mine = 2 * tok

    x1 = lax.ppermute(layer_input, "head", CHIP)
    x2 = lax.ppermute(layer_input, "head", CORE)
    x3 = lax.ppermute(x1, "head", CORE)
    x = (layer_input, x1, x2, x3)

    up1 = lax.ppermute(upstream, "head", CHIP)
    matrices = (query_weight, key_weight, value_weight, output_weight, up_weight, down_weight)
    biases = (
        query_bias,
        value_bias,
        output_bias,
        attn_gain,
        attn_shift,
        down_bias,
        final_gain,
        final_shift,
        up_bias,
    )
    if cube:
        first, *pieces, third = pack(matrices, biases)
        for flip in (3, 2, 1):
            pieces[flip] = lax.ppermute(pieces[flip], "head", [(i, i ^ flip) for i in range(4)])
        first = first.reshape(4, 4 * rows, 3 * share + SPARE)
        if AFTERY == 4:
            first = later(first, *pieces[1:])
        elif AFTERY:
            first = later(first, pieces[AFTERY])
        first = to_owners(first, rows).reshape(4, 4 * rows, 3 * share + SPARE)
        low = third.reshape(4 * rows, width)
        both = call(
            pair_kernel,
            shape((2, 4 * rows, width), BF),
            low,
            lax.ppermute(low, "dp", XSWAP),
            micros=C_MERGE,
        )
        wide = call(
            merge_rest_kernel,
            shape((4, rows, width + width // 2), BF),
            *pieces,
            after=(both,) if MERGE2 else (),
            micros=C_MERGE,
        ).reshape(4 * rows, -1)
        have = [wide, lax.ppermute(wide, "dp", zshift(1))]
        pairs = [both, lax.ppermute(both, "dp", zshift(1))]
        swapped = [lax.ppermute(wide, "dp", XSWAP)]
        hold = ((have[1],) if HOLD1 else ()) + ((swapped[0],) if HOLDX0 else ())
        hold += (pairs[1],) if HOLDB1 else ()
        theirs = lax.ppermute(later(first, *hold) if hold else first, "dp", XSWAP)
        have.append(lax.ppermute(have[1], "dp", zshift(1)))
        pairs.append(lax.ppermute(pairs[1], "dp", zshift(1)))
        hold = ((have[2],) if R2FIRST else ()) + ((pairs[2],) if B2FIRST else ())
        qkv_weight, columns = call(
            join_first_kernel,
            (shape((width, 3 * share), BF), shape((width, SPARE), BF)),
            first,
            theirs,
            after=hold,
            micros=C_JOIN,
        )
    else:
        qkv_weight, columns, up_full, near, down_full = gather_any(matrices, biases)
    qkv, probs, ctx, bias = call(
        functools.partial(attend_kernel, rows),
        (
            shape((4 * tok, 3 * share), BF),
            shape((share // HD, 4 * tok, 4 * tok), F32),
            shape((4 * tok, share), BF),
            shape((16, width), F32),
        ),
        segment_ids.reshape(4, tok),
        *x,
        qkv_weight,
        columns,
        micros=C_ATT,
    )
    ctx_chip = lax.ppermute(later(ctx, up1) if UP1CTX else ctx, "head", CHIP)
    ctx_core = lax.ppermute(ctx, "head", CORE)
    if cube:
        swapped.append(lax.ppermute(have[1], "dp", XSWAP))
        swapped.append(lax.ppermute(have[2], "dp", XSWAP))
        hold = ((ctx,) if R3CTX else ()) + ((swapped[1],) if X1R3 else ())
        have.append(lax.ppermute(later(have[2], *hold) if hold else have[2], "dp", zshift(1)))
        hold = ((ctx_chip,) if X3CHIP else ()) + ((swapped[2],) if XW1 else ())
        swapped.append(lax.ppermute(later(have[3], *hold) if hold else have[3], "dp", XSWAP))
        pairs.append(lax.ppermute(later(pairs[2], ctx) if B3CTX else pairs[2], "dp", zshift(1)))
        ctx_far = lax.ppermute(later(ctx_chip, pairs[3]) if HOLDB3 else ctx_chip, "head", CORE)
        down_full = call(
            join_pairs_kernel,
            shape((width, width), BF),
            *pairs,
            after=(ctx_far,),
            micros=C_JOIN,
        )
        splits = (width, width // 2)
        up_full, near = call(
            functools.partial(join_kernel, splits),
            tuple(shape((width, s), BF) for s in splits),
            *have,
            *swapped,
            after=(ctx_far, up1),
            micros=C_JOIN,
        )
    else:
        ctx_far = lax.ppermute(ctx_chip, "head", CORE)
    contexts = (ctx, ctx_chip, ctx_core, ctx_far)
    other = lax.ppermute(near, "head", CORE)

    def ffn(half):
        outs = (
            shape((mine, width), BF),
            shape((mine, width), BF),
            shape((mine, width), F32),
            shape((mine, width), F32 if half == 0 else BF),
        )
        if half == 0:
            outs += (shape((mine, width), F32), shape((mine, 128), F32), shape((mine, width), F32))
        return call(
            functools.partial(ffn_kernel, half),
            outs,
            *x[2 * half : 2 * half + 2],
            *contexts,
            near,
            other,
            up_full,
            down_full,
            bias,
            micros=C_FFN,
        )

    def pair_sum(part, sent):
        got = lax.ppermute(sent, "head", CORE)
        kept, low = call(
            add_kernel, (shape((mine, width), F32), shape((mine, width), BF)), part, got, micros=C_ADD
        )
        return kept, lax.ppermute(low, "head", CHIP)

    nl1, act1, slope1, sent = ffn(1)
    nl0, act0, slope0, part, unit1, rate1, normed = ffn(0)
    part, far = pair_sum(part, sent)
    layer_output, d_second, ds0, grads2 = call(
        final_kernel,
        (
            shape((tok, width), BF),
            shape((mine, width), F32),
            shape((mine, width), BF),
            shape((8, width), F32),
        ),
        part,
        far,
        normed,
        upstream,
        up1,
        bias,
 micros=C_FIN,
)
    ds1 = lax.ppermute(ds0, "head", CORE)

    def grad_outs(columns):
        if cube:
            dims = (4, width // 8, columns)
            return (shape(dims, F32), shape(dims, BF))
        return (shape((width, columns), F32),)

    def ffn_back(low, slope, kind, after):
        return call(
            ffn_back_kernel,
            (shape((mine, width), BF), shape((mine, width), kind), shape((8, width), F32)),
            low,
            slope,
            up_full,
            down_full,
            after=after,
            micros=C_FB,
        )

    down_first = DOWNFIRST or not cube
    if down_first:
        down_terms = call(
            weight_grad_kernel, grad_outs(width), act0, act1, ds0, ds1, micros=C_WG
        )
    order = (down_terms[-1],) if down_first else ()
    dh1, sent, hidden1 = ffn_back(ds1, slope1, BF, order)
    dh0, part, hidden0 = ffn_back(ds0, slope0, F32, order)
    part, far = pair_sum(part, sent)
    if cube:
        up_whole, up_run = call(
            z_grad_kernel,
            (shape((4, 2, 4 * rows, width), F32), shape((2, 4 * rows, width), BF)),
            nl0,
            nl1,
            dh0,
            dh1,
            after=(part,),
            micros=C_WG,
        )
        up_got = [lax.ppermute(up_run, "dp", zshift(1))]
        if not down_first:
            down_terms = call(
                weight_grad_kernel,
                grad_outs(width),
                act0,
                act1,
                ds0,
                ds1,
                after=(up_run,),
                micros=C_WG,
            )
        order = (down_terms[-1],) + ((up_got[0],) if Z1FIRST else ())
        got_down = lax.ppermute(down_terms[1], "dp", XSWAP)
    else:
        up_terms = call(
            weight_grad_kernel, grad_outs(width), nl0, nl1, dh0, dh1, after=(part,), micros=C_WG
        )
        order = (up_terms[-1],)
    d_first, df0, grads1 = call(
        first_back_kernel,
        (shape((tok, width), F32), shape((mine, width), BF), shape((8, width), F32)),
        part,
        far,
        d_second,
        unit1,
        rate1,
        bias,
        after=order,
        micros=C_FIRST,
    )
    df1 = lax.ppermute(df0, "head", CORE)
    def next_step(step, after):
        run = call(
            functools.partial(z_step_kernel, step),
            shape((2, 4 * rows, width), BF),
            up_whole,
            up_got[-1],
            after=after,
            micros=0.3,
        )
        up_got.append(lax.ppermute(run, "dp", zshift(1)))
        return run

    order = (next_step(2, (df0,)),) if cube else ()
    output_terms = call(
        output_grad_kernel,
        grad_outs(share),
        *contexts,
        df0,
        df1,
        after=order,
        scratch=(pltpu.VMEM((width, share), F32),),
        micros=C_OUT,
    )
    d_qkv = call(
        attend_back_kernel,
        shape((4 * tok, 3 * share), BF),
        df0,
        df1,
        near,
        other,
        qkv,
        probs,
        after=(output_terms[-1],),
        micros=C_AB,
    )
    last_columns = 4 * share + SPARE
    order = ()
    if cube:
        down_kept, *down_sent = call(
            rows_kernel,
            (shape((4 * rows, width), F32),) + (shape((4 * rows, width), BF),) * 3,
            down_terms[0],
            got_down,
            after=(d_qkv,) if ROWSLATE else (df0,),
            micros=C_ROWS,
        )
        down_got = [lax.ppermute(o, "dp", zshift(k)) for k, o in zip((1, 2, 3), down_sent)]
        order = (down_sent[0],)
    last_terms = call(
        functools.partial(last_grad_kernel, rows),
        grad_outs(3 * share + SPARE),
        *x,
        d_qkv,
        grads2,
        grads1,
        hidden0,
        hidden1,
        after=order,
        micros=C_LG,
    )
    order = (last_terms[-1],)
    if cube:
        got_last = lax.ppermute(last_terms[1], "dp", XSWAP)
        got_output = lax.ppermute(output_terms[1], "dp", XSWAP)
        order = (next_step(3, order),)
    part, sent = call(
        input_grad_kernel,
        (shape((mine, width), F32), shape((mine, width), BF)),
        d_qkv,
        qkv_weight,
        after=order,
        micros=C_IN,
    )
    got = lax.ppermute(sent, "head", CORE)
    if cube:
        up_kept, up_cross = call(
            z_sum_kernel,
            (shape((4 * rows, width), F32), shape((4 * rows, width), BF)),
            up_whole,
            up_got[-1],
            after=order + ((sent,) if INFIRST else ()),
            micros=C_SUM,
        )
    part, sent = call(
        input_add_kernel,
        (shape((tok, width), F32), shape((tok, width), BF)),
        part,
        got,
        d_first,
        micros=0.4,
    )
    far = lax.ppermute(sent, "head", CHIP)
    input_grad = call(input_end_kernel, shape((tok, width), BF), part, far, micros=0.3)
    if cube:
        up_pieces = list(
            call(
                heads_kernel,
                (shape((rows, width), BF),) * 4,
                up_kept,
                lax.ppermute(up_cross, "dp", XSWAP),
                micros=C_SUM,
            )
        )
        for flip in (1, 2, 3):
            up_pieces[flip] = lax.ppermute(up_pieces[flip], "head", [(i, i ^ flip) for i in range(4)])
        down_grad = call(
            sum_kernel,
            shape((4 * rows, width), F32),
            down_kept,
            *down_got,
            after=(got_output,) if OEARLY else (),
            micros=C_SUM,
        )
    else:
        up_pieces = to_owners_any(up_terms[0], rows)
        up_pieces = [up_pieces[0, h] for h in range(4)]
        down_grad = lax.psum_scatter(down_terms[0], "dp", scatter_dimension=0, tiled=True)
    up_grad = call(
        functools.partial(finish_up_kernel, cube),
        shape((rows, 4 * width), F32),
        *up_pieces,
    )
    if cube:
        summed = call(
            sum_two_kernel,
            shape((4, 4 * rows, last_columns), BF),
            last_terms[0],
            got_last,
            output_terms[0],
            got_output,
            micros=C_LAST,
        )
        hold = ((up_kept,) if HOLDUP else ()) + ((down_grad,) if HOLDDOWN else ())
        last_got = to_owners(later(summed, *hold) if hold else summed, rows)
    else:
        last_got = to_owners_any(jnp.concatenate([last_terms[0], output_terms[0]], axis=1), rows)
    query_grad, key_grad, value_grad, output_grad, *bias_out = call(
        finish_last_kernel,
        (shape((rows, width), F32),) * 4 + (shape((rows,), F32),) * 8 + (shape((4 * rows,), F32),),
        last_got,
    )

    return (
        layer_output,
        input_grad,
        query_grad,
        key_grad,
        value_grad,
        bias_out[0],
        bias_out[1],
        output_grad,
        bias_out[2],
        bias_out[3],
        bias_out[4],
        up_grad,
        bias_out[8],
        down_grad,
        bias_out[5],
        bias_out[6],
        bias_out[7],
    )


def input_add_kernel(part, got, d_first, kept, sent):
    tok = kept.shape[0]
    total = part[...] + got[...].astype(F32)
    kept[...] = total[:tok] + d_first[...]
    sent[...] = total[tok:].astype(BF)


def input_end_kernel(kept, far, out):
    out[...] = (kept[...] + far[...].astype(F32)).astype(BF)


def input_grad_kernel(d_qkv, weight, part, sent):
    mine = part.shape[0]
    share = weight.shape[1] // 3
    d = d_qkv[...]
    total = dot(d, weight[...], NT)
    part[...] = total[:mine]
    sent[...] = total[mine:].astype(BF)


def solution(mesh):
    matrix = P(ALL, None)
    vector = P(ALL)
    placed = (
        matrix, P("dp"), matrix, matrix, matrix, matrix, vector, vector, matrix,
        vector, vector, vector, matrix, vector, matrix, vector, vector, vector,
    )
    given = (
        matrix, matrix, matrix, matrix, matrix, vector, vector, matrix, vector,
        vector, vector, matrix, vector, matrix, vector, vector, vector,
    )
    return jax.shard_map(body, mesh=mesh, in_specs=placed, out_specs=given, check_vma=False)
```

```python
import functools
import math

import jax
import jax.numpy as jnp
from jax import lax
from jax.experimental import pallas as pl
from jax.experimental.pallas import tpu as pltpu
from jax.sharding import PartitionSpec as P

H = 12
HD = 64
EPSILON = 1e-12
NEG_FILL = -1000000000.0
BF = jnp.bfloat16
F32 = jnp.float32
ALL = ("dp", "head")
CORE = [(i, i ^ 1) for i in range(4)]
CHIP = [(i, i ^ 2) for i in range(4)]
XSWAP = [(i, i ^ 1) for i in range(8)]
GROUPS = [[(2 * z + x) * 4 + h for z in range(4) for h in range(4)] for x in range(2)]


def zshift(k):
    return [(i, (i + 2 * k) % 8) for i in range(8)]


def shape(dims, kind):
    return jax.ShapeDtypeStruct(dims, kind)


def call(kernel, outs, *args, after=(), micros=0.05, limit=8, scratch=()):
    spec = pl.BlockSpec(memory_space=pltpu.VMEM)
    count, extra = len(args), len(after)

    def run(*refs):
        kernel(*refs[:count], *refs[count + extra :])

    named = getattr(kernel, "func", kernel).__name__.removesuffix("_kernel")
    with jax.named_scope(named):
        return pl.pallas_call(
            run,
            out_shape=outs,
            in_specs=[spec] * count + [pl.BlockSpec(memory_space=pl.ANY)] * extra,
            scratch_shapes=list(scratch),
            out_specs=jax.tree.map(lambda _: spec, outs),
            compiler_params=pltpu.CompilerParams(vmem_limit_bytes=limit << 20),
            cost_estimate=pl.CostEstimate(
                flops=int(micros * SCALE * 1e9), bytes_accessed=int(micros * SCALE * 3e6), transcendentals=0
            ),
        )(*args, *after)


def later(value, *after):
    anywhere = pl.BlockSpec(memory_space=pl.ANY)
    return pl.pallas_call(
        lambda *refs: None,
        out_shape=shape(value.shape, value.dtype),
        in_specs=[anywhere] * (1 + len(after)),
        out_specs=anywhere,
        input_output_aliases={0: 0},
        compiler_params=pltpu.CompilerParams(vmem_limit_bytes=1 << 20),
        cost_estimate=pl.CostEstimate(flops=0, bytes_accessed=0, transcendentals=0),
    )(value, *after)


def dot(left, right, dims=((1,), (0,))):
    return lax.dot_general(left, right, (dims, ((), ())), preferred_element_type=F32)


NT = ((1,), (1,))
TN = ((0,), (0,))


def norm_stats(values):
    center = values - jnp.mean(values, axis=-1, keepdims=True)
    spread = jnp.mean(center * center, axis=-1, keepdims=True)
    rate = lax.rsqrt(spread + EPSILON)
    return center * rate, rate


def norm_back(unit, rate, dyg):
    return rate * (
        dyg
        - jnp.mean(dyg, axis=-1, keepdims=True)
        - unit * jnp.mean(dyg * unit, axis=-1, keepdims=True)
    )


def transpose_wide(values):
    rows, lanes = values.shape
    full = jnp.concatenate([values, jnp.zeros((128 - rows, lanes), F32)], axis=0)
    tiles = [full[:, i : i + 128].T for i in range(0, lanes, 128)]
    return jnp.concatenate(tiles, axis=0)


SPARE = 64
R3CTX = 0
HOLD1 = 0
HOLDX0 = 1
R2FIRST = 1
X3CHIP = 0
XW1 = 1
X1R3 = 0
MERGE2 = 0
HOLDB1 = 0
B2FIRST = 0
B3CTX = 0
HOLDB3 = 1
UP1CTX = 1
AFTERY = 0
DOWNFIRST = 0
ROWSLATE = 1
INFIRST = 0
HOLDUP = 0
INHEADS = 0
INFIN = 1
OEARLY = 1
OSTEP = 1
ZLATE = 0
C_FUP = 26
CUT = 384
Z1FIRST = 1
HOLDDOWN = 1
C_MERGE = 0.3
C_JOIN = 0.6
C_ATT = 5
C_FFN = 1.9
C_ADD = 0.2
C_FIN = 1.2
C_WG = 0.8
C_FB = 1.0
C_FIRST = 0.5
C_ROWS = 0.3
C_OUT = 1.7
C_AB = 3.0
C_LG = 0.9
C_IN = 0.8
C_LAST = 10
C_SUM = 0.5
SCALE = 0.3


def pack_kernel(query, key, value, output, up, down, *refs):
    biases, outs, scratch = refs[:9], refs[9:15], refs[15:]
    first, second, third = outs[0], outs[1:5], outs[5]
    matrices, vectors, square, sems = scratch[:6], scratch[6:15], scratch[15], scratch[16]
    pairs = list(zip((query, key, value, output, up, down) + biases, matrices + vectors))
    copies = [pltpu.make_async_copy(a, b, sems.at[i]) for i, (a, b) in enumerate(pairs)]
    for copy in copies:
        copy.start()
    rows, width = query.shape
    share = width // 4
    piece = down.shape[0]
    here = lax.axis_index("head")
    square[...] = jnp.zeros_like(square)
    for copy in copies:
        copy.wait()
    query, key, value, output, up, down = matrices
    for i in range(8):
        square[i : i + 1, 0:rows] = vectors[i][...].reshape(1, rows)
    long = vectors[8][...].reshape(1, piece)
    for j in range(4):
        square[8 + j : 9 + j, 0:rows] = long[:, j * rows : (j + 1) * rows]
    columns = square[...].T[:rows, :SPARE]
    slabs = []
    for h in range(4):
        slab = jnp.concatenate(
            [w[:, h * share : (h + 1) * share] for w in (query, key, value)] + [columns], axis=1
        ).astype(BF)
        for z in range(4):
            first[z, h] = slab
        half = (h % 2) * (width // 2)
        slabs.append(
            jnp.concatenate(
                [up[:, piece * (4 * j + h) : piece * (4 * j + h + 1)] for j in range(width // piece)]
                + [output[:, half : half + width // 2]],
                axis=1,
            )
        )
        third[h] = down[h * rows : (h + 1) * rows, :].astype(BF)
    for flip in range(4):
        chosen = slabs[flip]
        for h in range(1, 4):
            chosen = jnp.where(here == h, slabs[h ^ flip], chosen)
        second[flip][...] = chosen.astype(BF)


def pack(matrices, biases):
    rows, width = matrices[0].shape
    piece = matrices[5].shape[0]
    share = width // 4
    hbm = pl.BlockSpec(memory_space=pltpu.HBM)
    vmem = pl.BlockSpec(memory_space=pltpu.VMEM)
    return pl.pallas_call(
        pack_kernel,
        out_shape=(shape((4, 4, rows, 3 * share + SPARE), BF),)
        + (shape((rows, width + width // 2), BF),) * 4
        + (shape((4, rows, width), BF),),
        in_specs=[hbm] * 15,
        out_specs=(vmem,) * 6,
        scratch_shapes=[pltpu.VMEM(v.shape, F32) for v in matrices + biases]
        + [pltpu.VMEM((128, 128), F32), pltpu.SemaphoreType.DMA((15,))],
        compiler_params=pltpu.CompilerParams(vmem_limit_bytes=56 << 20),
    )(*matrices, *biases)


def gather_any(matrices, biases):
    query, key, value, output, up, down = matrices
    rows, width = query.shape
    piece = down.shape[0]
    share = width // 4

    def by_head(weight):
        return weight.reshape(rows, 4, share).transpose(1, 0, 2)

    columns = jnp.concatenate([jnp.stack(biases[:8]), biases[8].reshape(4, rows)], axis=0).T
    columns = jnp.pad(columns, ((0, 0), (0, SPARE - 12)))
    columns = jnp.broadcast_to(columns[None], (4, rows, SPARE))
    halves = output.reshape(rows, 2, width // 2).transpose(1, 0, 2)
    ups = up.reshape(rows, width // piece, 4, piece).transpose(2, 0, 1, 3).reshape(4, rows, width)
    every = jnp.concatenate(
        [by_head(query), by_head(key), by_head(value), columns, ups]
        + [jnp.concatenate([halves, halves], axis=0)],
        axis=2,
    ).astype(BF)
    every = lax.all_to_all(every, "head", 0, 0, tiled=True).reshape(4 * rows, -1)
    every = jnp.concatenate([every, down.astype(BF)], axis=1)
    every = lax.all_gather(every, "dp", axis=0, tiled=True)
    cuts = [3 * share, 3 * share + SPARE, 3 * share + SPARE + width]
    cuts.append(cuts[-1] + width // 2)
    return jnp.split(every, cuts, axis=1)


def join_first_kernel(mine, theirs, weight, columns):
    rows = mine.shape[1]
    cut = weight.shape[1]
    x = lax.axis_index("dp") & 1
    for z in range(4):
        for flip, ref in ((0, mine), (1, theirs)):
            at = pl.ds(pl.multiple_of((2 * z + (x ^ flip)) * rows, 16), rows)
            weight[at, :] = ref[z, :, :cut]
            columns[at, :] = ref[z, :, cut:]


def merge_rest_kernel(own, core, chip, far, out):
    here = lax.axis_index("head")
    for flip, piece in ((0, own), (1, core), (2, chip), (3, far)):
        out[here ^ flip] = piece[...]


def pair_kernel(own, other, out):
    out[0] = own[...]
    out[1] = other[...]


def join_pairs_kernel(p0, p1, p2, p3, out):
    rows = p0.shape[1]
    place = lax.axis_index("dp")
    for i, piece in enumerate((p0, p1, p2, p3)):
        for flip in range(2):
            owner = lax.rem(place + 8 - 2 * i, 8) ^ flip
            out[pl.ds(pl.multiple_of(owner * rows, 16), rows), :] = piece[flip]


def join_kernel(splits, *refs):
    outs = refs[-len(splits) :]
    pieces = refs[: -len(splits)]
    rows = pieces[0].shape[0]
    place = lax.axis_index("dp")
    for i, piece in enumerate(pieces):
        owner = lax.rem(place + 8 - 2 * (i % 4), 8) ^ (i // 4)
        at = pl.ds(pl.multiple_of(owner * rows, 16), rows)
        column = 0
        for out in outs:
            out[at, :] = piece[:, column : column + out.shape[1]]
            column += out.shape[1]


def attend_kernel(rows, seg, x0, x1, x2, x3, weight, columns, qkv_out, probs_out, ctx_out, bias_out):
    share = ctx_out.shape[1]
    width = x0.shape[1]
    tok = seg.shape[1]
    here = lax.axis_index("head")
    across = columns[...].astype(F32)
    across = jnp.concatenate([across, jnp.zeros((width, 128 - SPARE), F32)], axis=1)
    across = jnp.concatenate(
        [across[i : i + 128].T[:16] for i in range(0, width, 128)], axis=1
    )
    mine = pltpu.roll(across[:8], lax.rem(width - here * share, width), 1)
    lane = lax.broadcasted_iota(jnp.int32, (8, width), 1)
    up_bias = jnp.zeros((8, width), F32)
    for j in range(4):
        moved = pltpu.roll(across[8:], lax.rem(width + rows * (j - here), width), 1)
        up_bias = jnp.where(lax.rem(lane, 4 * rows) // rows == j, moved[j : j + 1], up_bias)
    bias_out[...] = jnp.concatenate([mine[:2], across[2:8], up_bias], axis=0)
    q_bias = mine[0:1, :share]
    v_bias = mine[1:2, :share]
    bias = jnp.concatenate([q_bias, jnp.zeros((1, share), F32), v_bias], axis=1)
    scale = 1.0 / math.sqrt(HD)
    factor = jnp.concatenate(
        [jnp.full((1, share), scale, F32), jnp.ones((1, 2 * share), F32)], axis=1
    )
    xs = jnp.concatenate([x0[...], x1[...], x2[...], x3[...]], axis=0)
    qkv = (dot(xs, weight[...]) + bias).astype(BF)
    qkv = (qkv.astype(F32) * factor).astype(BF)
    qkv_out[...] = qkv
    ids = [seg[pl.ds(here ^ flip, 1), :].astype(F32) for flip in (0, 2, 1, 3)]
    contexts = []
    for b in range(4):
        column = jnp.broadcast_to(ids[b], (tok, tok)).T
        same = jnp.concatenate([column == ids[t] for t in range(4)], axis=1)
        parts = []
        for j in range(share // HD):
            q = qkv[b * tok : (b + 1) * tok, j * HD : (j + 1) * HD]
            k = qkv[:, share + j * HD : share + (j + 1) * HD]
            v = qkv[:, 2 * share + j * HD : 2 * share + (j + 1) * HD]
            scores = jnp.where(same, dot(q, k, NT), NEG_FILL)
            raised = jnp.exp(scores - jnp.max(scores, axis=1, keepdims=True))
            probs = raised * (1.0 / jnp.sum(raised, axis=1, keepdims=True))
            probs_out[j, b * tok : (b + 1) * tok, :] = probs
            parts.append(dot(probs.astype(BF), v))
        contexts.append(jnp.concatenate(parts, axis=1).astype(BF))
    ctx_out[...] = jnp.concatenate(contexts, axis=0)


def ffn_kernel(half, x0, x1, ctx, ctx_chip, ctx_core, ctx_far, near, other, up, down, bias, *outs):
    if half == 0:
        nl_out, act_out, slope_out, part_out, unit_out, rate_out, normed_out = outs
    else:
        nl_out, act_out, slope_out, part_out = outs
    mine = nl_out.shape[0]
    tok = mine // 2
    share = ctx.shape[1]
    here = lax.axis_index("head")
    o_bias, a_gain, a_shift, u_bias = [bias[i : i + 1, :] for i in (2, 3, 4, 8)]
    total = jnp.concatenate([x0[...], x1[...]], axis=0).astype(F32) + o_bias
    sums = [jnp.zeros((mine, near.shape[1]), F32)] * 2

    def pick(ref, order):
        order = order[2 * half : 2 * half + 2]
        return jnp.concatenate([ref[i * tok : (i + 1) * tok, :] for i in order], axis=0)

    for flip, ref, order in (
        (0, ctx, (0, 1, 2, 3)),
        (2, ctx_chip, (1, 0, 3, 2)),
        (1, ctx_core, (2, 3, 0, 1)),
        (3, ctx_far, (3, 2, 1, 0)),
    ):
        at = pl.multiple_of((here ^ flip) * share, 64)
        part = pick(ref, order)
        sums = [t + dot(part, w[pl.ds(at, share), :]) for t, w in zip(sums, (near, other))]
    total = total + jnp.concatenate(in_order(*sums), axis=1)
    unit, rate = norm_stats(total)
    normed = unit * a_gain + a_shift
    low = normed.astype(BF)
    nl_out[...] = low
    if half == 0:
        unit_out[...] = unit
        rate_out[...] = jnp.broadcast_to(rate, rate_out.shape)
        normed_out[...] = normed
    pre = dot(low, up[...]) + u_bias
    phi = 0.5 * (1.0 + lax.erf(pre * math.sqrt(0.5)))
    act = (pre * phi).astype(BF)
    act_out[...] = act
    slope_out[...] = phi + pre * jnp.exp(-0.5 * pre * pre) * (1.0 / math.sqrt(2 * math.pi))
    part_out[...] = dot(act, down[...]).astype(part_out.dtype)


def in_order(near, other):
    first = lax.axis_index("head") % 2 == 0
    return [jnp.where(first, near, other), jnp.where(first, other, near)]


def add_kernel(part, got, kept, sent):
    total = part[...] + got[...].astype(F32)
    kept[...] = total
    sent[...] = total.astype(BF)


def swap_blocks(values):
    tok = values.shape[0] // 2
    return jnp.concatenate([values[tok:], values[:tok]], axis=0)


def final_kernel(part, far, normed, up0, up1, bias, layer_out, d_second_out, low_out, grads):
    tok = layer_out.shape[0]
    d_bias, f_gain, f_shift = [bias[i : i + 1, :] for i in (5, 6, 7)]
    second = normed[...] + part[...] + swap_blocks(far[...].astype(F32)) + d_bias
    unit, rate = norm_stats(second)
    layer_out[...] = (unit[:tok] * f_gain + f_shift).astype(BF)
    dy = jnp.concatenate([up0[...], up1[...]], axis=0).astype(F32)
    d_second = norm_back(unit, rate, dy * f_gain)
    d_second_out[...] = d_second
    low_out[...] = d_second.astype(BF)
    sums = [d_second[:tok], dy[:tok] * unit[:tok], dy[:tok]]
    sums = [jnp.sum(s, axis=0, keepdims=True) for s in sums]
    grads[...] = jnp.concatenate(sums + [jnp.zeros_like(grads[3:, :])], axis=0)


def ffn_back_kernel(low, slope, up, down, dh_out, part_out, sum_out):
    d_hidden = dot(low[...], down[...], NT) * slope[...]
    total = jnp.sum(d_hidden, axis=0, keepdims=True)
    sum_out[...] = jnp.broadcast_to(total, sum_out.shape)
    dh = d_hidden.astype(BF)
    dh_out[...] = dh
    part_out[...] = dot(dh, up[...], NT).astype(part_out.dtype)


def split_rows(kept, sent, values):
    if not sent:
        kept[...] = values
        return
    rows = kept.shape[1]
    mine = lax.axis_index("dp") & 1
    pieces = values.reshape(4, 2, rows, values.shape[1])
    for z in range(4):
        even, odd = pieces[z, 0], pieces[z, 1]
        kept[z] = jnp.where(mine == 0, even, odd)
        leaving = jnp.where(mine == 0, odd, even).astype(BF)
        column = 0
        for out in sent:
            out[z] = leaving[:, column : column + out.shape[2]]
            column += out.shape[2]


def weight_grad_kernel(left0, left1, right0, right1, kept, *sent):
    grad = dot(left0[...], right0[...], TN) + dot(left1[...], right1[...], TN)
    split_rows(kept, sent, grad)


def first_back_kernel(part, far, d_second, unit, rate, bias, d_first_out, low_out, grads):
    tok = unit.shape[0] // 2
    a_gain = bias[3:4, :]
    d_normed = d_second[...] + part[...] + swap_blocks(far[...].astype(F32))
    u = unit[...]
    d_first = norm_back(u, rate[:, 0:1], d_normed * a_gain)
    d_first_out[...] = d_first[:tok]
    low_out[...] = d_first.astype(BF)
    sums = [d_first[:tok], d_normed[:tok] * u[:tok], d_normed[:tok]]
    sums = [jnp.sum(s, axis=0, keepdims=True) for s in sums]
    grads[...] = jnp.concatenate(sums + [jnp.zeros_like(grads[3:, :])], axis=0)


def attend_back_kernel(low0, low1, near, other, qkv, probs, d_qkv_out):
    share = qkv.shape[1] // 3
    here = lax.axis_index("head")
    at = pl.multiple_of(here * share, 64)
    halves = [near[pl.ds(at, share), :].astype(F32), other[pl.ds(at, share), :].astype(F32)]
    mine = jnp.concatenate(in_order(*halves), axis=1).astype(BF)
    d_ctx = jnp.concatenate([dot(low0[...], mine, NT), dot(low1[...], mine, NT)], axis=0).astype(BF)
    scale = 1.0 / math.sqrt(HD)
    parts = [[], [], []]
    for j in range(share // HD):
        q = qkv[:, j * HD : (j + 1) * HD]
        k = qkv[:, share + j * HD : share + (j + 1) * HD]
        v = qkv[:, 2 * share + j * HD : 2 * share + (j + 1) * HD]
        grad = d_ctx[:, j * HD : (j + 1) * HD]
        p = probs[j]
        d_probs = dot(grad, v, NT)
        inner = jnp.sum(d_probs * p, axis=1, keepdims=True)
        d_scores = (p * (d_probs - inner)).astype(BF)
        parts[0].append(dot(d_scores, k) * scale)
        parts[1].append(dot(d_scores, q, TN))
        parts[2].append(dot(p.astype(BF), grad, TN))
    d_qkv_out[...] = jnp.concatenate(parts[0] + parts[1] + parts[2], axis=1).astype(BF)


def output_grad_kernel(ctx, ctx_chip, ctx_core, ctx_far, low0, low1, kept, *rest):
    *sent, out = rest
    share = ctx.shape[1]
    width = low0.shape[1]
    tok = ctx.shape[0] // 4
    here = lax.axis_index("head")
    low = jnp.concatenate([low0[...], low1[...]], axis=0).astype(F32)
    low = pltpu.roll(low, lax.rem(width - here * share, width), 1)[:, :share].astype(BF)

    def pick(ref, order):
        return jnp.concatenate([ref[i * tok : (i + 1) * tok, :] for i in order], axis=0)

    for flip, ref, order in (
        (0, ctx, (0, 1, 2, 3)),
        (2, ctx_chip, (1, 0, 3, 2)),
        (1, ctx_core, (2, 3, 0, 1)),
        (3, ctx_far, (3, 2, 1, 0)),
    ):
        at = pl.multiple_of((here ^ flip) * share, 64)
        out[pl.ds(at, share), :] = dot(pick(ref, order), low, TN)
    split_rows(kept, sent, out[...])


def last_grad_kernel(rows, x0, x1, x2, x3, d_qkv, grads2, grads1, sum0, sum1, kept, *sent):
    width = x0.shape[1]
    share = width // 4
    here = lax.axis_index("head")
    d = d_qkv[...]
    xs = jnp.concatenate([x0[...], x1[...], x2[...], x3[...]], axis=0)
    weights = dot(xs, d, TN)
    sums = jnp.sum(d.astype(F32), axis=0, keepdims=True)
    zero = jnp.zeros((1, width - share), F32)
    two = jnp.concatenate(
        [
            jnp.concatenate([sums[:, :share], zero], axis=1),
            jnp.concatenate([sums[:, 2 * share :], zero], axis=1),
            jnp.zeros((6, width), F32),
        ],
        axis=0,
    )
    two = pltpu.roll(two, here * share, 1)
    hidden = sum0[...] + sum1[...]
    lane = lax.broadcasted_iota(jnp.int32, (1, width), 1)
    owner = lax.rem(lane, 4 * rows) // rows == here
    ups = [
        jnp.where(owner, pltpu.roll(hidden, lax.rem(width + rows * (here - j), width), 1)[0:1], 0.0)
        for j in range(4)
    ]
    g1, g2 = grads1[...], grads2[...]
    every = jnp.concatenate([two[:2], g1[0:3], g2[0:3]] + ups, axis=0)
    every = jnp.concatenate([every, jnp.zeros((4, width), F32)], axis=0)
    columns = transpose_wide(every)[:, :SPARE]
    split_rows(kept, sent, jnp.concatenate([weights, columns], axis=1))


def finish_up_kernel(relative, p0, p1, p2, p3, out):
    width = p0.shape[1]
    piece = out.shape[1] // width * p0.shape[0]
    given = [p[...].astype(F32) for p in (p0, p1, p2, p3)]
    if relative:
        given = by_rank(given)
    out[...] = jnp.concatenate(
        [given[h][:, j * piece : (j + 1) * piece] for j in range(width // piece) for h in range(4)],
        axis=1,
    )


def by_rank(given):
    here = lax.axis_index("head")
    chosen = []
    for i in range(4):
        value = given[i]
        for h in range(1, 4):
            value = jnp.where(here == h, given[h ^ i], value)
        chosen.append(value)
    return chosen


def finish_last_kernel(got, query_out, key_out, value_out, output_out, *bias_outs):
    depth, _, rows, columns = got.shape
    share = query_out.shape[1] // 4
    sums = []
    for h in range(4):
        total = got[0, h].astype(F32)
        for z in range(1, depth):
            total = total + got[z, h].astype(F32)
        sums.append(total)
    for i, out in enumerate((query_out, key_out, value_out)):
        out[...] = jnp.concatenate([t[:, i * share : (i + 1) * share] for t in sums], axis=1)
    every = sums[0] + sums[1] + sums[2] + sums[3]
    output_out[...] = jnp.concatenate([t[:, 3 * share + SPARE :] for t in sums], axis=1)
    every = jnp.concatenate([every[:, 3 * share : 3 * share + SPARE], jnp.zeros((rows, 128 - SPARE), F32)], axis=1)
    every = jnp.concatenate([every, jnp.zeros((128 - rows, 128), F32)], axis=0).T
    for i in range(8):
        bias_outs[i][...] = every[i : i + 1, :rows].reshape(rows)
    long = jnp.concatenate([every[8 + j : 9 + j, :rows] for j in range(4)], axis=1)
    bias_outs[8][...] = long.reshape(4 * rows)


def sum_two_kernel(kept0, kept1, *refs):
    *gots, out = refs
    cut, column = kept0.shape[2], 0
    for got in gots[:-1]:
        part = slice(column, column + got.shape[2])
        out[:, :, part] = (kept0[:, :, part] + got[...].astype(F32)).astype(BF)
        column = part.stop
    out[:, :, cut:] = (kept1[...] + gots[-1][...].astype(F32)).astype(BF)


def to_owners(summed, rows):
    columns = summed.shape[2]
    got = lax.all_to_all(
        summed.reshape(16 * rows, columns), ALL, 0, 0, tiled=True, axis_index_groups=GROUPS
    )
    return got.reshape(4, 4, rows, columns)


def to_owners_any(whole, rows):
    part = lax.psum_scatter(whole, "dp", scatter_dimension=0, tiled=True).astype(BF)
    return lax.all_to_all(part, "head", 0, 0, tiled=True).reshape(1, 4, rows, -1)


def z_grad_kernel(left0, left1, right0, right1, whole, sent):
    grad = dot(left0[...], right0[...], TN) + dot(left1[...], right1[...], TN)
    whole[...] = grad.reshape(whole.shape)
    sent[...] = whole[lax.rem(lax.axis_index("dp") // 2 + 3, 4)].astype(BF)


def z_step_kernel(step, whole, got, sent):
    at = lax.rem(lax.axis_index("dp") // 2 + 4 - step, 4)
    sent[...] = (whole[at] + got[...].astype(F32)).astype(BF)


def z_sum_kernel(whole, got, kept, sent):
    place = lax.axis_index("dp")
    x = place & 1
    total = whole.at[place // 2]
    kept[...] = total[x] + got[x].astype(F32)
    sent[...] = (total[1 - x] + got[1 - x].astype(F32)).astype(BF)


def heads_kernel(kept, got, *outs):
    rows = outs[0].shape[0]
    total = kept[...] + got[...].astype(F32)
    for out, value in zip(outs, by_rank([total[h * rows : (h + 1) * rows] for h in range(4)])):
        out[...] = value.astype(BF)


def rows_kernel(kept, got, mine, *sent):
    z = lax.axis_index("dp") // 2
    mine[...] = kept[z] + got[z].astype(F32)
    for k in (1, 2, 3):
        at = lax.rem(z + k, 4)
        sent[k - 1][...] = (kept[at] + got[at].astype(F32)).astype(BF)


def sum_kernel(mine, a, b, c, out):
    total = mine[...] + a[...].astype(F32) + b[...].astype(F32) + c[...].astype(F32)
    out[...] = total.astype(out.dtype)


def body(
    layer_input,
    segment_ids,
    upstream,
    query_weight,
    key_weight,
    value_weight,
    query_bias,
    value_bias,
    output_weight,
    output_bias,
    attn_gain,
    attn_shift,
    up_weight,
    up_bias,
    down_weight,
    down_bias,
    final_gain,
    final_shift,
):
    tok, width = layer_input.shape
    cube = lax.axis_size("dp") == 8
    rows = query_weight.shape[0]
    share = width // 4
    mine = 2 * tok

    x1 = lax.ppermute(layer_input, "head", CHIP)
    x2 = lax.ppermute(layer_input, "head", CORE)
    x3 = lax.ppermute(x1, "head", CORE)
    x = (layer_input, x1, x2, x3)

    up1 = lax.ppermute(upstream, "head", CHIP)
    matrices = (query_weight, key_weight, value_weight, output_weight, up_weight, down_weight)
    biases = (
        query_bias,
        value_bias,
        output_bias,
        attn_gain,
        attn_shift,
        down_bias,
        final_gain,
        final_shift,
        up_bias,
    )
    if cube:
        first, *pieces, third = pack(matrices, biases)
        for flip in (3, 2, 1):
            pieces[flip] = lax.ppermute(pieces[flip], "head", [(i, i ^ flip) for i in range(4)])
        first = first.reshape(4, 4 * rows, 3 * share + SPARE)
        if AFTERY == 4:
            first = later(first, *pieces[1:])
        elif AFTERY:
            first = later(first, pieces[AFTERY])
        first = to_owners(first, rows).reshape(4, 4 * rows, 3 * share + SPARE)
        low = third.reshape(4 * rows, width)
        both = call(
            pair_kernel,
            shape((2, 4 * rows, width), BF),
            low,
            lax.ppermute(low, "dp", XSWAP),
            micros=C_MERGE,
        )
        wide = call(
            merge_rest_kernel,
            shape((4, rows, width + width // 2), BF),
            *pieces,
            after=(both,) if MERGE2 else (),
            micros=C_MERGE,
        ).reshape(4 * rows, -1)
        have = [wide, lax.ppermute(wide, "dp", zshift(1))]
        pairs = [both, lax.ppermute(both, "dp", zshift(1))]
        swapped = [lax.ppermute(wide, "dp", XSWAP)]
        hold = ((have[1],) if HOLD1 else ()) + ((swapped[0],) if HOLDX0 else ())
        hold += (pairs[1],) if HOLDB1 else ()
        theirs = lax.ppermute(later(first, *hold) if hold else first, "dp", XSWAP)
        have.append(lax.ppermute(have[1], "dp", zshift(1)))
        pairs.append(lax.ppermute(pairs[1], "dp", zshift(1)))
        hold = ((have[2],) if R2FIRST else ()) + ((pairs[2],) if B2FIRST else ())
        qkv_weight, columns = call(
            join_first_kernel,
            (shape((width, 3 * share), BF), shape((width, SPARE), BF)),
            first,
            theirs,
            after=hold,
            micros=C_JOIN,
        )
    else:
        qkv_weight, columns, up_full, near, down_full = gather_any(matrices, biases)
    qkv, probs, ctx, bias = call(
        functools.partial(attend_kernel, rows),
        (
            shape((4 * tok, 3 * share), BF),
            shape((share // HD, 4 * tok, 4 * tok), F32),
            shape((4 * tok, share), BF),
            shape((16, width), F32),
        ),
        segment_ids.reshape(4, tok),
        *x,
        qkv_weight,
        columns,
        micros=C_ATT,
    )
    ctx_chip = lax.ppermute(later(ctx, up1) if UP1CTX else ctx, "head", CHIP)
    ctx_core = lax.ppermute(ctx, "head", CORE)
    if cube:
        swapped.append(lax.ppermute(have[1], "dp", XSWAP))
        swapped.append(lax.ppermute(have[2], "dp", XSWAP))
        hold = ((ctx,) if R3CTX else ()) + ((swapped[1],) if X1R3 else ())
        have.append(lax.ppermute(later(have[2], *hold) if hold else have[2], "dp", zshift(1)))
        hold = ((ctx_chip,) if X3CHIP else ()) + ((swapped[2],) if XW1 else ())
        swapped.append(lax.ppermute(later(have[3], *hold) if hold else have[3], "dp", XSWAP))
        pairs.append(lax.ppermute(later(pairs[2], ctx) if B3CTX else pairs[2], "dp", zshift(1)))
        ctx_far = lax.ppermute(later(ctx_chip, pairs[3]) if HOLDB3 else ctx_chip, "head", CORE)
        down_full = call(
            join_pairs_kernel,
            shape((width, width), BF),
            *pairs,
            after=(ctx_far,),
            micros=C_JOIN,
        )
        splits = (width, width // 2)
        up_full, near = call(
            functools.partial(join_kernel, splits),
            tuple(shape((width, s), BF) for s in splits),
            *have,
            *swapped,
            after=(ctx_far, up1),
            micros=C_JOIN,
        )
    else:
        ctx_far = lax.ppermute(ctx_chip, "head", CORE)
    contexts = (ctx, ctx_chip, ctx_core, ctx_far)
    other = lax.ppermute(near, "head", CORE)

    def ffn(half):
        outs = (
            shape((mine, width), BF),
            shape((mine, width), BF),
            shape((mine, width), F32),
            shape((mine, width), F32 if half == 0 else BF),
        )
        if half == 0:
            outs += (shape((mine, width), F32), shape((mine, 128), F32), shape((mine, width), F32))
        return call(
            functools.partial(ffn_kernel, half),
            outs,
            *x[2 * half : 2 * half + 2],
            *contexts,
            near,
            other,
            up_full,
            down_full,
            bias,
            micros=C_FFN,
        )

    def pair_sum(part, sent):
        got = lax.ppermute(sent, "head", CORE)
        kept, low = call(
            add_kernel, (shape((mine, width), F32), shape((mine, width), BF)), part, got, micros=C_ADD
        )
        return kept, lax.ppermute(low, "head", CHIP)

    nl1, act1, slope1, sent = ffn(1)
    nl0, act0, slope0, part, unit1, rate1, normed = ffn(0)
    part, far = pair_sum(part, sent)
    layer_output, d_second, ds0, grads2 = call(
        final_kernel,
        (
            shape((tok, width), BF),
            shape((mine, width), F32),
            shape((mine, width), BF),
            shape((8, width), F32),
        ),
        part,
        far,
        normed,
        upstream,
        up1,
        bias,
 micros=C_FIN,
)
    ds1 = lax.ppermute(ds0, "head", CORE)

    def grad_outs(columns, cuts=None):
        if cube:
            kept = shape((4, width // 8, columns), F32)
            return (kept,) + tuple(shape((4, width // 8, c), BF) for c in cuts or (columns,))
        return (shape((width, columns), F32),)

    def ffn_back(low, slope, kind, after):
        return call(
            ffn_back_kernel,
            (shape((mine, width), BF), shape((mine, width), kind), shape((8, width), F32)),
            low,
            slope,
            up_full,
            down_full,
            after=after,
            micros=C_FB,
        )

    down_first = DOWNFIRST or not cube
    if down_first:
        down_terms = call(
            weight_grad_kernel, grad_outs(width), act0, act1, ds0, ds1, micros=C_WG
        )
    order = (down_terms[-1],) if down_first else ()
    dh1, sent, hidden1 = ffn_back(ds1, slope1, BF, order)
    dh0, part, hidden0 = ffn_back(ds0, slope0, F32, order)
    part, far = pair_sum(part, sent)
    if cube:
        up_whole, up_run = call(
            z_grad_kernel,
            (shape((4, 2, 4 * rows, width), F32), shape((2, 4 * rows, width), BF)),
            nl0,
            nl1,
            dh0,
            dh1,
            after=(part,),
            micros=C_WG,
        )
        up_got = [lax.ppermute(up_run, "dp", zshift(1))]
        if not down_first:
            down_terms = call(
                weight_grad_kernel,
                grad_outs(width),
                act0,
                act1,
                ds0,
                ds1,
                after=(up_run,),
                micros=C_WG,
            )
        order = (down_terms[-1],) + ((up_got[0],) if Z1FIRST else ())
        got_down = lax.ppermute(down_terms[1], "dp", XSWAP)
    else:
        up_terms = call(
            weight_grad_kernel, grad_outs(width), nl0, nl1, dh0, dh1, after=(part,), micros=C_WG
        )
        order = (up_terms[-1],)
    d_first, df0, grads1 = call(
        first_back_kernel,
        (shape((tok, width), F32), shape((mine, width), BF), shape((8, width), F32)),
        part,
        far,
        d_second,
        unit1,
        rate1,
        bias,
        after=order,
        micros=C_FIRST,
    )
    df1 = lax.ppermute(df0, "head", CORE)
    def next_step(step, after):
        run = call(
            functools.partial(z_step_kernel, step),
            shape((2, 4 * rows, width), BF),
            up_whole,
            up_got[-1],
            after=after,
            micros=0.3,
        )
        up_got.append(lax.ppermute(run, "dp", zshift(1)))
        return run

    order = (next_step(2, (df0,)),) if cube else ()
    output_terms = call(
        output_grad_kernel,
        grad_outs(share),
        *contexts,
        df0,
        df1,
        after=order,
        scratch=(pltpu.VMEM((width, share), F32),),
        micros=C_OUT,
    )
    d_qkv = call(
        attend_back_kernel,
        shape((4 * tok, 3 * share), BF),
        df0,
        df1,
        near,
        other,
        qkv,
        probs,
        after=(output_terms[-1],),
        micros=C_AB,
    )
    last_columns = 4 * share + SPARE
    order = ()
    if cube:
        down_kept, *down_sent = call(
            rows_kernel,
            (shape((4 * rows, width), F32),) + (shape((4 * rows, width), BF),) * 3,
            down_terms[0],
            got_down,
            after=(d_qkv,) if ROWSLATE else (df0,),
            micros=C_ROWS,
        )
        order = (down_sent[0],)
    last_terms = call(
        functools.partial(last_grad_kernel, rows),
        grad_outs(3 * share + SPARE, (CUT, 3 * share + SPARE - CUT) if CUT else None),
        *x,
        d_qkv,
        grads2,
        grads1,
        hidden0,
        hidden1,
        after=order,
        micros=C_LG,
    )
    order = (last_terms[-1],)
    if cube:
        got_last = [lax.ppermute(term, "dp", XSWAP) for term in last_terms[1:]]
        got_output = lax.ppermute(output_terms[1], "dp", XSWAP)
        order = (next_step(3, order + ((got_output,) if OSTEP else ())),)
        down_got = [
            lax.ppermute(later(o, *order) if ZLATE == k else o, "dp", zshift(k))
            for k, o in zip((1, 2, 3), down_sent)
        ]
    part, sent = call(
        input_grad_kernel,
        (shape((mine, width), F32), shape((mine, width), BF)),
        d_qkv,
        qkv_weight,
        after=order,
        micros=C_IN,
    )
    got = lax.ppermute(sent, "head", CORE)
    if cube:
        up_kept, up_cross = call(
            z_sum_kernel,
            (shape((4 * rows, width), F32), shape((4 * rows, width), BF)),
            up_whole,
            up_got[-1],
            after=order + ((sent,) if INFIRST else ()),
            micros=C_SUM,
        )
    part, sent = call(
        input_add_kernel,
        (shape((tok, width), F32), shape((tok, width), BF)),
        part,
        got,
        d_first,
        micros=0.4,
    )
    far = lax.ppermute(sent, "head", CHIP)
    input_grad = call(input_end_kernel, shape((tok, width), BF), part, far, micros=0.3)
    if cube:
        up_pieces = list(
            call(
                heads_kernel,
                (shape((rows, width), BF),) * 4,
                up_kept,
                lax.ppermute(up_cross, "dp", XSWAP),
                after=(input_grad,) if INHEADS else (),
                micros=C_SUM,
            )
        )
        for flip in (1, 2, 3):
            up_pieces[flip] = lax.ppermute(up_pieces[flip], "head", [(i, i ^ flip) for i in range(4)])
        down_grad = call(
            sum_kernel,
            shape((4 * rows, width), F32),
            down_kept,
            *down_got,
            after=(got_output,) if OEARLY else (),
            micros=C_SUM,
        )
    else:
        up_pieces = to_owners_any(up_terms[0], rows)
        up_pieces = [up_pieces[0, h] for h in range(4)]
        down_grad = lax.psum_scatter(down_terms[0], "dp", scatter_dimension=0, tiled=True)
    up_grad = call(
        functools.partial(finish_up_kernel, cube),
        shape((rows, 4 * width), F32),
        *up_pieces,
        after=(input_grad,) if INFIN else (),
        micros=C_FUP,
    )
    if cube:
        summed = call(
            sum_two_kernel,
            shape((4, 4 * rows, last_columns), BF),
            last_terms[0],
            output_terms[0],
            *got_last,
            got_output,
            micros=C_LAST,
        )
        hold = ((up_kept,) if HOLDUP else ()) + ((down_grad,) if HOLDDOWN else ())
        last_got = to_owners(later(summed, *hold) if hold else summed, rows)
    else:
        last_got = to_owners_any(jnp.concatenate([last_terms[0], output_terms[0]], axis=1), rows)
    query_grad, key_grad, value_grad, output_grad, *bias_out = call(
        finish_last_kernel,
        (shape((rows, width), F32),) * 4 + (shape((rows,), F32),) * 8 + (shape((4 * rows,), F32),),
        last_got,
    )

    return (
        layer_output,
        input_grad,
        query_grad,
        key_grad,
        value_grad,
        bias_out[0],
        bias_out[1],
        output_grad,
        bias_out[2],
        bias_out[3],
        bias_out[4],
        up_grad,
        bias_out[8],
        down_grad,
        bias_out[5],
        bias_out[6],
        bias_out[7],
    )


def input_add_kernel(part, got, d_first, kept, sent):
    tok = kept.shape[0]
    total = part[...] + got[...].astype(F32)
    kept[...] = total[:tok] + d_first[...]
    sent[...] = total[tok:].astype(BF)


def input_end_kernel(kept, far, out):
    out[...] = (kept[...] + far[...].astype(F32)).astype(BF)


def input_grad_kernel(d_qkv, weight, part, sent):
    mine = part.shape[0]
    share = weight.shape[1] // 3
    d = d_qkv[...]
    total = dot(d, weight[...], NT)
    part[...] = total[:mine]
    sent[...] = total[mine:].astype(BF)


def solution(mesh):
    matrix = P(ALL, None)
    vector = P(ALL)
    placed = (
        matrix, P("dp"), matrix, matrix, matrix, matrix, vector, vector, matrix,
        vector, vector, vector, matrix, vector, matrix, vector, vector, vector,
    )
    given = (
        matrix, matrix, matrix, matrix, matrix, vector, vector, matrix, vector,
        vector, vector, matrix, vector, matrix, vector, vector, vector,
    )
    return jax.shard_map(body, mesh=mesh, in_specs=placed, out_specs=given, check_vma=False)
```

```python
import functools
import math

import jax
import jax.numpy as jnp
from jax import lax
from jax.experimental import pallas as pl
from jax.experimental.pallas import tpu as pltpu
from jax.sharding import PartitionSpec as P

H = 12
HD = 64
EPSILON = 1e-12
NEG_FILL = -1000000000.0
BF = jnp.bfloat16
F32 = jnp.float32
ALL = ("dp", "head")
CORE = [(i, i ^ 1) for i in range(4)]
CHIP = [(i, i ^ 2) for i in range(4)]
XSWAP = [(i, i ^ 1) for i in range(8)]
GROUPS = [[(2 * z + x) * 4 + h for z in range(4) for h in range(4)] for x in range(2)]


def zshift(k):
    return [(i, (i + 2 * k) % 8) for i in range(8)]


def shape(dims, kind):
    return jax.ShapeDtypeStruct(dims, kind)


def call(kernel, outs, *args, after=(), micros=0.05, limit=8, scratch=()):
    spec = pl.BlockSpec(memory_space=pltpu.VMEM)
    count, extra = len(args), len(after)

    def run(*refs):
        kernel(*refs[:count], *refs[count + extra :])

    named = getattr(kernel, "func", kernel).__name__.removesuffix("_kernel")
    with jax.named_scope(named):
        return pl.pallas_call(
            run,
            out_shape=outs,
            in_specs=[spec] * count + [pl.BlockSpec(memory_space=pl.ANY)] * extra,
            scratch_shapes=list(scratch),
            out_specs=jax.tree.map(lambda _: spec, outs),
            compiler_params=pltpu.CompilerParams(vmem_limit_bytes=limit << 20),
            cost_estimate=pl.CostEstimate(
                flops=int(micros * SCALE * 1e9), bytes_accessed=int(micros * SCALE * 3e6), transcendentals=0
            ),
        )(*args, *after)


def later(value, *after):
    anywhere = pl.BlockSpec(memory_space=pl.ANY)
    return pl.pallas_call(
        lambda *refs: None,
        out_shape=shape(value.shape, value.dtype),
        in_specs=[anywhere] * (1 + len(after)),
        out_specs=anywhere,
        input_output_aliases={0: 0},
        compiler_params=pltpu.CompilerParams(vmem_limit_bytes=1 << 20),
        cost_estimate=pl.CostEstimate(flops=0, bytes_accessed=0, transcendentals=0),
    )(value, *after)


def dot(left, right, dims=((1,), (0,))):
    return lax.dot_general(left, right, (dims, ((), ())), preferred_element_type=F32)


NT = ((1,), (1,))
TN = ((0,), (0,))


def norm_stats(values):
    center = values - jnp.mean(values, axis=-1, keepdims=True)
    spread = jnp.mean(center * center, axis=-1, keepdims=True)
    rate = lax.rsqrt(spread + EPSILON)
    return center * rate, rate


def norm_back(unit, rate, dyg):
    return rate * (
        dyg
        - jnp.mean(dyg, axis=-1, keepdims=True)
        - unit * jnp.mean(dyg * unit, axis=-1, keepdims=True)
    )


def transpose_wide(values):
    rows, lanes = values.shape
    full = jnp.concatenate([values, jnp.zeros((128 - rows, lanes), F32)], axis=0)
    tiles = [full[:, i : i + 128].T for i in range(0, lanes, 128)]
    return jnp.concatenate(tiles, axis=0)


SPARE = 64
R3CTX = 0
HOLD1 = 0
HOLDX0 = 1
R2FIRST = 1
X3CHIP = 0
XW1 = 1
X1R3 = 0
MERGE2 = 0
HOLDB1 = 0
B2FIRST = 0
B3CTX = 0
HOLDB3 = 1
UP1CTX = 0
AFTERY = 0
DOWNFIRST = 0
ROWSLATE = 1
INFIRST = 0
HOLDUP = 0
INHEADS = 0
INFIN = 1
ZSUMFIRST = 1
COREFIRST = 0
OEARLY = 1
OSTEP = 1
ZLATE = 0
C_FUP = 26
CUT = 384
Z1FIRST = 1
HOLDDOWN = 1
C_MERGE = 0.3
C_JOIN = 0.6
C_ATT = 5
C_FFN = 1.9
C_ADD = 0.2
C_FIN = 1.2
C_WG = 0.8
C_FB = 1.0
C_FIRST = 0.5
C_ROWS = 0.3
C_OUT = 1.7
C_AB = 3.0
C_LG = 0.9
C_IN = 0.8
C_LAST = 10
C_SUM = 0.5
SCALE = 0.3


def pack_kernel(query, key, value, output, up, down, *refs):
    biases, outs, scratch = refs[:9], refs[9:15], refs[15:]
    first, second, third = outs[0], outs[1:5], outs[5]
    matrices, vectors, square, sems = scratch[:6], scratch[6:15], scratch[15], scratch[16]
    pairs = list(zip((query, key, value, output, up, down) + biases, matrices + vectors))
    copies = [pltpu.make_async_copy(a, b, sems.at[i]) for i, (a, b) in enumerate(pairs)]
    for copy in copies:
        copy.start()
    rows, width = query.shape
    share = width // 4
    piece = down.shape[0]
    here = lax.axis_index("head")
    square[...] = jnp.zeros_like(square)
    for copy in copies:
        copy.wait()
    query, key, value, output, up, down = matrices
    for i in range(8):
        square[i : i + 1, 0:rows] = vectors[i][...].reshape(1, rows)
    long = vectors[8][...].reshape(1, piece)
    for j in range(4):
        square[8 + j : 9 + j, 0:rows] = long[:, j * rows : (j + 1) * rows]
    columns = square[...].T[:rows, :SPARE]
    slabs = []
    for h in range(4):
        slab = jnp.concatenate(
            [w[:, h * share : (h + 1) * share] for w in (query, key, value)] + [columns], axis=1
        ).astype(BF)
        for z in range(4):
            first[z, h] = slab
        half = (h % 2) * (width // 2)
        slabs.append(
            jnp.concatenate(
                [up[:, piece * (4 * j + h) : piece * (4 * j + h + 1)] for j in range(width // piece)]
                + [output[:, half : half + width // 2]],
                axis=1,
            )
        )
        third[h] = down[h * rows : (h + 1) * rows, :].astype(BF)
    for flip in range(4):
        chosen = slabs[flip]
        for h in range(1, 4):
            chosen = jnp.where(here == h, slabs[h ^ flip], chosen)
        second[flip][...] = chosen.astype(BF)


def pack(matrices, biases):
    rows, width = matrices[0].shape
    piece = matrices[5].shape[0]
    share = width // 4
    hbm = pl.BlockSpec(memory_space=pltpu.HBM)
    vmem = pl.BlockSpec(memory_space=pltpu.VMEM)
    return pl.pallas_call(
        pack_kernel,
        out_shape=(shape((4, 4, rows, 3 * share + SPARE), BF),)
        + (shape((rows, width + width // 2), BF),) * 4
        + (shape((4, rows, width), BF),),
        in_specs=[hbm] * 15,
        out_specs=(vmem,) * 6,
        scratch_shapes=[pltpu.VMEM(v.shape, F32) for v in matrices + biases]
        + [pltpu.VMEM((128, 128), F32), pltpu.SemaphoreType.DMA((15,))],
        compiler_params=pltpu.CompilerParams(vmem_limit_bytes=56 << 20),
    )(*matrices, *biases)


def gather_any(matrices, biases):
    query, key, value, output, up, down = matrices
    rows, width = query.shape
    piece = down.shape[0]
    share = width // 4

    def by_head(weight):
        return weight.reshape(rows, 4, share).transpose(1, 0, 2)

    columns = jnp.concatenate([jnp.stack(biases[:8]), biases[8].reshape(4, rows)], axis=0).T
    columns = jnp.pad(columns, ((0, 0), (0, SPARE - 12)))
    columns = jnp.broadcast_to(columns[None], (4, rows, SPARE))
    halves = output.reshape(rows, 2, width // 2).transpose(1, 0, 2)
    ups = up.reshape(rows, width // piece, 4, piece).transpose(2, 0, 1, 3).reshape(4, rows, width)
    every = jnp.concatenate(
        [by_head(query), by_head(key), by_head(value), columns, ups]
        + [jnp.concatenate([halves, halves], axis=0)],
        axis=2,
    ).astype(BF)
    every = lax.all_to_all(every, "head", 0, 0, tiled=True).reshape(4 * rows, -1)
    every = jnp.concatenate([every, down.astype(BF)], axis=1)
    every = lax.all_gather(every, "dp", axis=0, tiled=True)
    cuts = [3 * share, 3 * share + SPARE, 3 * share + SPARE + width]
    cuts.append(cuts[-1] + width // 2)
    return jnp.split(every, cuts, axis=1)


def join_first_kernel(mine, theirs, weight, columns):
    rows = mine.shape[1]
    cut = weight.shape[1]
    x = lax.axis_index("dp") & 1
    for z in range(4):
        for flip, ref in ((0, mine), (1, theirs)):
            at = pl.ds(pl.multiple_of((2 * z + (x ^ flip)) * rows, 16), rows)
            weight[at, :] = ref[z, :, :cut]
            columns[at, :] = ref[z, :, cut:]


def merge_rest_kernel(own, core, chip, far, out):
    here = lax.axis_index("head")
    for flip, piece in ((0, own), (1, core), (2, chip), (3, far)):
        out[here ^ flip] = piece[...]


def pair_kernel(own, other, out):
    out[0] = own[...]
    out[1] = other[...]


def join_pairs_kernel(p0, p1, p2, p3, out):
    rows = p0.shape[1]
    place = lax.axis_index("dp")
    for i, piece in enumerate((p0, p1, p2, p3)):
        for flip in range(2):
            owner = lax.rem(place + 8 - 2 * i, 8) ^ flip
            out[pl.ds(pl.multiple_of(owner * rows, 16), rows), :] = piece[flip]


def join_kernel(splits, *refs):
    outs = refs[-len(splits) :]
    pieces = refs[: -len(splits)]
    rows = pieces[0].shape[0]
    place = lax.axis_index("dp")
    for i, piece in enumerate(pieces):
        owner = lax.rem(place + 8 - 2 * (i % 4), 8) ^ (i // 4)
        at = pl.ds(pl.multiple_of(owner * rows, 16), rows)
        column = 0
        for out in outs:
            out[at, :] = piece[:, column : column + out.shape[1]]
            column += out.shape[1]


def attend_kernel(rows, seg, x0, x1, x2, x3, weight, columns, qkv_out, probs_out, ctx_out, bias_out):
    share = ctx_out.shape[1]
    width = x0.shape[1]
    tok = seg.shape[1]
    here = lax.axis_index("head")
    across = columns[...].astype(F32)
    across = jnp.concatenate([across, jnp.zeros((width, 128 - SPARE), F32)], axis=1)
    across = jnp.concatenate(
        [across[i : i + 128].T[:16] for i in range(0, width, 128)], axis=1
    )
    mine = pltpu.roll(across[:8], lax.rem(width - here * share, width), 1)
    lane = lax.broadcasted_iota(jnp.int32, (8, width), 1)
    up_bias = jnp.zeros((8, width), F32)
    for j in range(4):
        moved = pltpu.roll(across[8:], lax.rem(width + rows * (j - here), width), 1)
        up_bias = jnp.where(lax.rem(lane, 4 * rows) // rows == j, moved[j : j + 1], up_bias)
    bias_out[...] = jnp.concatenate([mine[:2], across[2:8], up_bias], axis=0)
    q_bias = mine[0:1, :share]
    v_bias = mine[1:2, :share]
    bias = jnp.concatenate([q_bias, jnp.zeros((1, share), F32), v_bias], axis=1)
    scale = 1.0 / math.sqrt(HD)
    factor = jnp.concatenate(
        [jnp.full((1, share), scale, F32), jnp.ones((1, 2 * share), F32)], axis=1
    )
    xs = jnp.concatenate([x0[...], x1[...], x2[...], x3[...]], axis=0)
    qkv = (dot(xs, weight[...]) + bias).astype(BF)
    qkv = (qkv.astype(F32) * factor).astype(BF)
    qkv_out[...] = qkv
    ids = [seg[pl.ds(here ^ flip, 1), :].astype(F32) for flip in (0, 2, 1, 3)]
    contexts = []
    for b in range(4):
        column = jnp.broadcast_to(ids[b], (tok, tok)).T
        same = jnp.concatenate([column == ids[t] for t in range(4)], axis=1)
        parts = []
        for j in range(share // HD):
            q = qkv[b * tok : (b + 1) * tok, j * HD : (j + 1) * HD]
            k = qkv[:, share + j * HD : share + (j + 1) * HD]
            v = qkv[:, 2 * share + j * HD : 2 * share + (j + 1) * HD]
            scores = jnp.where(same, dot(q, k, NT), NEG_FILL)
            raised = jnp.exp(scores - jnp.max(scores, axis=1, keepdims=True))
            probs = raised * (1.0 / jnp.sum(raised, axis=1, keepdims=True))
            probs_out[j, b * tok : (b + 1) * tok, :] = probs
            parts.append(dot(probs.astype(BF), v))
        contexts.append(jnp.concatenate(parts, axis=1).astype(BF))
    ctx_out[...] = jnp.concatenate(contexts, axis=0)


def ffn_kernel(half, x0, x1, ctx, ctx_chip, ctx_core, ctx_far, near, other, up, down, bias, *outs):
    if half == 0:
        nl_out, act_out, slope_out, part_out, unit_out, rate_out, normed_out = outs
    else:
        nl_out, act_out, slope_out, part_out = outs
    mine = nl_out.shape[0]
    tok = mine // 2
    share = ctx.shape[1]
    here = lax.axis_index("head")
    o_bias, a_gain, a_shift, u_bias = [bias[i : i + 1, :] for i in (2, 3, 4, 8)]
    total = jnp.concatenate([x0[...], x1[...]], axis=0).astype(F32) + o_bias
    sums = [jnp.zeros((mine, near.shape[1]), F32)] * 2

    def pick(ref, order):
        order = order[2 * half : 2 * half + 2]
        return jnp.concatenate([ref[i * tok : (i + 1) * tok, :] for i in order], axis=0)

    for flip, ref, order in (
        (0, ctx, (0, 1, 2, 3)),
        (2, ctx_chip, (1, 0, 3, 2)),
        (1, ctx_core, (2, 3, 0, 1)),
        (3, ctx_far, (3, 2, 1, 0)),
    ):
        at = pl.multiple_of((here ^ flip) * share, 64)
        part = pick(ref, order)
        sums = [t + dot(part, w[pl.ds(at, share), :]) for t, w in zip(sums, (near, other))]
    total = total + jnp.concatenate(in_order(*sums), axis=1)
    unit, rate = norm_stats(total)
    normed = unit * a_gain + a_shift
    low = normed.astype(BF)
    nl_out[...] = low
    if half == 0:
        unit_out[...] = unit
        rate_out[...] = jnp.broadcast_to(rate, rate_out.shape)
        normed_out[...] = normed
    pre = dot(low, up[...]) + u_bias
    phi = 0.5 * (1.0 + lax.erf(pre * math.sqrt(0.5)))
    act = (pre * phi).astype(BF)
    act_out[...] = act
    slope_out[...] = phi + pre * jnp.exp(-0.5 * pre * pre) * (1.0 / math.sqrt(2 * math.pi))
    part_out[...] = dot(act, down[...]).astype(part_out.dtype)


def in_order(near, other):
    first = lax.axis_index("head") % 2 == 0
    return [jnp.where(first, near, other), jnp.where(first, other, near)]


def add_kernel(part, got, kept, sent):
    total = part[...] + got[...].astype(F32)
    kept[...] = total
    sent[...] = total.astype(BF)


def swap_blocks(values):
    tok = values.shape[0] // 2
    return jnp.concatenate([values[tok:], values[:tok]], axis=0)


def final_kernel(part, far, normed, up0, up1, bias, layer_out, d_second_out, low_out, grads):
    tok = layer_out.shape[0]
    d_bias, f_gain, f_shift = [bias[i : i + 1, :] for i in (5, 6, 7)]
    second = normed[...] + part[...] + swap_blocks(far[...].astype(F32)) + d_bias
    unit, rate = norm_stats(second)
    layer_out[...] = (unit[:tok] * f_gain + f_shift).astype(BF)
    dy = jnp.concatenate([up0[...], up1[...]], axis=0).astype(F32)
    d_second = norm_back(unit, rate, dy * f_gain)
    d_second_out[...] = d_second
    low_out[...] = d_second.astype(BF)
    sums = [d_second[:tok], dy[:tok] * unit[:tok], dy[:tok]]
    sums = [jnp.sum(s, axis=0, keepdims=True) for s in sums]
    grads[...] = jnp.concatenate(sums + [jnp.zeros_like(grads[3:, :])], axis=0)


def ffn_back_kernel(low, slope, up, down, dh_out, part_out, sum_out):
    d_hidden = dot(low[...], down[...], NT) * slope[...]
    total = jnp.sum(d_hidden, axis=0, keepdims=True)
    sum_out[...] = jnp.broadcast_to(total, sum_out.shape)
    dh = d_hidden.astype(BF)
    dh_out[...] = dh
    part_out[...] = dot(dh, up[...], NT).astype(part_out.dtype)


def split_rows(kept, sent, values):
    if not sent:
        kept[...] = values
        return
    rows = kept.shape[1]
    mine = lax.axis_index("dp") & 1
    pieces = values.reshape(4, 2, rows, values.shape[1])
    for z in range(4):
        even, odd = pieces[z, 0], pieces[z, 1]
        kept[z] = jnp.where(mine == 0, even, odd)
        leaving = jnp.where(mine == 0, odd, even).astype(BF)
        column = 0
        for out in sent:
            out[z] = leaving[:, column : column + out.shape[2]]
            column += out.shape[2]


def weight_grad_kernel(left0, left1, right0, right1, kept, *sent):
    grad = dot(left0[...], right0[...], TN) + dot(left1[...], right1[...], TN)
    split_rows(kept, sent, grad)


def first_back_kernel(part, far, d_second, unit, rate, bias, d_first_out, low_out, grads):
    tok = unit.shape[0] // 2
    a_gain = bias[3:4, :]
    d_normed = d_second[...] + part[...] + swap_blocks(far[...].astype(F32))
    u = unit[...]
    d_first = norm_back(u, rate[:, 0:1], d_normed * a_gain)
    d_first_out[...] = d_first[:tok]
    low_out[...] = d_first.astype(BF)
    sums = [d_first[:tok], d_normed[:tok] * u[:tok], d_normed[:tok]]
    sums = [jnp.sum(s, axis=0, keepdims=True) for s in sums]
    grads[...] = jnp.concatenate(sums + [jnp.zeros_like(grads[3:, :])], axis=0)


def attend_back_kernel(low0, low1, near, other, qkv, probs, d_qkv_out):
    share = qkv.shape[1] // 3
    here = lax.axis_index("head")
    at = pl.multiple_of(here * share, 64)
    halves = [near[pl.ds(at, share), :].astype(F32), other[pl.ds(at, share), :].astype(F32)]
    mine = jnp.concatenate(in_order(*halves), axis=1).astype(BF)
    d_ctx = jnp.concatenate([dot(low0[...], mine, NT), dot(low1[...], mine, NT)], axis=0).astype(BF)
    scale = 1.0 / math.sqrt(HD)
    parts = [[], [], []]
    for j in range(share // HD):
        q = qkv[:, j * HD : (j + 1) * HD]
        k = qkv[:, share + j * HD : share + (j + 1) * HD]
        v = qkv[:, 2 * share + j * HD : 2 * share + (j + 1) * HD]
        grad = d_ctx[:, j * HD : (j + 1) * HD]
        p = probs[j]
        d_probs = dot(grad, v, NT)
        inner = jnp.sum(d_probs * p, axis=1, keepdims=True)
        d_scores = (p * (d_probs - inner)).astype(BF)
        parts[0].append(dot(d_scores, k) * scale)
        parts[1].append(dot(d_scores, q, TN))
        parts[2].append(dot(p.astype(BF), grad, TN))
    d_qkv_out[...] = jnp.concatenate(parts[0] + parts[1] + parts[2], axis=1).astype(BF)


def output_grad_kernel(ctx, ctx_chip, ctx_core, ctx_far, low0, low1, kept, *rest):
    *sent, out = rest
    share = ctx.shape[1]
    width = low0.shape[1]
    tok = ctx.shape[0] // 4
    here = lax.axis_index("head")
    low = jnp.concatenate([low0[...], low1[...]], axis=0).astype(F32)
    low = pltpu.roll(low, lax.rem(width - here * share, width), 1)[:, :share].astype(BF)

    def pick(ref, order):
        return jnp.concatenate([ref[i * tok : (i + 1) * tok, :] for i in order], axis=0)

    for flip, ref, order in (
        (0, ctx, (0, 1, 2, 3)),
        (2, ctx_chip, (1, 0, 3, 2)),
        (1, ctx_core, (2, 3, 0, 1)),
        (3, ctx_far, (3, 2, 1, 0)),
    ):
        at = pl.multiple_of((here ^ flip) * share, 64)
        out[pl.ds(at, share), :] = dot(pick(ref, order), low, TN)
    split_rows(kept, sent, out[...])


def last_grad_kernel(rows, x0, x1, x2, x3, d_qkv, grads2, grads1, sum0, sum1, kept, *sent):
    width = x0.shape[1]
    share = width // 4
    here = lax.axis_index("head")
    d = d_qkv[...]
    xs = jnp.concatenate([x0[...], x1[...], x2[...], x3[...]], axis=0)
    weights = dot(xs, d, TN)
    sums = jnp.sum(d.astype(F32), axis=0, keepdims=True)
    zero = jnp.zeros((1, width - share), F32)
    two = jnp.concatenate(
        [
            jnp.concatenate([sums[:, :share], zero], axis=1),
            jnp.concatenate([sums[:, 2 * share :], zero], axis=1),
            jnp.zeros((6, width), F32),
        ],
        axis=0,
    )
    two = pltpu.roll(two, here * share, 1)
    hidden = sum0[...] + sum1[...]
    lane = lax.broadcasted_iota(jnp.int32, (1, width), 1)
    owner = lax.rem(lane, 4 * rows) // rows == here
    ups = [
        jnp.where(owner, pltpu.roll(hidden, lax.rem(width + rows * (here - j), width), 1)[0:1], 0.0)
        for j in range(4)
    ]
    g1, g2 = grads1[...], grads2[...]
    every = jnp.concatenate([two[:2], g1[0:3], g2[0:3]] + ups, axis=0)
    every = jnp.concatenate([every, jnp.zeros((4, width), F32)], axis=0)
    columns = transpose_wide(every)[:, :SPARE]
    split_rows(kept, sent, jnp.concatenate([weights, columns], axis=1))


def finish_up_kernel(relative, p0, p1, p2, p3, out):
    width = p0.shape[1]
    piece = out.shape[1] // width * p0.shape[0]
    given = [p[...].astype(F32) for p in (p0, p1, p2, p3)]
    if relative:
        given = by_rank(given)
    out[...] = jnp.concatenate(
        [given[h][:, j * piece : (j + 1) * piece] for j in range(width // piece) for h in range(4)],
        axis=1,
    )


def by_rank(given):
    here = lax.axis_index("head")
    chosen = []
    for i in range(4):
        value = given[i]
        for h in range(1, 4):
            value = jnp.where(here == h, given[h ^ i], value)
        chosen.append(value)
    return chosen


def finish_last_kernel(got, query_out, key_out, value_out, output_out, *bias_outs):
    depth, _, rows, columns = got.shape
    share = query_out.shape[1] // 4
    sums = []
    for h in range(4):
        total = got[0, h].astype(F32)
        for z in range(1, depth):
            total = total + got[z, h].astype(F32)
        sums.append(total)
    for i, out in enumerate((query_out, key_out, value_out)):
        out[...] = jnp.concatenate([t[:, i * share : (i + 1) * share] for t in sums], axis=1)
    every = sums[0] + sums[1] + sums[2] + sums[3]
    output_out[...] = jnp.concatenate([t[:, 3 * share + SPARE :] for t in sums], axis=1)
    every = jnp.concatenate([every[:, 3 * share : 3 * share + SPARE], jnp.zeros((rows, 128 - SPARE), F32)], axis=1)
    every = jnp.concatenate([every, jnp.zeros((128 - rows, 128), F32)], axis=0).T
    for i in range(8):
        bias_outs[i][...] = every[i : i + 1, :rows].reshape(rows)
    long = jnp.concatenate([every[8 + j : 9 + j, :rows] for j in range(4)], axis=1)
    bias_outs[8][...] = long.reshape(4 * rows)


def sum_two_kernel(kept0, kept1, *refs):
    *gots, out = refs
    cut, column = kept0.shape[2], 0
    for got in gots[:-1]:
        part = slice(column, column + got.shape[2])
        out[:, :, part] = (kept0[:, :, part] + got[...].astype(F32)).astype(BF)
        column = part.stop
    out[:, :, cut:] = (kept1[...] + gots[-1][...].astype(F32)).astype(BF)


def to_owners(summed, rows):
    columns = summed.shape[2]
    got = lax.all_to_all(
        summed.reshape(16 * rows, columns), ALL, 0, 0, tiled=True, axis_index_groups=GROUPS
    )
    return got.reshape(4, 4, rows, columns)


def to_owners_any(whole, rows):
    part = lax.psum_scatter(whole, "dp", scatter_dimension=0, tiled=True).astype(BF)
    return lax.all_to_all(part, "head", 0, 0, tiled=True).reshape(1, 4, rows, -1)


def z_grad_kernel(left0, left1, right0, right1, whole, sent):
    grad = dot(left0[...], right0[...], TN) + dot(left1[...], right1[...], TN)
    whole[...] = grad.reshape(whole.shape)
    sent[...] = whole[lax.rem(lax.axis_index("dp") // 2 + 3, 4)].astype(BF)


def z_step_kernel(step, whole, got, sent):
    at = lax.rem(lax.axis_index("dp") // 2 + 4 - step, 4)
    sent[...] = (whole[at] + got[...].astype(F32)).astype(BF)


def z_sum_kernel(whole, got, kept, sent):
    place = lax.axis_index("dp")
    x = place & 1
    total = whole.at[place // 2]
    kept[...] = total[x] + got[x].astype(F32)
    sent[...] = (total[1 - x] + got[1 - x].astype(F32)).astype(BF)


def heads_kernel(kept, got, *outs):
    rows = outs[0].shape[0]
    total = kept[...] + got[...].astype(F32)
    for out, value in zip(outs, by_rank([total[h * rows : (h + 1) * rows] for h in range(4)])):
        out[...] = value.astype(BF)


def rows_kernel(kept, got, mine, *sent):
    z = lax.axis_index("dp") // 2
    mine[...] = kept[z] + got[z].astype(F32)
    for k in (1, 2, 3):
        at = lax.rem(z + k, 4)
        sent[k - 1][...] = (kept[at] + got[at].astype(F32)).astype(BF)


def sum_kernel(mine, a, b, c, out):
    total = mine[...] + a[...].astype(F32) + b[...].astype(F32) + c[...].astype(F32)
    out[...] = total.astype(out.dtype)


def body(
    layer_input,
    segment_ids,
    upstream,
    query_weight,
    key_weight,
    value_weight,
    query_bias,
    value_bias,
    output_weight,
    output_bias,
    attn_gain,
    attn_shift,
    up_weight,
    up_bias,
    down_weight,
    down_bias,
    final_gain,
    final_shift,
):
    tok, width = layer_input.shape
    cube = lax.axis_size("dp") == 8
    rows = query_weight.shape[0]
    share = width // 4
    mine = 2 * tok

    x1 = lax.ppermute(layer_input, "head", CHIP)
    x2 = lax.ppermute(layer_input, "head", CORE)
    x3 = lax.ppermute(x1, "head", CORE)
    x = (layer_input, x1, x2, x3)

    up1 = lax.ppermute(upstream, "head", CHIP)
    matrices = (query_weight, key_weight, value_weight, output_weight, up_weight, down_weight)
    biases = (
        query_bias,
        value_bias,
        output_bias,
        attn_gain,
        attn_shift,
        down_bias,
        final_gain,
        final_shift,
        up_bias,
    )
    if cube:
        first, *pieces, third = pack(matrices, biases)
        for flip in (3, 2, 1):
            pieces[flip] = lax.ppermute(pieces[flip], "head", [(i, i ^ flip) for i in range(4)])
        first = first.reshape(4, 4 * rows, 3 * share + SPARE)
        if AFTERY == 4:
            first = later(first, *pieces[1:])
        elif AFTERY:
            first = later(first, pieces[AFTERY])
        first = to_owners(first, rows).reshape(4, 4 * rows, 3 * share + SPARE)
        low = third.reshape(4 * rows, width)
        both = call(
            pair_kernel,
            shape((2, 4 * rows, width), BF),
            low,
            lax.ppermute(low, "dp", XSWAP),
            micros=C_MERGE,
        )
        wide = call(
            merge_rest_kernel,
            shape((4, rows, width + width // 2), BF),
            *pieces,
            after=(both,) if MERGE2 else (),
            micros=C_MERGE,
        ).reshape(4 * rows, -1)
        have = [wide, lax.ppermute(wide, "dp", zshift(1))]
        pairs = [both, lax.ppermute(both, "dp", zshift(1))]
        swapped = [lax.ppermute(wide, "dp", XSWAP)]
        hold = ((have[1],) if HOLD1 else ()) + ((swapped[0],) if HOLDX0 else ())
        hold += (pairs[1],) if HOLDB1 else ()
        theirs = lax.ppermute(later(first, *hold) if hold else first, "dp", XSWAP)
        have.append(lax.ppermute(have[1], "dp", zshift(1)))
        pairs.append(lax.ppermute(pairs[1], "dp", zshift(1)))
        hold = ((have[2],) if R2FIRST else ()) + ((pairs[2],) if B2FIRST else ())
        qkv_weight, columns = call(
            join_first_kernel,
            (shape((width, 3 * share), BF), shape((width, SPARE), BF)),
            first,
            theirs,
            after=hold,
            micros=C_JOIN,
        )
    else:
        qkv_weight, columns, up_full, near, down_full = gather_any(matrices, biases)
    qkv, probs, ctx, bias = call(
        functools.partial(attend_kernel, rows),
        (
            shape((4 * tok, 3 * share), BF),
            shape((share // HD, 4 * tok, 4 * tok), F32),
            shape((4 * tok, share), BF),
            shape((16, width), F32),
        ),
        segment_ids.reshape(4, tok),
        *x,
        qkv_weight,
        columns,
        micros=C_ATT,
    )
    ctx_chip = lax.ppermute(later(ctx, up1) if UP1CTX else ctx, "head", CHIP)
    ctx_core = lax.ppermute(ctx, "head", CORE)
    if cube:
        swapped.append(lax.ppermute(have[1], "dp", XSWAP))
        swapped.append(lax.ppermute(have[2], "dp", XSWAP))
        hold = ((ctx,) if R3CTX else ()) + ((swapped[1],) if X1R3 else ())
        have.append(lax.ppermute(later(have[2], *hold) if hold else have[2], "dp", zshift(1)))
        hold = ((ctx_chip,) if X3CHIP else ()) + ((swapped[2],) if XW1 else ())
        swapped.append(lax.ppermute(later(have[3], *hold) if hold else have[3], "dp", XSWAP))
        pairs.append(lax.ppermute(later(pairs[2], ctx) if B3CTX else pairs[2], "dp", zshift(1)))
        ctx_far = lax.ppermute(later(ctx_chip, pairs[3], *((ctx_core,) if COREFIRST else ())) if HOLDB3 else ctx_chip, "head", CORE)
        down_full = call(
            join_pairs_kernel,
            shape((width, width), BF),
            *pairs,
            after=(ctx_far,),
            micros=C_JOIN,
        )
        splits = (width, width // 2)
        up_full, near = call(
            functools.partial(join_kernel, splits),
            tuple(shape((width, s), BF) for s in splits),
            *have,
            *swapped,
            after=(ctx_far, up1),
            micros=C_JOIN,
        )
    else:
        ctx_far = lax.ppermute(ctx_chip, "head", CORE)
    contexts = (ctx, ctx_chip, ctx_core, ctx_far)
    other = lax.ppermute(near, "head", CORE)

    def ffn(half):
        outs = (
            shape((mine, width), BF),
            shape((mine, width), BF),
            shape((mine, width), F32),
            shape((mine, width), F32 if half == 0 else BF),
        )
        if half == 0:
            outs += (shape((mine, width), F32), shape((mine, 128), F32), shape((mine, width), F32))
        return call(
            functools.partial(ffn_kernel, half),
            outs,
            *x[2 * half : 2 * half + 2],
            *contexts,
            near,
            other,
            up_full,
            down_full,
            bias,
            micros=C_FFN,
        )

    def pair_sum(part, sent):
        got = lax.ppermute(sent, "head", CORE)
        kept, low = call(
            add_kernel, (shape((mine, width), F32), shape((mine, width), BF)), part, got, micros=C_ADD
        )
        return kept, lax.ppermute(low, "head", CHIP)

    nl1, act1, slope1, sent = ffn(1)
    nl0, act0, slope0, part, unit1, rate1, normed = ffn(0)
    part, far = pair_sum(part, sent)
    layer_output, d_second, ds0, grads2 = call(
        final_kernel,
        (
            shape((tok, width), BF),
            shape((mine, width), F32),
            shape((mine, width), BF),
            shape((8, width), F32),
        ),
        part,
        far,
        normed,
        upstream,
        up1,
        bias,
 micros=C_FIN,
)
    ds1 = lax.ppermute(ds0, "head", CORE)

    def grad_outs(columns, cuts=None):
        if cube:
            kept = shape((4, width // 8, columns), F32)
            return (kept,) + tuple(shape((4, width // 8, c), BF) for c in cuts or (columns,))
        return (shape((width, columns), F32),)

    def ffn_back(low, slope, kind, after):
        return call(
            ffn_back_kernel,
            (shape((mine, width), BF), shape((mine, width), kind), shape((8, width), F32)),
            low,
            slope,
            up_full,
            down_full,
            after=after,
            micros=C_FB,
        )

    down_first = DOWNFIRST or not cube
    if down_first:
        down_terms = call(
            weight_grad_kernel, grad_outs(width), act0, act1, ds0, ds1, micros=C_WG
        )
    order = (down_terms[-1],) if down_first else ()
    dh1, sent, hidden1 = ffn_back(ds1, slope1, BF, order)
    dh0, part, hidden0 = ffn_back(ds0, slope0, F32, order)
    part, far = pair_sum(part, sent)
    if cube:
        up_whole, up_run = call(
            z_grad_kernel,
            (shape((4, 2, 4 * rows, width), F32), shape((2, 4 * rows, width), BF)),
            nl0,
            nl1,
            dh0,
            dh1,
            after=(part,),
            micros=C_WG,
        )
        up_got = [lax.ppermute(up_run, "dp", zshift(1))]
        if not down_first:
            down_terms = call(
                weight_grad_kernel,
                grad_outs(width),
                act0,
                act1,
                ds0,
                ds1,
                after=(up_run,),
                micros=C_WG,
            )
        order = (down_terms[-1],) + ((up_got[0],) if Z1FIRST else ())
        got_down = lax.ppermute(down_terms[1], "dp", XSWAP)
    else:
        up_terms = call(
            weight_grad_kernel, grad_outs(width), nl0, nl1, dh0, dh1, after=(part,), micros=C_WG
        )
        order = (up_terms[-1],)
    d_first, df0, grads1 = call(
        first_back_kernel,
        (shape((tok, width), F32), shape((mine, width), BF), shape((8, width), F32)),
        part,
        far,
        d_second,
        unit1,
        rate1,
        bias,
        after=order,
        micros=C_FIRST,
    )
    df1 = lax.ppermute(df0, "head", CORE)
    def next_step(step, after):
        run = call(
            functools.partial(z_step_kernel, step),
            shape((2, 4 * rows, width), BF),
            up_whole,
            up_got[-1],
            after=after,
            micros=0.3,
        )
        up_got.append(lax.ppermute(run, "dp", zshift(1)))
        return run

    order = (next_step(2, (df0,)),) if cube else ()
    output_terms = call(
        output_grad_kernel,
        grad_outs(share),
        *contexts,
        df0,
        df1,
        after=order,
        scratch=(pltpu.VMEM((width, share), F32),),
        micros=C_OUT,
    )
    d_qkv = call(
        attend_back_kernel,
        shape((4 * tok, 3 * share), BF),
        df0,
        df1,
        near,
        other,
        qkv,
        probs,
        after=(output_terms[-1],),
        micros=C_AB,
    )
    last_columns = 4 * share + SPARE
    order = ()
    if cube:
        down_kept, *down_sent = call(
            rows_kernel,
            (shape((4 * rows, width), F32),) + (shape((4 * rows, width), BF),) * 3,
            down_terms[0],
            got_down,
            after=(d_qkv,) if ROWSLATE else (df0,),
            micros=C_ROWS,
        )
        order = (down_sent[0],)
    last_terms = call(
        functools.partial(last_grad_kernel, rows),
        grad_outs(3 * share + SPARE, (CUT, 3 * share + SPARE - CUT) if CUT else None),
        *x,
        d_qkv,
        grads2,
        grads1,
        hidden0,
        hidden1,
        after=order,
        micros=C_LG,
    )
    order = (last_terms[-1],)
    if cube:
        got_last = [lax.ppermute(term, "dp", XSWAP) for term in last_terms[1:]]
        got_output = lax.ppermute(output_terms[1], "dp", XSWAP)
        order = (next_step(3, order + ((got_output,) if OSTEP else ())),)
        down_got = [
            lax.ppermute(later(o, *order) if ZLATE == k else o, "dp", zshift(k))
            for k, o in zip((1, 2, 3), down_sent)
        ]
    part, sent = call(
        input_grad_kernel,
        (shape((mine, width), F32), shape((mine, width), BF)),
        d_qkv,
        qkv_weight,
        after=order,
        micros=C_IN,
    )
    got = lax.ppermute(sent, "head", CORE)
    if cube:
        up_kept, up_cross = call(
            z_sum_kernel,
            (shape((4 * rows, width), F32), shape((4 * rows, width), BF)),
            up_whole,
            up_got[-1],
            after=order + ((sent,) if INFIRST else ()),
            micros=C_SUM,
        )
    part, sent = call(
        input_add_kernel,
        (shape((tok, width), F32), shape((tok, width), BF)),
        part,
        got,
        d_first,
        after=(up_cross,) if ZSUMFIRST and cube else (),
        micros=0.4,
    )
    far = lax.ppermute(sent, "head", CHIP)
    input_grad = call(input_end_kernel, shape((tok, width), BF), part, far, micros=0.3)
    if cube:
        up_pieces = list(
            call(
                heads_kernel,
                (shape((rows, width), BF),) * 4,
                up_kept,
                lax.ppermute(up_cross, "dp", XSWAP),
                after=(input_grad,) if INHEADS else (),
                micros=C_SUM,
            )
        )
        for flip in (1, 2, 3):
            up_pieces[flip] = lax.ppermute(up_pieces[flip], "head", [(i, i ^ flip) for i in range(4)])
        down_grad = call(
            sum_kernel,
            shape((4 * rows, width), F32),
            down_kept,
            *down_got,
            after=(got_output,) if OEARLY else (),
            micros=C_SUM,
        )
    else:
        up_pieces = to_owners_any(up_terms[0], rows)
        up_pieces = [up_pieces[0, h] for h in range(4)]
        down_grad = lax.psum_scatter(down_terms[0], "dp", scatter_dimension=0, tiled=True)
    up_grad = call(
        functools.partial(finish_up_kernel, cube),
        shape((rows, 4 * width), F32),
        *up_pieces,
        after=(input_grad,) if INFIN else (),
        micros=C_FUP,
    )
    if cube:
        summed = call(
            sum_two_kernel,
            shape((4, 4 * rows, last_columns), BF),
            last_terms[0],
            output_terms[0],
            *got_last,
            got_output,
            micros=C_LAST,
        )
        hold = ((up_kept,) if HOLDUP else ()) + ((down_grad,) if HOLDDOWN else ())
        last_got = to_owners(later(summed, *hold) if hold else summed, rows)
    else:
        last_got = to_owners_any(jnp.concatenate([last_terms[0], output_terms[0]], axis=1), rows)
    query_grad, key_grad, value_grad, output_grad, *bias_out = call(
        finish_last_kernel,
        (shape((rows, width), F32),) * 4 + (shape((rows,), F32),) * 8 + (shape((4 * rows,), F32),),
        last_got,
    )

    return (
        layer_output,
        input_grad,
        query_grad,
        key_grad,
        value_grad,
        bias_out[0],
        bias_out[1],
        output_grad,
        bias_out[2],
        bias_out[3],
        bias_out[4],
        up_grad,
        bias_out[8],
        down_grad,
        bias_out[5],
        bias_out[6],
        bias_out[7],
    )


def input_add_kernel(part, got, d_first, kept, sent):
    tok = kept.shape[0]
    total = part[...] + got[...].astype(F32)
    kept[...] = total[:tok] + d_first[...]
    sent[...] = total[tok:].astype(BF)


def input_end_kernel(kept, far, out):
    out[...] = (kept[...] + far[...].astype(F32)).astype(BF)


def input_grad_kernel(d_qkv, weight, part, sent):
    mine = part.shape[0]
    share = weight.shape[1] // 3
    d = d_qkv[...]
    total = dot(d, weight[...], NT)
    part[...] = total[:mine]
    sent[...] = total[mine:].astype(BF)


def solution(mesh):
    matrix = P(ALL, None)
    vector = P(ALL)
    placed = (
        matrix, P("dp"), matrix, matrix, matrix, matrix, vector, vector, matrix,
        vector, vector, vector, matrix, vector, matrix, vector, vector, vector,
    )
    given = (
        matrix, matrix, matrix, matrix, matrix, vector, vector, matrix, vector,
        vector, vector, matrix, vector, matrix, vector, vector, vector,
    )
    return jax.shard_map(body, mesh=mesh, in_specs=placed, out_specs=given, check_vma=False)
```

```python
import functools
import math

import jax
import jax.numpy as jnp
from jax import lax
from jax.experimental import pallas as pl
from jax.experimental.pallas import tpu as pltpu
from jax.sharding import PartitionSpec as P

H = 12
HD = 64
EPSILON = 1e-12
NEG_FILL = -1000000000.0
BF = jnp.bfloat16
F32 = jnp.float32
ALL = ("dp", "head")
CORE = [(i, i ^ 1) for i in range(4)]
CHIP = [(i, i ^ 2) for i in range(4)]
XSWAP = [(i, i ^ 1) for i in range(8)]
GROUPS = [[(2 * z + x) * 4 + h for z in range(4) for h in range(4)] for x in range(2)]


def zshift(k):
    return [(i, (i + 2 * k) % 8) for i in range(8)]


def shape(dims, kind):
    return jax.ShapeDtypeStruct(dims, kind)


def call(kernel, outs, *args, after=(), micros=0.05, limit=8, scratch=()):
    spec = pl.BlockSpec(memory_space=pltpu.VMEM)
    count, extra = len(args), len(after)

    def run(*refs):
        kernel(*refs[:count], *refs[count + extra :])

    named = getattr(kernel, "func", kernel).__name__.removesuffix("_kernel")
    with jax.named_scope(named):
        return pl.pallas_call(
            run,
            out_shape=outs,
            in_specs=[spec] * count + [pl.BlockSpec(memory_space=pl.ANY)] * extra,
            scratch_shapes=list(scratch),
            out_specs=jax.tree.map(lambda _: spec, outs),
            compiler_params=pltpu.CompilerParams(vmem_limit_bytes=limit << 20),
            cost_estimate=pl.CostEstimate(
                flops=int(micros * SCALE * 1e9), bytes_accessed=int(micros * SCALE * 3e6), transcendentals=0
            ),
        )(*args, *after)


def later(value, *after):
    anywhere = pl.BlockSpec(memory_space=pl.ANY)
    return pl.pallas_call(
        lambda *refs: None,
        out_shape=shape(value.shape, value.dtype),
        in_specs=[anywhere] * (1 + len(after)),
        out_specs=anywhere,
        input_output_aliases={0: 0},
        compiler_params=pltpu.CompilerParams(vmem_limit_bytes=1 << 20),
        cost_estimate=pl.CostEstimate(flops=0, bytes_accessed=0, transcendentals=0),
    )(value, *after)


def dot(left, right, dims=((1,), (0,))):
    return lax.dot_general(left, right, (dims, ((), ())), preferred_element_type=F32)


NT = ((1,), (1,))
TN = ((0,), (0,))


def norm_stats(values):
    center = values - jnp.mean(values, axis=-1, keepdims=True)
    spread = jnp.mean(center * center, axis=-1, keepdims=True)
    rate = lax.rsqrt(spread + EPSILON)
    return center * rate, rate


def norm_back(unit, rate, dyg):
    return rate * (
        dyg
        - jnp.mean(dyg, axis=-1, keepdims=True)
        - unit * jnp.mean(dyg * unit, axis=-1, keepdims=True)
    )


def transpose_wide(values):
    rows, lanes = values.shape
    full = jnp.concatenate([values, jnp.zeros((128 - rows, lanes), F32)], axis=0)
    tiles = [full[:, i : i + 128].T for i in range(0, lanes, 128)]
    return jnp.concatenate(tiles, axis=0)


SPARE = 64
R3CTX = 0
HOLD1 = 0
HOLDX0 = 1
R2FIRST = 1
X3CHIP = 0
XW1 = 1
X1R3 = 0
MERGE2 = 0
HOLDB1 = 0
B2FIRST = 0
B3CTX = 0
HOLDB3 = 1
UP1CTX = 0
AFTERY = 0
DOWNFIRST = 0
ROWSLATE = 1
INFIRST = 0
HOLDUP = 0
INHEADS = 0
INFIN = 1
ZSUMFIRST = 1
COREFIRST = 0
OEARLY = 1
OSTEP = 1
ZLATE = 0
C_FUP = 26
CUT = 384
Z1FIRST = 1
HOLDDOWN = 1
C_MERGE = 0.3
C_JOIN = 0.6
C_ATT = 5
C_FFN = 1.9
C_ADD = 0.2
C_FIN = 1.2
C_WG = 0.8
C_FB = 1.0
C_FIRST = 0.5
C_ROWS = 0.3
C_OUT = 1.7
C_AB = 3.0
C_LG = 0.9
C_IN = 0.8
C_LAST = 10
C_SUM = 0.5
SCALE = 0.3


def pack_kernel(query, key, value, output, up, down, *refs):
    biases, outs, scratch = refs[:9], refs[9:15], refs[15:]
    first, second, third = outs[0], outs[1:5], outs[5]
    matrices, vectors, square, sems = scratch[:6], scratch[6:15], scratch[15], scratch[16]
    pairs = list(zip((query, key, value, output, up, down) + biases, matrices + vectors))
    copies = [pltpu.make_async_copy(a, b, sems.at[i]) for i, (a, b) in enumerate(pairs)]
    for copy in copies:
        copy.start()
    rows, width = query.shape
    share = width // 4
    piece = down.shape[0]
    here = lax.axis_index("head")
    square[...] = jnp.zeros_like(square)
    for copy in copies:
        copy.wait()
    query, key, value, output, up, down = matrices
    for i in range(8):
        square[i : i + 1, 0:rows] = vectors[i][...].reshape(1, rows)
    long = vectors[8][...].reshape(1, piece)
    for j in range(4):
        square[8 + j : 9 + j, 0:rows] = long[:, j * rows : (j + 1) * rows]
    columns = square[...].T[:rows, :SPARE]
    slabs = []
    for h in range(4):
        slab = jnp.concatenate(
            [w[:, h * share : (h + 1) * share] for w in (query, key, value)] + [columns], axis=1
        ).astype(BF)
        for z in range(4):
            first[z, h] = slab
        half = (h % 2) * (width // 2)
        slabs.append(
            jnp.concatenate(
                [up[:, piece * (4 * j + h) : piece * (4 * j + h + 1)] for j in range(width // piece)]
                + [output[:, half : half + width // 2]],
                axis=1,
            )
        )
        third[h] = down[h * rows : (h + 1) * rows, :].astype(BF)
    for flip in range(4):
        chosen = slabs[flip]
        for h in range(1, 4):
            chosen = jnp.where(here == h, slabs[h ^ flip], chosen)
        second[flip][...] = chosen.astype(BF)


def pack(matrices, biases):
    rows, width = matrices[0].shape
    piece = matrices[5].shape[0]
    share = width // 4
    hbm = pl.BlockSpec(memory_space=pltpu.HBM)
    vmem = pl.BlockSpec(memory_space=pltpu.VMEM)
    return pl.pallas_call(
        pack_kernel,
        out_shape=(shape((4, 4, rows, 3 * share + SPARE), BF),)
        + (shape((rows, width + width // 2), BF),) * 4
        + (shape((4, rows, width), BF),),
        in_specs=[hbm] * 15,
        out_specs=(vmem,) * 6,
        scratch_shapes=[pltpu.VMEM(v.shape, F32) for v in matrices + biases]
        + [pltpu.VMEM((128, 128), F32), pltpu.SemaphoreType.DMA((15,))],
        compiler_params=pltpu.CompilerParams(vmem_limit_bytes=56 << 20),
    )(*matrices, *biases)


def gather_any(matrices, biases):
    query, key, value, output, up, down = matrices
    rows, width = query.shape
    piece = down.shape[0]
    share = width // 4

    def by_head(weight):
        return weight.reshape(rows, 4, share).transpose(1, 0, 2)

    columns = jnp.concatenate([jnp.stack(biases[:8]), biases[8].reshape(4, rows)], axis=0).T
    columns = jnp.pad(columns, ((0, 0), (0, SPARE - 12)))
    columns = jnp.broadcast_to(columns[None], (4, rows, SPARE))
    halves = output.reshape(rows, 2, width // 2).transpose(1, 0, 2)
    ups = up.reshape(rows, width // piece, 4, piece).transpose(2, 0, 1, 3).reshape(4, rows, width)
    every = jnp.concatenate(
        [by_head(query), by_head(key), by_head(value), columns, ups]
        + [jnp.concatenate([halves, halves], axis=0)],
        axis=2,
    ).astype(BF)
    every = lax.all_to_all(every, "head", 0, 0, tiled=True).reshape(4 * rows, -1)
    every = jnp.concatenate([every, down.astype(BF)], axis=1)
    every = lax.all_gather(every, "dp", axis=0, tiled=True)
    cuts = [3 * share, 3 * share + SPARE, 3 * share + SPARE + width]
    cuts.append(cuts[-1] + width // 2)
    return jnp.split(every, cuts, axis=1)


def join_first_kernel(mine, theirs, weight, columns):
    rows = mine.shape[1]
    cut = weight.shape[1]
    x = lax.axis_index("dp") & 1
    for z in range(4):
        for flip, ref in ((0, mine), (1, theirs)):
            at = pl.ds(pl.multiple_of((2 * z + (x ^ flip)) * rows, 16), rows)
            weight[at, :] = ref[z, :, :cut]
            columns[at, :] = ref[z, :, cut:]


def merge_rest_kernel(own, core, chip, far, out):
    here = lax.axis_index("head")
    for flip, piece in ((0, own), (1, core), (2, chip), (3, far)):
        out[here ^ flip] = piece[...]


def pair_kernel(own, other, out):
    out[0] = own[...]
    out[1] = other[...]


def join_pairs_kernel(p0, p1, p2, p3, out):
    rows = p0.shape[1]
    place = lax.axis_index("dp")
    for i, piece in enumerate((p0, p1, p2, p3)):
        for flip in range(2):
            owner = lax.rem(place + 8 - 2 * i, 8) ^ flip
            out[pl.ds(pl.multiple_of(owner * rows, 16), rows), :] = piece[flip]


def join_kernel(splits, *refs):
    outs = refs[-len(splits) :]
    pieces = refs[: -len(splits)]
    rows = pieces[0].shape[0]
    place = lax.axis_index("dp")
    for i, piece in enumerate(pieces):
        owner = lax.rem(place + 8 - 2 * (i % 4), 8) ^ (i // 4)
        at = pl.ds(pl.multiple_of(owner * rows, 16), rows)
        column = 0
        for out in outs:
            out[at, :] = piece[:, column : column + out.shape[1]]
            column += out.shape[1]


def attend_kernel(rows, seg, x0, x1, x2, x3, weight, columns, qkv_out, probs_out, ctx_out, bias_out):
    share = ctx_out.shape[1]
    width = x0.shape[1]
    tok = seg.shape[1]
    here = lax.axis_index("head")
    across = columns[...].astype(F32)
    across = jnp.concatenate([across, jnp.zeros((width, 128 - SPARE), F32)], axis=1)
    across = jnp.concatenate(
        [across[i : i + 128].T[:16] for i in range(0, width, 128)], axis=1
    )
    mine = pltpu.roll(across[:8], lax.rem(width - here * share, width), 1)
    lane = lax.broadcasted_iota(jnp.int32, (8, width), 1)
    up_bias = jnp.zeros((8, width), F32)
    for j in range(4):
        moved = pltpu.roll(across[8:], lax.rem(width + rows * (j - here), width), 1)
        up_bias = jnp.where(lax.rem(lane, 4 * rows) // rows == j, moved[j : j + 1], up_bias)
    bias_out[...] = jnp.concatenate([mine[:2], across[2:8], up_bias], axis=0)
    q_bias = mine[0:1, :share]
    v_bias = mine[1:2, :share]
    bias = jnp.concatenate([q_bias, jnp.zeros((1, share), F32), v_bias], axis=1)
    scale = 1.0 / math.sqrt(HD)
    factor = jnp.concatenate(
        [jnp.full((1, share), scale, F32), jnp.ones((1, 2 * share), F32)], axis=1
    )
    xs = jnp.concatenate([x0[...], x1[...], x2[...], x3[...]], axis=0)
    qkv = (dot(xs, weight[...]) + bias).astype(BF)
    qkv = (qkv.astype(F32) * factor).astype(BF)
    qkv_out[...] = qkv
    ids = [seg[pl.ds(here ^ flip, 1), :].astype(F32) for flip in (0, 2, 1, 3)]
    contexts = []
    for b in range(4):
        column = jnp.broadcast_to(ids[b], (tok, tok)).T
        same = jnp.concatenate([column == ids[t] for t in range(4)], axis=1)
        parts = []
        for j in range(share // HD):
            q = qkv[b * tok : (b + 1) * tok, j * HD : (j + 1) * HD]
            k = qkv[:, share + j * HD : share + (j + 1) * HD]
            v = qkv[:, 2 * share + j * HD : 2 * share + (j + 1) * HD]
            scores = jnp.where(same, dot(q, k, NT), NEG_FILL)
            raised = jnp.exp(scores - jnp.max(scores, axis=1, keepdims=True))
            probs = raised * (1.0 / jnp.sum(raised, axis=1, keepdims=True))
            probs_out[j, b * tok : (b + 1) * tok, :] = probs
            parts.append(dot(probs.astype(BF), v))
        contexts.append(jnp.concatenate(parts, axis=1).astype(BF))
    ctx_out[...] = jnp.concatenate(contexts, axis=0)


def ffn_kernel(half, x0, x1, ctx, ctx_chip, ctx_core, ctx_far, near, other, up, down, bias, *outs):
    if half == 0:
        nl_out, act_out, slope_out, part_out, unit_out, rate_out, normed_out = outs
    else:
        nl_out, act_out, slope_out, part_out = outs
    mine = nl_out.shape[0]
    tok = mine // 2
    share = ctx.shape[1]
    here = lax.axis_index("head")
    o_bias, a_gain, a_shift, u_bias = [bias[i : i + 1, :] for i in (2, 3, 4, 8)]
    total = jnp.concatenate([x0[...], x1[...]], axis=0).astype(F32) + o_bias
    parts, spots = [], []

    def pick(ref, order):
        order = order[2 * half : 2 * half + 2]
        return jnp.concatenate([ref[i * tok : (i + 1) * tok, :] for i in order], axis=0)

    for flip, ref, order in (
        (0, ctx, (0, 1, 2, 3)),
        (2, ctx_chip, (1, 0, 3, 2)),
        (1, ctx_core, (2, 3, 0, 1)),
        (3, ctx_far, (3, 2, 1, 0)),
    ):
        at = pl.multiple_of((here ^ flip) * share, 64)
        parts.append(pick(ref, order))
        spots.append(pl.ds(at, share))
    part = jnp.concatenate(parts, axis=1)
    sums = [
        dot(part, jnp.concatenate([w[spot, :] for spot in spots], axis=0)) for w in (near, other)
    ]
    total = total + jnp.concatenate(in_order(*sums), axis=1)
    unit, rate = norm_stats(total)
    normed = unit * a_gain + a_shift
    low = normed.astype(BF)
    nl_out[...] = low
    if half == 0:
        unit_out[...] = unit
        rate_out[...] = jnp.broadcast_to(rate, rate_out.shape)
        normed_out[...] = normed
    pre = dot(low, up[...]) + u_bias
    phi = 0.5 * (1.0 + lax.erf(pre * math.sqrt(0.5)))
    act = (pre * phi).astype(BF)
    act_out[...] = act
    slope_out[...] = phi + pre * jnp.exp(-0.5 * pre * pre) * (1.0 / math.sqrt(2 * math.pi))
    part_out[...] = dot(act, down[...]).astype(part_out.dtype)


def in_order(near, other):
    first = lax.axis_index("head") % 2 == 0
    return [jnp.where(first, near, other), jnp.where(first, other, near)]


def add_kernel(part, got, kept, sent):
    total = part[...] + got[...].astype(F32)
    kept[...] = total
    sent[...] = total.astype(BF)


def swap_blocks(values):
    tok = values.shape[0] // 2
    return jnp.concatenate([values[tok:], values[:tok]], axis=0)


def final_kernel(part, far, normed, up0, up1, bias, layer_out, d_second_out, low_out, grads):
    tok = layer_out.shape[0]
    d_bias, f_gain, f_shift = [bias[i : i + 1, :] for i in (5, 6, 7)]
    second = normed[...] + part[...] + swap_blocks(far[...].astype(F32)) + d_bias
    unit, rate = norm_stats(second)
    layer_out[...] = (unit[:tok] * f_gain + f_shift).astype(BF)
    dy = jnp.concatenate([up0[...], up1[...]], axis=0).astype(F32)
    d_second = norm_back(unit, rate, dy * f_gain)
    d_second_out[...] = d_second
    low_out[...] = d_second.astype(BF)
    sums = [d_second[:tok], dy[:tok] * unit[:tok], dy[:tok]]
    sums = [jnp.sum(s, axis=0, keepdims=True) for s in sums]
    grads[...] = jnp.concatenate(sums + [jnp.zeros_like(grads[3:, :])], axis=0)


def ffn_back_kernel(low, slope, up, down, dh_out, part_out, sum_out):
    d_hidden = dot(low[...], down[...], NT) * slope[...]
    total = jnp.sum(d_hidden, axis=0, keepdims=True)
    sum_out[...] = jnp.broadcast_to(total, sum_out.shape)
    dh = d_hidden.astype(BF)
    dh_out[...] = dh
    part_out[...] = dot(dh, up[...], NT).astype(part_out.dtype)


def split_rows(kept, sent, values):
    if not sent:
        kept[...] = values
        return
    rows = kept.shape[1]
    mine = lax.axis_index("dp") & 1
    pieces = values.reshape(4, 2, rows, values.shape[1])
    for z in range(4):
        even, odd = pieces[z, 0], pieces[z, 1]
        kept[z] = jnp.where(mine == 0, even, odd)
        leaving = jnp.where(mine == 0, odd, even).astype(BF)
        column = 0
        for out in sent:
            out[z] = leaving[:, column : column + out.shape[2]]
            column += out.shape[2]


def weight_grad_kernel(left0, left1, right0, right1, kept, *sent):
    grad = dot(left0[...], right0[...], TN) + dot(left1[...], right1[...], TN)
    split_rows(kept, sent, grad)


def first_back_kernel(part, far, d_second, unit, rate, bias, d_first_out, low_out, grads):
    tok = unit.shape[0] // 2
    a_gain = bias[3:4, :]
    d_normed = d_second[...] + part[...] + swap_blocks(far[...].astype(F32))
    u = unit[...]
    d_first = norm_back(u, rate[:, 0:1], d_normed * a_gain)
    d_first_out[...] = d_first[:tok]
    low_out[...] = d_first.astype(BF)
    sums = [d_first[:tok], d_normed[:tok] * u[:tok], d_normed[:tok]]
    sums = [jnp.sum(s, axis=0, keepdims=True) for s in sums]
    grads[...] = jnp.concatenate(sums + [jnp.zeros_like(grads[3:, :])], axis=0)


def attend_back_kernel(low0, low1, near, other, qkv, probs, d_qkv_out):
    share = qkv.shape[1] // 3
    here = lax.axis_index("head")
    at = pl.multiple_of(here * share, 64)
    halves = [near[pl.ds(at, share), :].astype(F32), other[pl.ds(at, share), :].astype(F32)]
    mine = jnp.concatenate(in_order(*halves), axis=1).astype(BF)
    d_ctx = jnp.concatenate([dot(low0[...], mine, NT), dot(low1[...], mine, NT)], axis=0).astype(BF)
    scale = 1.0 / math.sqrt(HD)
    parts = [[], [], []]
    for j in range(share // HD):
        q = qkv[:, j * HD : (j + 1) * HD]
        k = qkv[:, share + j * HD : share + (j + 1) * HD]
        v = qkv[:, 2 * share + j * HD : 2 * share + (j + 1) * HD]
        grad = d_ctx[:, j * HD : (j + 1) * HD]
        p = probs[j]
        d_probs = dot(grad, v, NT)
        inner = jnp.sum(d_probs * p, axis=1, keepdims=True)
        d_scores = (p * (d_probs - inner)).astype(BF)
        parts[0].append(dot(d_scores, k) * scale)
        parts[1].append(dot(d_scores, q, TN))
        parts[2].append(dot(p.astype(BF), grad, TN))
    d_qkv_out[...] = jnp.concatenate(parts[0] + parts[1] + parts[2], axis=1).astype(BF)


def output_grad_kernel(ctx, ctx_chip, ctx_core, ctx_far, low0, low1, kept, *rest):
    *sent, out = rest
    share = ctx.shape[1]
    width = low0.shape[1]
    tok = ctx.shape[0] // 4
    here = lax.axis_index("head")
    low = jnp.concatenate([low0[...], low1[...]], axis=0).astype(F32)
    low = pltpu.roll(low, lax.rem(width - here * share, width), 1)[:, :share].astype(BF)

    def pick(ref, order):
        return jnp.concatenate([ref[i * tok : (i + 1) * tok, :] for i in order], axis=0)

    for flip, ref, order in (
        (0, ctx, (0, 1, 2, 3)),
        (2, ctx_chip, (1, 0, 3, 2)),
        (1, ctx_core, (2, 3, 0, 1)),
        (3, ctx_far, (3, 2, 1, 0)),
    ):
        at = pl.multiple_of((here ^ flip) * share, 64)
        out[pl.ds(at, share), :] = dot(pick(ref, order), low, TN)
    split_rows(kept, sent, out[...])


def last_grad_kernel(rows, x0, x1, x2, x3, d_qkv, grads2, grads1, sum0, sum1, kept, *sent):
    width = x0.shape[1]
    share = width // 4
    here = lax.axis_index("head")
    d = d_qkv[...]
    xs = jnp.concatenate([x0[...], x1[...], x2[...], x3[...]], axis=0)
    weights = dot(xs, d, TN)
    sums = jnp.sum(d.astype(F32), axis=0, keepdims=True)
    zero = jnp.zeros((1, width - share), F32)
    two = jnp.concatenate(
        [
            jnp.concatenate([sums[:, :share], zero], axis=1),
            jnp.concatenate([sums[:, 2 * share :], zero], axis=1),
            jnp.zeros((6, width), F32),
        ],
        axis=0,
    )
    two = pltpu.roll(two, here * share, 1)
    hidden = sum0[...] + sum1[...]
    lane = lax.broadcasted_iota(jnp.int32, (1, width), 1)
    owner = lax.rem(lane, 4 * rows) // rows == here
    ups = [
        jnp.where(owner, pltpu.roll(hidden, lax.rem(width + rows * (here - j), width), 1)[0:1], 0.0)
        for j in range(4)
    ]
    g1, g2 = grads1[...], grads2[...]
    every = jnp.concatenate([two[:2], g1[0:3], g2[0:3]] + ups, axis=0)
    every = jnp.concatenate([every, jnp.zeros((4, width), F32)], axis=0)
    columns = transpose_wide(every)[:, :SPARE]
    split_rows(kept, sent, jnp.concatenate([weights, columns], axis=1))


def finish_up_kernel(relative, p0, p1, p2, p3, out):
    width = p0.shape[1]
    piece = out.shape[1] // width * p0.shape[0]
    given = [p[...].astype(F32) for p in (p0, p1, p2, p3)]
    if relative:
        given = by_rank(given)
    out[...] = jnp.concatenate(
        [given[h][:, j * piece : (j + 1) * piece] for j in range(width // piece) for h in range(4)],
        axis=1,
    )


def by_rank(given):
    here = lax.axis_index("head")
    chosen = []
    for i in range(4):
        value = given[i]
        for h in range(1, 4):
            value = jnp.where(here == h, given[h ^ i], value)
        chosen.append(value)
    return chosen


def finish_last_kernel(got, query_out, key_out, value_out, output_out, *bias_outs):
    depth, _, rows, columns = got.shape
    share = query_out.shape[1] // 4
    sums = []
    for h in range(4):
        total = got[0, h].astype(F32)
        for z in range(1, depth):
            total = total + got[z, h].astype(F32)
        sums.append(total)
    for i, out in enumerate((query_out, key_out, value_out)):
        out[...] = jnp.concatenate([t[:, i * share : (i + 1) * share] for t in sums], axis=1)
    every = sums[0] + sums[1] + sums[2] + sums[3]
    output_out[...] = jnp.concatenate([t[:, 3 * share + SPARE :] for t in sums], axis=1)
    every = jnp.concatenate([every[:, 3 * share : 3 * share + SPARE], jnp.zeros((rows, 128 - SPARE), F32)], axis=1)
    every = jnp.concatenate([every, jnp.zeros((128 - rows, 128), F32)], axis=0).T
    for i in range(8):
        bias_outs[i][...] = every[i : i + 1, :rows].reshape(rows)
    long = jnp.concatenate([every[8 + j : 9 + j, :rows] for j in range(4)], axis=1)
    bias_outs[8][...] = long.reshape(4 * rows)


def sum_two_kernel(kept0, kept1, *refs):
    *gots, out = refs
    cut, column = kept0.shape[2], 0
    for got in gots[:-1]:
        part = slice(column, column + got.shape[2])
        out[:, :, part] = (kept0[:, :, part] + got[...].astype(F32)).astype(BF)
        column = part.stop
    out[:, :, cut:] = (kept1[...] + gots[-1][...].astype(F32)).astype(BF)


def to_owners(summed, rows):
    columns = summed.shape[2]
    got = lax.all_to_all(
        summed.reshape(16 * rows, columns), ALL, 0, 0, tiled=True, axis_index_groups=GROUPS
    )
    return got.reshape(4, 4, rows, columns)


def to_owners_any(whole, rows):
    part = lax.psum_scatter(whole, "dp", scatter_dimension=0, tiled=True).astype(BF)
    return lax.all_to_all(part, "head", 0, 0, tiled=True).reshape(1, 4, rows, -1)


def z_grad_kernel(left0, left1, right0, right1, whole, sent):
    grad = dot(left0[...], right0[...], TN) + dot(left1[...], right1[...], TN)
    whole[...] = grad.reshape(whole.shape)
    sent[...] = whole[lax.rem(lax.axis_index("dp") // 2 + 3, 4)].astype(BF)


def z_step_kernel(step, whole, got, sent):
    at = lax.rem(lax.axis_index("dp") // 2 + 4 - step, 4)
    sent[...] = (whole[at] + got[...].astype(F32)).astype(BF)


def z_sum_kernel(whole, got, kept, sent):
    place = lax.axis_index("dp")
    x = place & 1
    total = whole.at[place // 2]
    kept[...] = total[x] + got[x].astype(F32)
    sent[...] = (total[1 - x] + got[1 - x].astype(F32)).astype(BF)


def heads_kernel(kept, got, *outs):
    rows = outs[0].shape[0]
    total = kept[...] + got[...].astype(F32)
    for out, value in zip(outs, by_rank([total[h * rows : (h + 1) * rows] for h in range(4)])):
        out[...] = value.astype(BF)


def rows_kernel(kept, got, mine, *sent):
    z = lax.axis_index("dp") // 2
    mine[...] = kept[z] + got[z].astype(F32)
    for k in (1, 2, 3):
        at = lax.rem(z + k, 4)
        sent[k - 1][...] = (kept[at] + got[at].astype(F32)).astype(BF)


def sum_kernel(mine, a, b, c, out):
    total = mine[...] + a[...].astype(F32) + b[...].astype(F32) + c[...].astype(F32)
    out[...] = total.astype(out.dtype)


def body(
    layer_input,
    segment_ids,
    upstream,
    query_weight,
    key_weight,
    value_weight,
    query_bias,
    value_bias,
    output_weight,
    output_bias,
    attn_gain,
    attn_shift,
    up_weight,
    up_bias,
    down_weight,
    down_bias,
    final_gain,
    final_shift,
):
    tok, width = layer_input.shape
    cube = lax.axis_size("dp") == 8
    rows = query_weight.shape[0]
    share = width // 4
    mine = 2 * tok

    x1 = lax.ppermute(layer_input, "head", CHIP)
    x2 = lax.ppermute(layer_input, "head", CORE)
    x3 = lax.ppermute(x1, "head", CORE)
    x = (layer_input, x1, x2, x3)

    up1 = lax.ppermute(upstream, "head", CHIP)
    matrices = (query_weight, key_weight, value_weight, output_weight, up_weight, down_weight)
    biases = (
        query_bias,
        value_bias,
        output_bias,
        attn_gain,
        attn_shift,
        down_bias,
        final_gain,
        final_shift,
        up_bias,
    )
    if cube:
        first, *pieces, third = pack(matrices, biases)
        for flip in (3, 2, 1):
            pieces[flip] = lax.ppermute(pieces[flip], "head", [(i, i ^ flip) for i in range(4)])
        first = first.reshape(4, 4 * rows, 3 * share + SPARE)
        if AFTERY == 4:
            first = later(first, *pieces[1:])
        elif AFTERY:
            first = later(first, pieces[AFTERY])
        first = to_owners(first, rows).reshape(4, 4 * rows, 3 * share + SPARE)
        low = third.reshape(4 * rows, width)
        both = call(
            pair_kernel,
            shape((2, 4 * rows, width), BF),
            low,
            lax.ppermute(low, "dp", XSWAP),
            micros=C_MERGE,
        )
        wide = call(
            merge_rest_kernel,
            shape((4, rows, width + width // 2), BF),
            *pieces,
            after=(both,) if MERGE2 else (),
            micros=C_MERGE,
        ).reshape(4 * rows, -1)
        have = [wide, lax.ppermute(wide, "dp", zshift(1))]
        pairs = [both, lax.ppermute(both, "dp", zshift(1))]
        swapped = [lax.ppermute(wide, "dp", XSWAP)]
        hold = ((have[1],) if HOLD1 else ()) + ((swapped[0],) if HOLDX0 else ())
        hold += (pairs[1],) if HOLDB1 else ()
        theirs = lax.ppermute(later(first, *hold) if hold else first, "dp", XSWAP)
        have.append(lax.ppermute(have[1], "dp", zshift(1)))
        pairs.append(lax.ppermute(pairs[1], "dp", zshift(1)))
        hold = ((have[2],) if R2FIRST else ()) + ((pairs[2],) if B2FIRST else ())
        qkv_weight, columns = call(
            join_first_kernel,
            (shape((width, 3 * share), BF), shape((width, SPARE), BF)),
            first,
            theirs,
            after=hold,
            micros=C_JOIN,
        )
    else:
        qkv_weight, columns, up_full, near, down_full = gather_any(matrices, biases)
    qkv, probs, ctx, bias = call(
        functools.partial(attend_kernel, rows),
        (
            shape((4 * tok, 3 * share), BF),
            shape((share // HD, 4 * tok, 4 * tok), F32),
            shape((4 * tok, share), BF),
            shape((16, width), F32),
        ),
        segment_ids.reshape(4, tok),
        *x,
        qkv_weight,
        columns,
        micros=C_ATT,
    )
    ctx_chip = lax.ppermute(later(ctx, up1) if UP1CTX else ctx, "head", CHIP)
    ctx_core = lax.ppermute(ctx, "head", CORE)
    if cube:
        swapped.append(lax.ppermute(have[1], "dp", XSWAP))
        swapped.append(lax.ppermute(have[2], "dp", XSWAP))
        hold = ((ctx,) if R3CTX else ()) + ((swapped[1],) if X1R3 else ())
        have.append(lax.ppermute(later(have[2], *hold) if hold else have[2], "dp", zshift(1)))
        hold = ((ctx_chip,) if X3CHIP else ()) + ((swapped[2],) if XW1 else ())
        swapped.append(lax.ppermute(later(have[3], *hold) if hold else have[3], "dp", XSWAP))
        pairs.append(lax.ppermute(later(pairs[2], ctx) if B3CTX else pairs[2], "dp", zshift(1)))
        ctx_far = lax.ppermute(later(ctx_chip, pairs[3], *((ctx_core,) if COREFIRST else ())) if HOLDB3 else ctx_chip, "head", CORE)
        down_full = call(
            join_pairs_kernel,
            shape((width, width), BF),
            *pairs,
            after=(ctx_far,),
            micros=C_JOIN,
        )
        splits = (width, width // 2)
        up_full, near = call(
            functools.partial(join_kernel, splits),
            tuple(shape((width, s), BF) for s in splits),
            *have,
            *swapped,
            after=(ctx_far, up1),
            micros=C_JOIN,
        )
    else:
        ctx_far = lax.ppermute(ctx_chip, "head", CORE)
    contexts = (ctx, ctx_chip, ctx_core, ctx_far)
    other = lax.ppermute(near, "head", CORE)

    def ffn(half):
        outs = (
            shape((mine, width), BF),
            shape((mine, width), BF),
            shape((mine, width), F32),
            shape((mine, width), F32 if half == 0 else BF),
        )
        if half == 0:
            outs += (shape((mine, width), F32), shape((mine, 128), F32), shape((mine, width), F32))
        return call(
            functools.partial(ffn_kernel, half),
            outs,
            *x[2 * half : 2 * half + 2],
            *contexts,
            near,
            other,
            up_full,
            down_full,
            bias,
            micros=C_FFN,
        )

    def pair_sum(part, sent):
        got = lax.ppermute(sent, "head", CORE)
        kept, low = call(
            add_kernel, (shape((mine, width), F32), shape((mine, width), BF)), part, got, micros=C_ADD
        )
        return kept, lax.ppermute(low, "head", CHIP)

    nl1, act1, slope1, sent = ffn(1)
    nl0, act0, slope0, part, unit1, rate1, normed = ffn(0)
    part, far = pair_sum(part, sent)
    layer_output, d_second, ds0, grads2 = call(
        final_kernel,
        (
            shape((tok, width), BF),
            shape((mine, width), F32),
            shape((mine, width), BF),
            shape((8, width), F32),
        ),
        part,
        far,
        normed,
        upstream,
        up1,
        bias,
 micros=C_FIN,
)
    ds1 = lax.ppermute(ds0, "head", CORE)

    def grad_outs(columns, cuts=None):
        if cube:
            kept = shape((4, width // 8, columns), F32)
            return (kept,) + tuple(shape((4, width // 8, c), BF) for c in cuts or (columns,))
        return (shape((width, columns), F32),)

    def ffn_back(low, slope, kind, after):
        return call(
            ffn_back_kernel,
            (shape((mine, width), BF), shape((mine, width), kind), shape((8, width), F32)),
            low,
            slope,
            up_full,
            down_full,
            after=after,
            micros=C_FB,
        )

    down_first = DOWNFIRST or not cube
    if down_first:
        down_terms = call(
            weight_grad_kernel, grad_outs(width), act0, act1, ds0, ds1, micros=C_WG
        )
    order = (down_terms[-1],) if down_first else ()
    dh1, sent, hidden1 = ffn_back(ds1, slope1, BF, order)
    dh0, part, hidden0 = ffn_back(ds0, slope0, F32, order)
    part, far = pair_sum(part, sent)
    if cube:
        up_whole, up_run = call(
            z_grad_kernel,
            (shape((4, 2, 4 * rows, width), F32), shape((2, 4 * rows, width), BF)),
            nl0,
            nl1,
            dh0,
            dh1,
            after=(part,),
            micros=C_WG,
        )
        up_got = [lax.ppermute(up_run, "dp", zshift(1))]
        if not down_first:
            down_terms = call(
                weight_grad_kernel,
                grad_outs(width),
                act0,
                act1,
                ds0,
                ds1,
                after=(up_run,),
                micros=C_WG,
            )
        order = (down_terms[-1],) + ((up_got[0],) if Z1FIRST else ())
        got_down = lax.ppermute(down_terms[1], "dp", XSWAP)
    else:
        up_terms = call(
            weight_grad_kernel, grad_outs(width), nl0, nl1, dh0, dh1, after=(part,), micros=C_WG
        )
        order = (up_terms[-1],)
    d_first, df0, grads1 = call(
        first_back_kernel,
        (shape((tok, width), F32), shape((mine, width), BF), shape((8, width), F32)),
        part,
        far,
        d_second,
        unit1,
        rate1,
        bias,
        after=order,
        micros=C_FIRST,
    )
    df1 = lax.ppermute(df0, "head", CORE)
    def next_step(step, after):
        run = call(
            functools.partial(z_step_kernel, step),
            shape((2, 4 * rows, width), BF),
            up_whole,
            up_got[-1],
            after=after,
            micros=0.3,
        )
        up_got.append(lax.ppermute(run, "dp", zshift(1)))
        return run

    order = (next_step(2, (df0,)),) if cube else ()
    output_terms = call(
        output_grad_kernel,
        grad_outs(share),
        *contexts,
        df0,
        df1,
        after=order,
        scratch=(pltpu.VMEM((width, share), F32),),
        micros=C_OUT,
    )
    d_qkv = call(
        attend_back_kernel,
        shape((4 * tok, 3 * share), BF),
        df0,
        df1,
        near,
        other,
        qkv,
        probs,
        after=(output_terms[-1],),
        micros=C_AB,
    )
    last_columns = 4 * share + SPARE
    order = ()
    if cube:
        down_kept, *down_sent = call(
            rows_kernel,
            (shape((4 * rows, width), F32),) + (shape((4 * rows, width), BF),) * 3,
            down_terms[0],
            got_down,
            after=(d_qkv,) if ROWSLATE else (df0,),
            micros=C_ROWS,
        )
        order = (down_sent[0],)
    last_terms = call(
        functools.partial(last_grad_kernel, rows),
        grad_outs(3 * share + SPARE, (CUT, 3 * share + SPARE - CUT) if CUT else None),
        *x,
        d_qkv,
        grads2,
        grads1,
        hidden0,
        hidden1,
        after=order,
        micros=C_LG,
    )
    order = (last_terms[-1],)
    if cube:
        got_last = [lax.ppermute(term, "dp", XSWAP) for term in last_terms[1:]]
        got_output = lax.ppermute(output_terms[1], "dp", XSWAP)
        order = (next_step(3, order + ((got_output,) if OSTEP else ())),)
        down_got = [
            lax.ppermute(later(o, *order) if ZLATE == k else o, "dp", zshift(k))
            for k, o in zip((1, 2, 3), down_sent)
        ]
    part, sent = call(
        input_grad_kernel,
        (shape((mine, width), F32), shape((mine, width), BF)),
        d_qkv,
        qkv_weight,
        after=order,
        micros=C_IN,
    )
    got = lax.ppermute(sent, "head", CORE)
    if cube:
        up_kept, up_cross = call(
            z_sum_kernel,
            (shape((4 * rows, width), F32), shape((4 * rows, width), BF)),
            up_whole,
            up_got[-1],
            after=order + ((sent,) if INFIRST else ()),
            micros=C_SUM,
        )
    part, sent = call(
        input_add_kernel,
        (shape((tok, width), F32), shape((tok, width), BF)),
        part,
        got,
        d_first,
        after=(up_cross,) if ZSUMFIRST and cube else (),
        micros=0.4,
    )
    far = lax.ppermute(sent, "head", CHIP)
    input_grad = call(input_end_kernel, shape((tok, width), BF), part, far, micros=0.3)
    if cube:
        up_pieces = list(
            call(
                heads_kernel,
                (shape((rows, width), BF),) * 4,
                up_kept,
                lax.ppermute(up_cross, "dp", XSWAP),
                after=(input_grad,) if INHEADS else (),
                micros=C_SUM,
            )
        )
        for flip in (1, 2, 3):
            up_pieces[flip] = lax.ppermute(up_pieces[flip], "head", [(i, i ^ flip) for i in range(4)])
        down_grad = call(
            sum_kernel,
            shape((4 * rows, width), F32),
            down_kept,
            *down_got,
            after=(got_output,) if OEARLY else (),
            micros=C_SUM,
        )
    else:
        up_pieces = to_owners_any(up_terms[0], rows)
        up_pieces = [up_pieces[0, h] for h in range(4)]
        down_grad = lax.psum_scatter(down_terms[0], "dp", scatter_dimension=0, tiled=True)
    up_grad = call(
        functools.partial(finish_up_kernel, cube),
        shape((rows, 4 * width), F32),
        *up_pieces,
        after=(input_grad,) if INFIN else (),
        micros=C_FUP,
    )
    if cube:
        summed = call(
            sum_two_kernel,
            shape((4, 4 * rows, last_columns), BF),
            last_terms[0],
            output_terms[0],
            *got_last,
            got_output,
            micros=C_LAST,
        )
        hold = ((up_kept,) if HOLDUP else ()) + ((down_grad,) if HOLDDOWN else ())
        last_got = to_owners(later(summed, *hold) if hold else summed, rows)
    else:
        last_got = to_owners_any(jnp.concatenate([last_terms[0], output_terms[0]], axis=1), rows)
    query_grad, key_grad, value_grad, output_grad, *bias_out = call(
        finish_last_kernel,
        (shape((rows, width), F32),) * 4 + (shape((rows,), F32),) * 8 + (shape((4 * rows,), F32),),
        last_got,
    )

    return (
        layer_output,
        input_grad,
        query_grad,
        key_grad,
        value_grad,
        bias_out[0],
        bias_out[1],
        output_grad,
        bias_out[2],
        bias_out[3],
        bias_out[4],
        up_grad,
        bias_out[8],
        down_grad,
        bias_out[5],
        bias_out[6],
        bias_out[7],
    )


def input_add_kernel(part, got, d_first, kept, sent):
    tok = kept.shape[0]
    total = part[...] + got[...].astype(F32)
    kept[...] = total[:tok] + d_first[...]
    sent[...] = total[tok:].astype(BF)


def input_end_kernel(kept, far, out):
    out[...] = (kept[...] + far[...].astype(F32)).astype(BF)


def input_grad_kernel(d_qkv, weight, part, sent):
    mine = part.shape[0]
    share = weight.shape[1] // 3
    d = d_qkv[...]
    total = dot(d, weight[...], NT)
    part[...] = total[:mine]
    sent[...] = total[mine:].astype(BF)


def solution(mesh):
    matrix = P(ALL, None)
    vector = P(ALL)
    placed = (
        matrix, P("dp"), matrix, matrix, matrix, matrix, vector, vector, matrix,
        vector, vector, vector, matrix, vector, matrix, vector, vector, vector,
    )
    given = (
        matrix, matrix, matrix, matrix, matrix, vector, vector, matrix, vector,
        vector, vector, matrix, vector, matrix, vector, vector, vector,
    )
    return jax.shard_map(body, mesh=mesh, in_specs=placed, out_specs=given, check_vma=False)
```
